512 devices in a mesh: blk: 256 (over z, x, y_hi, core), head: 2 (over y_lo).
Axes of the slice: x: 4, y: 4 (y_hi: 2, y_lo: 2; y = y_hi * 2 + y_lo), z: 16, core: 2. Of those that a mesh axis runs over, the one named last changes fastest.
Arguments:
- ref_a: bfloat16 [32768, 1024], P('blk', 'head'), may hold values from -8 to 8
- val_a: bfloat16 [32768, 1024], P('blk', 'head'), may hold values from -6 to 6
- ref_b: bfloat16 [32768, 1024], P('blk', 'head'), may hold values from -8 to 8
- val_b: bfloat16 [32768, 1024], P('blk', 'head'), may hold values from -6 to 6
- w_out_a: bfloat16 [1024, 1024], P('head'), may hold values from -0.1875 to 0.1875
- w_out_b: bfloat16 [1024, 1024], P('head'), may hold values from -0.1875 to 0.1875
Outputs:
- out_a: bfloat16 [32768, 1024], P(('blk', 'head'))
- out_b: bfloat16 [32768, 1024], P(('blk', 'head'))
The draws below stay inside these ranges and needn't reach their ends.
All inputs are finite; a program needn't handle non-finite values.
Results may differ from the reference program's by a relative error of at most 0.0055.
Values may be sent and summed in bfloat16 or wider, within the bound.
A program may use at most 64 MiB of HBM per device.

```python
import jax
import jax.numpy as jnp
from jax import lax

D = 1024
HEAD_DIM = 64
ROWS = 128
NBLOCKS = 256
TOKENS = 32768


def draw_ref_a(key, part):
    key = jax.random.fold_in(key, 1)
    values = jnp.clip(jax.random.normal(key, (TOKENS, D), jnp.float32), -6.0, 6.0)
    return values.astype(jnp.bfloat16)


def draw_ref_b(key, part):
    key = jax.random.fold_in(key, 2)
    values = jnp.clip(jax.random.normal(key, (TOKENS, D), jnp.float32), -6.0, 6.0)
    return values.astype(jnp.bfloat16)


def block_levels(own_key, dims, split, low, high):
    factor_of, own = 1.0, jax.random.fold_in(own_key, 6)
    for position, parts in split:
        steps = jnp.exp(jax.random.uniform(jax.random.fold_in(own, position), (parts,), jnp.float32, low / len(split), high / len(split)))
        factor_of = factor_of * jnp.repeat(steps, dims[position] // parts).reshape([-1 if axis == position else 1 for axis in range(len(dims))])
    return factor_of


def bell_draw(key, shape, spread, reach, cuts=(), held_as=jnp.bfloat16):
    values = jax.random.normal(key, shape, jnp.float32) * spread
    if len(cuts) > 0:
        values = block_levels(key, shape, cuts, -0.22, 0.18) * values
    return jnp.clip(values, min=-reach, max=reach).astype(held_as)


def setup_inputs(seed: int = 0) -> dict:
    seeds = jax.random.split(jax.random.key(seed), 7)
    return {
        "ref_a": draw_ref_a(jax.random.fold_in(seeds[6], 71), 0),
        "val_a": bell_draw(seeds[1], (TOKENS, D), 1.0, 6.0, ((0, 256), (1, 2))),
        "ref_b": draw_ref_b(jax.random.fold_in(seeds[6], 71), 0),
        "val_b": bell_draw(seeds[3], (TOKENS, D), 1.0, 6.0, ((0, 256), (1, 2))),
        "w_out_a": bell_draw(seeds[4], (D, D), D ** -0.5, 0.1875, ((0, 2),)),
        "w_out_b": bell_draw(seeds[5], (D, D), D ** -0.5, 0.1875, ((0, 2),)),
    }


score_scale = 0.125
offsets = (-2, -1, 0, 1)


def pair_scores(query, keys):
    return jnp.einsum('ahd,bhd->hab', query.astype(jnp.float32), keys.astype(jnp.float32)) * score_scale


def rounded(values):
    return lax.optimization_barrier(values.astype(jnp.bfloat16)).astype(jnp.float32)


def row_part(scores, values):
    maxima = jnp.max(scores, axis=2)
    expo = jnp.exp(scores - maxima[:, :, None])
    total = jnp.sum(expo, axis=2)
    accum = jnp.einsum('hab,bhd->ahd', rounded(expo), values.astype(jnp.float32))
    return maxima.T, total.T, accum


def col_part(scores, values):
    maxima = jnp.max(scores, axis=1)
    expo = jnp.exp(scores - maxima[:, None, :])
    total = jnp.sum(expo, axis=1)
    accum = jnp.einsum('hab,ahd->bhd', rounded(expo), values.astype(jnp.float32))
    return maxima.T, total.T, accum


def merge_parts(first, second):
    top = jnp.maximum(first[0], second[0])
    left = jnp.exp(first[0] - top)
    right = jnp.exp(second[0] - top)
    return top, left * first[1] + right * second[1], left[:, :, None] * first[2] + right[:, :, None] * second[2]


def finish(state):
    return (state[2] / state[1][:, :, None]).reshape(ROWS, D).astype(jnp.bfloat16)


def reference(ref_a, val_a, ref_b, val_b, w_out_a, w_out_b):
    heads = D // HEAD_DIM
    block_ra = ref_a.reshape(NBLOCKS, ROWS, heads, HEAD_DIM)
    block_va = val_a.reshape(NBLOCKS, ROWS, heads, HEAD_DIM)
    block_rb = ref_b.reshape(NBLOCKS, ROWS, heads, HEAD_DIM)
    block_vb = val_b.reshape(NBLOCKS, ROWS, heads, HEAD_DIM)

    def rows_of(index):
        state = None
        for shift_by in offsets:
            other = ((index + shift_by) % NBLOCKS).astype(jnp.int32)
            part = row_part(pair_scores(block_ra[index], block_rb[other]), block_vb[other])
            state = part if state is None else merge_parts(state, part)
        return finish(state)

    def cols_of(index):
        state = None
        for shift_by in offsets:
            other = ((index - shift_by) % NBLOCKS).astype(jnp.int32)
            part = col_part(pair_scores(block_ra[other], block_rb[index]), block_va[other])
            state = part if state is None else merge_parts(state, part)
        return finish(state)

    blocks = jnp.arange(NBLOCKS, dtype=jnp.int32)
    attn_a = lax.map(rows_of, blocks).reshape(TOKENS, D)
    attn_b = lax.map(cols_of, blocks).reshape(TOKENS, D)
    out_a = jnp.dot(attn_a, w_out_a, preferred_element_type=jnp.float32).astype(jnp.bfloat16)
    out_b = jnp.dot(attn_b, w_out_b, preferred_element_type=jnp.float32).astype(jnp.bfloat16)
    return out_a, out_b
```

```python
import functools
import math

import jax
import jax.numpy as jnp
from jax import lax
from jax.experimental import pallas as pl
from jax.experimental.pallas import tpu as pltpu
from jax.sharding import PartitionSpec as P


ROWS = 128
HALF = 64
PAIR = 128
WIDTH = 1024
CHUNKS = 2
PIECE = WIDTH // CHUNKS
SCORE = 0.125 * math.log2(math.e)
BF16 = jnp.bfloat16
F32 = jnp.float32


def attend(query, keys, values):
    lane = lax.broadcasted_iota(jnp.int32, (ROWS, PAIR), 1)
    query = query.astype(F32)
    zero = jnp.zeros_like(query)
    both = jnp.concatenate(
        [jnp.where(lane < HALF, query, zero), jnp.where(lane < HALF, zero, query)], axis=0
    ).astype(BF16)
    scores = lax.dot_general(keys, both, (((1,), (1,)), ((), ())), preferred_element_type=F32)
    top = jnp.max(scores, axis=0, keepdims=True)
    expo = jnp.exp2((scores - top) * SCORE)
    total = jnp.sum(expo, axis=0, keepdims=True)
    accum = jnp.dot(values, expo.astype(BF16), preferred_element_type=F32)
    result = jnp.concatenate(
        [
            accum[:HALF, :ROWS] / total[:, :ROWS],
            accum[HALF:, ROWS:] / total[:, ROWS:],
        ],
        axis=0,
    )
    return result.T.astype(BF16)


def kernel(
    count,
    ref_a,
    val_a,
    ref_b,
    val_b,
    w_a,
    w_b,
    out_a,
    out_b,
    held,
    turned,
    weights,
    attn,
    gathered,
    outgoing,
    incoming,
    own,
    weight_sem,
    share_send,
    share_recv,
    band_send,
    band_recv,
    attn_send,
    attn_recv,
    part_send,
    part_recv,
):
    blk, head = lax.axis_index("blk"), lax.axis_index("head")
    place = lax.rem(blk, 4)
    base = blk - place
    other = 1 - head
    following = lax.rem(blk + 4, count)
    previous = lax.rem(blk + count - 4, count)
    swapped = lax.rem(place, 2) * 2 + place // 2
    sources = ((ref_a, val_a), (ref_b, val_b))

    loads = [
        pltpu.make_async_copy(w, weights.at[side], weight_sem.at[side])
        for side, w in enumerate((w_a, w_b))
    ]
    for load in loads:
        load.start()

    barrier = pltpu.get_barrier_semaphore()
    for p in range(4):
        pl.semaphore_signal(barrier, inc=1, device_id={"blk": base + p, "head": other})
    pl.semaphore_signal(barrier, inc=1, device_id={"blk": following})
    pl.semaphore_signal(barrier, inc=1, device_id={"blk": previous})
    pl.semaphore_wait(barrier, 6)

    def share(side, p, t):
        return pltpu.make_async_remote_copy(
            src_ref=sources[side][t].at[:, pl.ds(p * PAIR, PAIR)],
            dst_ref=held.at[side, place + 1 + side, t],
            send_sem=share_send.at[side, p, t],
            recv_sem=share_recv.at[side, place, t],
            device_id={"blk": base + p, "head": other},
        )

    def send_shares(side):
        for t in range(2):
            for p in range(4):
                share(side, p, t).start()

    @pl.when(place < 2)
    def _():
        send_shares(0)
        send_shares(1)

    @pl.when(place >= 2)
    def _():
        send_shares(1)
        send_shares(0)

    def landed(ref, sem):
        pltpu.make_async_remote_copy(
            src_ref=ref, dst_ref=ref, send_sem=sem, recv_sem=sem, device_id={"head": other}
        ).wait_recv()

    def wait_share(side, block):
        for t in range(2):
            landed(held.at[side, block + 1 + side, t], share_recv.at[side, block, t])

    bands = ((0, 1, 5, 2, False), (1, 4, 0, 2, True), (1, 2, 6, 1, False), (0, 4, 0, 1, True))

    def band(index):
        side, first, target, blocks, forward = bands[index]
        return pltpu.make_async_remote_copy(
            src_ref=held.at[side, pl.ds(first, blocks)],
            dst_ref=held.at[side, pl.ds(target, blocks)],
            send_sem=band_send.at[index],
            recv_sem=band_recv.at[index],
            device_id={"blk": following if forward else previous},
        )

    def turn(side, first, blocks):
        for position in range(first, first + blocks):
            turned[side, position] = held[side, position, 1].T

    wait_share(0, 0)
    wait_share(0, 1)
    band(0).start()
    wait_share(1, 2)
    wait_share(1, 3)
    band(1).start()
    turn(0, 1, 2)
    turn(1, 4, 2)
    wait_share(1, 0)
    band(2).start()
    wait_share(0, 3)
    band(3).start()
    wait_share(1, 1)
    wait_share(0, 2)
    turn(1, 2, 2)
    turn(0, 3, 2)

    def attn_copies(side, n):
        if n in (0, 3):
            pieces = ((n, pl.ds(0, ROWS)),)
        else:
            pieces = (
                (n, pl.ds(pl.multiple_of(other * HALF, HALF), HALF)),
                (3 - n, pl.ds(pl.multiple_of(head * HALF, HALF), HALF)),
            )
        return [
            pltpu.make_async_remote_copy(
                src_ref=attn.at[side, n, rows],
                dst_ref=gathered.at[side, place, rows],
                send_sem=attn_send.at[side, n, index],
                recv_sem=attn_recv.at[side, place],
                device_id={"blk": base + target, "head": other},
            )
            for index, (target, rows) in enumerate(pieces)
        ]

    def work(side, n):
        keys = held[1 - side, n : n + 4, 0].reshape(4 * ROWS, PAIR)
        values = jnp.concatenate([turned[1 - side, n + k] for k in range(4)], axis=1)
        attn[side, n] = attend(held[side, n + 1 + side, 0], keys, values)
        for copy in attn_copies(side, n):
            copy.start()

    work(0, 2)
    work(1, 1)
    band(1).wait_recv()
    turn(1, 0, 2)
    work(0, 1)
    work(0, 0)
    band(2).wait_recv()
    turn(1, 6, 1)
    work(0, 3)
    band(0).wait_recv()
    turn(0, 5, 2)
    work(1, 2)
    work(1, 3)
    band(3).wait_recv()
    turn(0, 0, 1)
    work(1, 0)

    mine = pl.ds(pl.multiple_of(head * HALF, HALF), HALF)
    theirs = pl.ds(pl.multiple_of(other * HALF, HALF), HALF)

    def part(side, chunk):
        return pltpu.make_async_remote_copy(
            src_ref=outgoing.at[side, chunk],
            dst_ref=incoming.at[side, chunk],
            send_sem=part_send.at[side, chunk],
            recv_sem=part_recv.at[side, chunk],
            device_id={"blk": base + swapped, "head": other},
        )

    for side in range(2):
        loads[side].wait()
        for p in range(4):
            landed(gathered.at[side, p], attn_recv.at[side, p])
        rows = jnp.concatenate(
            [
                jnp.concatenate([gathered[side, p, half] for p in range(4)], axis=1)
                for half in (mine, theirs)
            ],
            axis=0,
        )
        for chunk in range(CHUNKS):
            product = jnp.dot(
                rows,
                weights[side, :, chunk * PIECE : (chunk + 1) * PIECE],
                preferred_element_type=F32,
            )
            outgoing[side, chunk] = product[HALF:].astype(BF16)
            part(side, chunk).start()
            own[side, chunk] = product[:HALF]

    for side, out in enumerate((out_a, out_b)):
        for chunk in range(CHUNKS):
            part(side, chunk).wait_recv()
            out[:, chunk * PIECE : (chunk + 1) * PIECE] = (
                own[side, chunk] + incoming[side, chunk].astype(F32)
            ).astype(BF16)

    for side in range(2):
        for p in range(4):
            for t in range(2):
                share(side, p, t).wait_send()
            for copy in attn_copies(side, p):
                copy.wait_send()
        for chunk in range(CHUNKS):
            part(side, chunk).wait_send()
    for index in range(len(bands)):
        band(index).wait_send()


def solution(mesh):
    count = mesh.shape["blk"]

    def shards(ref_a, val_a, ref_b, val_b, w_out_a, w_out_b):
        anywhere = pl.BlockSpec(memory_space=pl.ANY)
        vmem = pl.BlockSpec(memory_space=pltpu.VMEM)
        out = jax.ShapeDtypeStruct((HALF, WIDTH), BF16)
        return pl.pallas_call(
            functools.partial(kernel, count),
            out_shape=(out, out),
            in_specs=[anywhere] * 6,
            out_specs=(vmem, vmem),
            scratch_shapes=[
                pltpu.VMEM((2, 7, 2, ROWS, PAIR), BF16),
                pltpu.VMEM((2, 7, PAIR, ROWS), BF16),
                pltpu.VMEM((2, WIDTH // 2, WIDTH), BF16),
                pltpu.VMEM((2, 4, ROWS, PAIR), BF16),
                pltpu.VMEM((2, 4, ROWS, PAIR), BF16),
                pltpu.VMEM((2, CHUNKS, HALF, PIECE), BF16),
                pltpu.VMEM((2, CHUNKS, HALF, PIECE), BF16),
                pltpu.VMEM((2, CHUNKS, HALF, PIECE), F32),
                pltpu.SemaphoreType.DMA((2,)),
                pltpu.SemaphoreType.DMA((2, 4, 2)),
                pltpu.SemaphoreType.DMA((2, 4, 2)),
                pltpu.SemaphoreType.DMA((4,)),
                pltpu.SemaphoreType.DMA((4,)),
                pltpu.SemaphoreType.DMA((2, 4, 2)),
                pltpu.SemaphoreType.DMA((2, 4)),
                pltpu.SemaphoreType.DMA((2, CHUNKS)),
                pltpu.SemaphoreType.DMA((2, CHUNKS)),
            ],
            compiler_params=pltpu.CompilerParams(
                collective_id=0, has_side_effects=True, vmem_limit_bytes=32 * 1024 * 1024
            ),
        )(ref_a, val_a, ref_b, val_b, w_out_a, w_out_b)

    return jax.shard_map(
        shards,
        mesh=mesh,
        in_specs=(
            P("blk", "head"),
            P("blk", "head"),
            P("blk", "head"),
            P("blk", "head"),
            P("head", None),
            P("head", None),
        ),
        out_specs=(P(("blk", "head"), None), P(("blk", "head"), None)),
        check_vma=False,
    )
```

```python
import functools
import math

import jax
import jax.numpy as jnp
from jax import lax
from jax.experimental import pallas as pl
from jax.experimental.pallas import tpu as pltpu
from jax.sharding import PartitionSpec as P


ROWS = 128
HALF = 64
PAIR = 128
WIDTH = 1024
CHUNKS = 2
PIECE = WIDTH // CHUNKS
SCORE = 0.125 * math.log2(math.e)
BF16 = jnp.bfloat16
F32 = jnp.float32


def attend(query, keys, values):
    lane = lax.broadcasted_iota(jnp.int32, (ROWS, PAIR), 1)
    query = query.astype(F32)
    zero = jnp.zeros_like(query)
    both = jnp.concatenate(
        [jnp.where(lane < HALF, query, zero), jnp.where(lane < HALF, zero, query)], axis=0
    ).astype(BF16)
    scores = lax.dot_general(keys, both, (((1,), (1,)), ((), ())), preferred_element_type=F32)
    top = jnp.max(scores, axis=0, keepdims=True)
    expo = jnp.exp2((scores - top) * SCORE)
    total = jnp.sum(expo, axis=0, keepdims=True)
    accum = jnp.dot(values, expo.astype(BF16), preferred_element_type=F32)
    result = jnp.concatenate(
        [
            accum[:HALF, :ROWS] / total[:, :ROWS],
            accum[HALF:, ROWS:] / total[:, ROWS:],
        ],
        axis=0,
    )
    return result.T.astype(BF16)


def kernel(
    count,
    ref_a,
    val_a,
    ref_b,
    val_b,
    w_a,
    w_b,
    out_a,
    out_b,
    held,
    turned,
    weights,
    attn,
    gathered,
    outgoing,
    incoming,
    own,
    weight_sem,
    share_send,
    share_recv,
    band_send,
    band_recv,
    attn_send,
    attn_recv,
    part_send,
    part_recv,
):
    blk, head = lax.axis_index("blk"), lax.axis_index("head")
    place = lax.rem(blk, 4)
    base = blk - place
    other = 1 - head
    following = lax.rem(blk + 4, count)
    previous = lax.rem(blk + count - 4, count)
    swapped = lax.rem(place, 2) * 2 + place // 2
    sources = ((ref_a, val_a), (ref_b, val_b))

    loads = [
        pltpu.make_async_copy(w, weights.at[side], weight_sem.at[side])
        for side, w in enumerate((w_a, w_b))
    ]
    for load in loads:
        load.start()

    barrier = pltpu.get_barrier_semaphore()
    for p in range(4):
        pl.semaphore_signal(barrier, inc=1, device_id={"blk": base + p, "head": other})
    pl.semaphore_signal(barrier, inc=1, device_id={"blk": following})
    pl.semaphore_signal(barrier, inc=1, device_id={"blk": previous})
    pl.semaphore_wait(barrier, 6)

    def share(side, p, t):
        return pltpu.make_async_remote_copy(
            src_ref=sources[side][t].at[:, pl.ds(p * PAIR, PAIR)],
            dst_ref=held.at[side, place + 1 + side, t],
            send_sem=share_send.at[side, p, t],
            recv_sem=share_recv.at[side, place, t],
            device_id={"blk": base + p, "head": other},
        )

    def send_shares(side):
        for t in range(2):
            for p in range(4):
                share(side, p, t).start()

    @pl.when(place < 2)
    def _():
        send_shares(0)
        send_shares(1)

    @pl.when(place >= 2)
    def _():
        send_shares(1)
        send_shares(0)

    def landed(ref, sem):
        pltpu.make_async_remote_copy(
            src_ref=ref, dst_ref=ref, send_sem=sem, recv_sem=sem, device_id={"head": other}
        ).wait_recv()

    def wait_share(side, block):
        for t in range(2):
            landed(held.at[side, block + 1 + side, t], share_recv.at[side, block, t])

    bands = ((0, 1, 5, 2, False), (1, 4, 0, 2, True), (1, 2, 6, 1, False), (0, 4, 0, 1, True))

    def band(index):
        side, first, target, blocks, forward = bands[index]
        return pltpu.make_async_remote_copy(
            src_ref=held.at[side, pl.ds(first, blocks)],
            dst_ref=held.at[side, pl.ds(target, blocks)],
            send_sem=band_send.at[index],
            recv_sem=band_recv.at[index],
            device_id={"blk": following if forward else previous},
        )

    def turn(side, first, blocks):
        for position in range(first, first + blocks):
            turned[side, position] = held[side, position, 1].T

    wait_share(0, 0)
    wait_share(0, 1)
    band(0).start()
    wait_share(1, 2)
    wait_share(1, 3)
    band(1).start()
    turn(0, 1, 2)
    turn(1, 4, 2)
    wait_share(1, 0)
    band(2).start()
    wait_share(0, 3)
    band(3).start()
    wait_share(1, 1)
    wait_share(0, 2)
    turn(1, 2, 2)
    turn(0, 3, 2)

    def attn_copies(side, n):
        if n in (0, 3):
            pieces = ((n, pl.ds(0, ROWS)),)
        else:
            pieces = (
                (n, pl.ds(pl.multiple_of(other * HALF, HALF), HALF)),
                (3 - n, pl.ds(pl.multiple_of(head * HALF, HALF), HALF)),
            )
        return [
            pltpu.make_async_remote_copy(
                src_ref=attn.at[side, n, rows],
                dst_ref=gathered.at[side, place, rows],
                send_sem=attn_send.at[side, n, index],
                recv_sem=attn_recv.at[side, place],
                device_id={"blk": base + target, "head": other},
            )
            for index, (target, rows) in enumerate(pieces)
        ]

    def work(side, n):
        keys = held[1 - side, n : n + 4, 0].reshape(4 * ROWS, PAIR)
        values = jnp.concatenate([turned[1 - side, n + k] for k in range(4)], axis=1)
        attn[side, n] = attend(held[side, n + 1 + side, 0], keys, values)
        for copy in attn_copies(side, n):
            copy.start()

    work(0, 2)
    work(1, 1)
    band(1).wait_recv()
    turn(1, 0, 2)
    work(0, 1)
    work(0, 0)
    band(2).wait_recv()
    turn(1, 6, 1)
    work(0, 3)
    band(0).wait_recv()
    turn(0, 5, 2)
    work(1, 2)
    work(1, 3)
    band(3).wait_recv()
    turn(0, 0, 1)
    work(1, 0)

    mine = pl.ds(pl.multiple_of(head * HALF, HALF), HALF)
    theirs = pl.ds(pl.multiple_of(other * HALF, HALF), HALF)

    def part(side, chunk):
        return pltpu.make_async_remote_copy(
            src_ref=outgoing.at[side, chunk],
            dst_ref=incoming.at[side, chunk],
            send_sem=part_send.at[side, chunk],
            recv_sem=part_recv.at[side, chunk],
            device_id={"blk": base + swapped, "head": other},
        )

    for side in range(2):
        loads[side].wait()
        for p in range(4):
            landed(gathered.at[side, p], attn_recv.at[side, p])
        rows = jnp.concatenate(
            [
                jnp.concatenate([gathered[side, p, half] for p in range(4)], axis=1)
                for half in (mine, theirs)
            ],
            axis=0,
        )
        for chunk in range(CHUNKS):
            product = jnp.dot(
                rows,
                weights[side, :, chunk * PIECE : (chunk + 1) * PIECE],
                preferred_element_type=F32,
            )
            outgoing[side, chunk] = product[HALF:].astype(BF16)
            part(side, chunk).start()
            own[side, chunk] = product[:HALF]

    for side, out in enumerate((out_a, out_b)):
        for chunk in range(CHUNKS):
            part(side, chunk).wait_recv()
            out[:, chunk * PIECE : (chunk + 1) * PIECE] = (
                own[side, chunk] + incoming[side, chunk].astype(F32)
            ).astype(BF16)

    for side in range(2):
        for p in range(4):
            for t in range(2):
                share(side, p, t).wait_send()
            for copy in attn_copies(side, p):
                copy.wait_send()
        for chunk in range(CHUNKS):
            part(side, chunk).wait_send()
    for index in range(len(bands)):
        band(index).wait_send()


def leave(from_a, from_b, out_a, out_b, sem):
    copies = [
        pltpu.make_async_copy(source, target, sem.at[index])
        for index, (source, target) in enumerate(((from_a, out_a), (from_b, out_b)))
    ]
    for copy in copies:
        copy.start()
    for copy in copies:
        copy.wait()


def solution(mesh):
    count = mesh.shape["blk"]

    def shards(ref_a, val_a, ref_b, val_b, w_out_a, w_out_b):
        hbm = pl.BlockSpec(memory_space=pltpu.HBM)
        vmem = pl.BlockSpec(memory_space=pltpu.VMEM)
        out = jax.ShapeDtypeStruct((HALF, WIDTH), BF16)
        results = pl.pallas_call(
            functools.partial(kernel, count),
            out_shape=(out, out),
            in_specs=[hbm] * 6,
            out_specs=(vmem, vmem),
            scratch_shapes=[
                pltpu.VMEM((2, 7, 2, ROWS, PAIR), BF16),
                pltpu.VMEM((2, 7, PAIR, ROWS), BF16),
                pltpu.VMEM((2, WIDTH // 2, WIDTH), BF16),
                pltpu.VMEM((2, 4, ROWS, PAIR), BF16),
                pltpu.VMEM((2, 4, ROWS, PAIR), BF16),
                pltpu.VMEM((2, CHUNKS, HALF, PIECE), BF16),
                pltpu.VMEM((2, CHUNKS, HALF, PIECE), BF16),
                pltpu.VMEM((2, CHUNKS, HALF, PIECE), F32),
                pltpu.SemaphoreType.DMA((2,)),
                pltpu.SemaphoreType.DMA((2, 4, 2)),
                pltpu.SemaphoreType.DMA((2, 4, 2)),
                pltpu.SemaphoreType.DMA((4,)),
                pltpu.SemaphoreType.DMA((4,)),
                pltpu.SemaphoreType.DMA((2, 4, 2)),
                pltpu.SemaphoreType.DMA((2, 4)),
                pltpu.SemaphoreType.DMA((2, CHUNKS)),
                pltpu.SemaphoreType.DMA((2, CHUNKS)),
            ],
            compiler_params=pltpu.CompilerParams(
                collective_id=0, has_side_effects=True, vmem_limit_bytes=32 * 1024 * 1024
            ),
        )(
            *(
                pltpu.with_memory_space_constraint(array, pltpu.HBM)
                for array in (ref_a, val_a, ref_b, val_b, w_out_a, w_out_b)
            )
        )
        return pl.pallas_call(
            leave,
            out_shape=(out, out),
            in_specs=[vmem, vmem],
            out_specs=(hbm, hbm),
            scratch_shapes=[pltpu.SemaphoreType.DMA((2,))],
        )(*results)

    return jax.shard_map(
        shards,
        mesh=mesh,
        in_specs=(
            P("blk", "head"),
            P("blk", "head"),
            P("blk", "head"),
            P("blk", "head"),
            P("head", None),
            P("head", None),
        ),
        out_specs=(P(("blk", "head"), None), P(("blk", "head"), None)),
        check_vma=False,
    )
```

```python
import functools
import math

import jax
import jax.numpy as jnp
from jax import lax
from jax.experimental import pallas as pl
from jax.experimental.pallas import tpu as pltpu
from jax.sharding import PartitionSpec as P


ROWS = 128
HALF = 64
PAIR = 128
WIDTH = 1024
CHUNKS = 2
PIECE = WIDTH // CHUNKS
SCORE = 0.125 * math.log2(math.e)
BF16 = jnp.bfloat16
F32 = jnp.float32


def attend(query, keys, values):
    lane = lax.broadcasted_iota(jnp.int32, (ROWS, PAIR), 1)
    query = query.astype(F32)
    zero = jnp.zeros_like(query)
    both = jnp.concatenate(
        [jnp.where(lane < HALF, query, zero), jnp.where(lane < HALF, zero, query)], axis=0
    ).astype(BF16)
    scores = lax.dot_general(keys, both, (((1,), (1,)), ((), ())), preferred_element_type=F32)
    top = jnp.max(scores, axis=0, keepdims=True)
    expo = jnp.exp2((scores - top) * SCORE)
    total = jnp.sum(expo, axis=0, keepdims=True)
    accum = jnp.dot(values, expo.astype(BF16), preferred_element_type=F32)
    result = jnp.concatenate(
        [
            accum[:HALF, :ROWS] / total[:, :ROWS],
            accum[HALF:, ROWS:] / total[:, ROWS:],
        ],
        axis=0,
    )
    return result.T.astype(BF16)


def kernel(
    count,
    ref_a,
    val_a,
    ref_b,
    val_b,
    w_a,
    w_b,
    out_a,
    out_b,
    held,
    turned,
    weights,
    attn,
    gathered,
    outgoing,
    incoming,
    own,
    weight_sem,
    share_send,
    share_recv,
    band_send,
    band_recv,
    attn_send,
    attn_recv,
    part_send,
    part_recv,
):
    blk, head = lax.axis_index("blk"), lax.axis_index("head")
    place = lax.rem(blk, 4)
    base = blk - place
    other = 1 - head
    following = lax.rem(blk + 4, count)
    previous = lax.rem(blk + count - 4, count)
    swapped = lax.rem(place, 2) * 2 + place // 2
    sources = ((ref_a, val_a), (ref_b, val_b))

    loads = [
        pltpu.make_async_copy(w, weights.at[side], weight_sem.at[side])
        for side, w in enumerate((w_a, w_b))
    ]
    for load in loads:
        load.start()

    barrier = pltpu.get_barrier_semaphore()
    for p in range(4):
        pl.semaphore_signal(barrier, inc=1, device_id={"blk": base + p, "head": other})
    pl.semaphore_signal(barrier, inc=1, device_id={"blk": following})
    pl.semaphore_signal(barrier, inc=1, device_id={"blk": previous})
    pl.semaphore_wait(barrier, 6)

    def share(side, p, t):
        return pltpu.make_async_remote_copy(
            src_ref=sources[side][t].at[:, pl.ds(p * PAIR, PAIR)],
            dst_ref=held.at[side, place + 1 + side, t],
            send_sem=share_send.at[side, p, t],
            recv_sem=share_recv.at[side, place, t],
            device_id={"blk": base + p, "head": other},
        )

    def send_shares(side):
        for t in range(2):
            for p in range(4):
                share(side, p, t).start()

    @pl.when(place < 2)
    def _():
        send_shares(0)
        send_shares(1)

    @pl.when(place >= 2)
    def _():
        send_shares(1)
        send_shares(0)

    def landed(ref, sem):
        pltpu.make_async_remote_copy(
            src_ref=ref, dst_ref=ref, send_sem=sem, recv_sem=sem, device_id={"head": other}
        ).wait_recv()

    def wait_share(side, block):
        for t in range(2):
            landed(held.at[side, block + 1 + side, t], share_recv.at[side, block, t])

    bands = ((0, 1, 5, 2, False), (1, 4, 0, 2, True), (1, 2, 6, 1, False), (0, 4, 0, 1, True))

    def band(index):
        side, first, target, blocks, forward = bands[index]
        return pltpu.make_async_remote_copy(
            src_ref=held.at[side, pl.ds(first, blocks)],
            dst_ref=held.at[side, pl.ds(target, blocks)],
            send_sem=band_send.at[index],
            recv_sem=band_recv.at[index],
            device_id={"blk": following if forward else previous},
        )

    def turn(side, first, blocks):
        @pl.loop(first, first + blocks)
        def _(position):
            turned[side, position] = held[side, position, 1].T

    wait_share(0, 0)
    wait_share(0, 1)
    band(0).start()
    wait_share(1, 2)
    wait_share(1, 3)
    band(1).start()
    wait_share(1, 0)
    band(2).start()
    wait_share(0, 3)
    band(3).start()
    wait_share(1, 1)
    wait_share(0, 2)
    turn(0, 1, 4)
    turn(1, 2, 4)

    def attn_copies(side, n):
        pieces = (
            (n, pl.ds(pl.multiple_of(other * HALF, HALF), HALF)),
            (lax.rem(n, 2) * 2 + n // 2, pl.ds(pl.multiple_of(head * HALF, HALF), HALF)),
        )
        return [
            pltpu.make_async_remote_copy(
                src_ref=attn.at[side, n, rows],
                dst_ref=gathered.at[side, place, rows],
                send_sem=attn_send.at[side, n, index],
                recv_sem=attn_recv.at[side, place],
                device_id={"blk": base + target, "head": other},
            )
            for index, (target, rows) in enumerate(pieces)
        ]

    def work(side, n):
        keys = held[1 - side, pl.ds(n, 4), 0].reshape(4 * ROWS, PAIR)
        values = jnp.concatenate([turned[1 - side, n + k] for k in range(4)], axis=1)
        attn[side, n] = attend(held[side, n + 1 + side, 0], keys, values)

    @pl.loop(0, 4)
    def _(step):
        @pl.when(step == 1)
        def _():
            band(1).wait_recv()
            turn(1, 0, 2)
            band(0).wait_recv()
            turn(0, 5, 2)

        @pl.when(step == 3)
        def _():
            band(2).wait_recv()
            turn(1, 6, 1)
            band(3).wait_recv()
            turn(0, 0, 1)

        block = lax.rem(6 - step, 4)
        work(0, block)
        work(1, 3 - block)
        for copy in attn_copies(0, block) + attn_copies(1, 3 - block):
            copy.start()

    mine = pl.ds(pl.multiple_of(head * HALF, HALF), HALF)
    theirs = pl.ds(pl.multiple_of(other * HALF, HALF), HALF)

    def part(side, chunk):
        return pltpu.make_async_remote_copy(
            src_ref=outgoing.at[side, chunk],
            dst_ref=incoming.at[side, chunk],
            send_sem=part_send.at[side, chunk],
            recv_sem=part_recv.at[side, chunk],
            device_id={"blk": base + swapped, "head": other},
        )

    for side in range(2):
        loads[side].wait()
        for p in range(4):
            landed(gathered.at[side, p], attn_recv.at[side, p])
        rows = jnp.concatenate(
            [
                jnp.concatenate([gathered[side, p, half] for p in range(4)], axis=1)
                for half in (mine, theirs)
            ],
            axis=0,
        )
        for chunk in range(CHUNKS):
            product = jnp.dot(
                rows,
                weights[side, :, chunk * PIECE : (chunk + 1) * PIECE],
                preferred_element_type=F32,
            )
            outgoing[side, chunk] = product[HALF:].astype(BF16)
            part(side, chunk).start()
            own[side, chunk] = product[:HALF]

    for side, out in enumerate((out_a, out_b)):
        for chunk in range(CHUNKS):
            part(side, chunk).wait_recv()
            out[:, chunk * PIECE : (chunk + 1) * PIECE] = (
                own[side, chunk] + incoming[side, chunk].astype(F32)
            ).astype(BF16)

    for side in range(2):
        for p in range(4):
            for t in range(2):
                share(side, p, t).wait_send()
            for copy in attn_copies(side, p):
                copy.wait_send()
        for chunk in range(CHUNKS):
            part(side, chunk).wait_send()
    for index in range(len(bands)):
        band(index).wait_send()


def solution(mesh):
    count = mesh.shape["blk"]

    def shards(ref_a, val_a, ref_b, val_b, w_out_a, w_out_b):
        hbm = pl.BlockSpec(memory_space=pltpu.HBM)
        vmem = pl.BlockSpec(memory_space=pltpu.VMEM)
        out = pltpu.VMEM((HALF, WIDTH), BF16)
        return pl.pallas_call(
            functools.partial(kernel, count),
            out_shape=(out, out),
            in_specs=[hbm] * 6,
            out_specs=(vmem, vmem),
            scratch_shapes=[
                pltpu.VMEM((2, 7, 2, ROWS, PAIR), BF16),
                pltpu.VMEM((2, 7, PAIR, ROWS), BF16),
                pltpu.VMEM((2, WIDTH // 2, WIDTH), BF16),
                pltpu.VMEM((2, 4, ROWS, PAIR), BF16),
                pltpu.VMEM((2, 4, ROWS, PAIR), BF16),
                pltpu.VMEM((2, CHUNKS, HALF, PIECE), BF16),
                pltpu.VMEM((2, CHUNKS, HALF, PIECE), BF16),
                pltpu.VMEM((2, CHUNKS, HALF, PIECE), F32),
                pltpu.SemaphoreType.DMA((2,)),
                pltpu.SemaphoreType.DMA((2, 4, 2)),
                pltpu.SemaphoreType.DMA((2, 4, 2)),
                pltpu.SemaphoreType.DMA((4,)),
                pltpu.SemaphoreType.DMA((4,)),
                pltpu.SemaphoreType.DMA((2, 4, 2)),
                pltpu.SemaphoreType.DMA((2, 4)),
                pltpu.SemaphoreType.DMA((2, CHUNKS)),
                pltpu.SemaphoreType.DMA((2, CHUNKS)),
            ],
            compiler_params=pltpu.CompilerParams(
                collective_id=0, has_side_effects=True, vmem_limit_bytes=32 * 1024 * 1024
            ),
        )(
            *(
                pltpu.with_memory_space_constraint(array, pltpu.HBM)
                for array in (ref_a, val_a, ref_b, val_b, w_out_a, w_out_b)
            )
        )

    return jax.shard_map(
        shards,
        mesh=mesh,
        in_specs=(
            P("blk", "head"),
            P("blk", "head"),
            P("blk", "head"),
            P("blk", "head"),
            P("head", None),
            P("head", None),
        ),
        out_specs=(P(("blk", "head"), None), P(("blk", "head"), None)),
        check_vma=False,
    )
```

```python
import functools
import math

import jax
import jax.numpy as jnp
from jax import lax
from jax.experimental import pallas as pl
from jax.experimental.pallas import tpu as pltpu
from jax.sharding import PartitionSpec as P


ROWS = 128
HALF = 64
PAIR = 128
WIDTH = 1024
CHUNKS = 2
PIECE = WIDTH // CHUNKS
SCORE = 0.125 * math.log2(math.e)
BF16 = jnp.bfloat16
F32 = jnp.float32


def attend(query, keys, values):
    lane = lax.broadcasted_iota(jnp.int32, (ROWS, PAIR), 1)
    query = query.astype(F32)
    zero = jnp.zeros_like(query)
    both = jnp.concatenate(
        [jnp.where(lane < HALF, query, zero), jnp.where(lane < HALF, zero, query)], axis=0
    ).astype(BF16)
    scores = lax.dot_general(keys, both, (((1,), (1,)), ((), ())), preferred_element_type=F32)
    top = jnp.max(scores, axis=0, keepdims=True)
    expo = jnp.exp2((scores - top) * SCORE)
    total = jnp.sum(expo, axis=0, keepdims=True)
    accum = jnp.dot(values, expo.astype(BF16), preferred_element_type=F32)
    result = jnp.concatenate(
        [
            accum[:HALF, :ROWS] / total[:, :ROWS],
            accum[HALF:, ROWS:] / total[:, ROWS:],
        ],
        axis=0,
    )
    return result.T.astype(BF16)


def kernel(
    count,
    ref_a,
    val_a,
    ref_b,
    val_b,
    w_a,
    w_b,
    out_a,
    out_b,
    held,
    turned,
    weights,
    attn,
    gathered,
    outgoing,
    incoming,
    own,
    weight_sem,
    share_send,
    share_recv,
    band_send,
    band_recv,
    attn_send,
    attn_recv,
    part_send,
    part_recv,
):
    blk, head = lax.axis_index("blk"), lax.axis_index("head")
    place = lax.rem(blk, 4)
    base = blk - place
    other = 1 - head
    following = lax.rem(blk + 4, count)
    previous = lax.rem(blk + count - 4, count)
    swapped = lax.rem(place, 2) * 2 + place // 2
    sources = ((ref_a, val_a), (ref_b, val_b))

    loads = [
        pltpu.make_async_copy(w, weights.at[side], weight_sem.at[side])
        for side, w in enumerate((w_a, w_b))
    ]
    for load in loads:
        load.start()

    barrier = pltpu.get_barrier_semaphore()
    for p in range(4):
        pl.semaphore_signal(barrier, inc=1, device_id={"blk": base + p, "head": other})
    pl.semaphore_signal(barrier, inc=1, device_id={"blk": following})
    pl.semaphore_signal(barrier, inc=1, device_id={"blk": previous})
    pl.semaphore_wait(barrier, 6)

    def share(side, p, t):
        return pltpu.make_async_remote_copy(
            src_ref=sources[side][t].at[:, pl.ds(p * PAIR, PAIR)],
            dst_ref=held.at[side, t, place + 1 + side],
            send_sem=share_send.at[side, p, t],
            recv_sem=share_recv.at[side, place, t],
            device_id={"blk": base + p, "head": other},
        )

    for side in (1, 0):
        for t in range(2):
            for p in range(4):
                share(side, p, t).start()

    def landed(ref, sem):
        pltpu.make_async_remote_copy(
            src_ref=ref, dst_ref=ref, send_sem=sem, recv_sem=sem, device_id={"head": other}
        ).wait_recv()

    def wait_share(side, t, blocks):
        for block in blocks:
            landed(held.at[side, t, block + 1 + side], share_recv.at[side, block, t])

    bands = (((1, 5, 2, False), (4, 0, 1, True)), ((4, 0, 2, True), (2, 6, 1, False)))

    def band(side, t, index):
        first, target, blocks, forward = bands[side][index]
        return pltpu.make_async_remote_copy(
            src_ref=held.at[side, t, pl.ds(first, blocks)],
            dst_ref=held.at[side, t, pl.ds(target, blocks)],
            send_sem=band_send.at[side, t, index],
            recv_sem=band_recv.at[side, t, index],
            device_id={"blk": following if forward else previous},
        )

    def forward(side, t):
        for index, (first, _, blocks, _) in enumerate(bands[side]):
            block = first - 1 - side
            wait_share(side, t, range(block, block + blocks))
            band(side, t, index).start()

    def wait_band(side):
        for t in range(2):
            for index in range(2):
                band(side, t, index).wait_recv()

    def turn(side, first, blocks):
        @pl.loop(first, first + blocks)
        def _(position):
            turned[side, position] = held[side, 1, position].T

    def attn_copies(side, n):
        pieces = (
            (n, pl.ds(pl.multiple_of(other * HALF, HALF), HALF)),
            (lax.rem(n, 2) * 2 + n // 2, pl.ds(pl.multiple_of(head * HALF, HALF), HALF)),
        )
        return [
            pltpu.make_async_remote_copy(
                src_ref=attn.at[side, n, rows],
                dst_ref=gathered.at[side, place, rows],
                send_sem=attn_send.at[side, n, index],
                recv_sem=attn_recv.at[side, place],
                device_id={"blk": base + target, "head": other},
            )
            for index, (target, rows) in enumerate(pieces)
        ]

    def work(side, n):
        keys = held[1 - side, 0, pl.ds(n, 4)].reshape(4 * ROWS, PAIR)
        values = jnp.concatenate([turned[1 - side, n + k] for k in range(4)], axis=1)
        attn[side, n] = attend(held[side, 0, n + 1 + side], keys, values)
        for copy in attn_copies(side, n):
            copy.start()

    forward(1, 0)
    forward(1, 1)
    wait_share(1, 0, (1,))
    wait_share(1, 1, (1,))
    turn(1, 2, 4)
    forward(0, 0)
    wait_share(0, 0, (2,))
    work(0, 2)
    forward(0, 1)
    wait_share(0, 1, (2,))
    wait_band(1)
    turn(1, 0, 2)
    turn(1, 6, 1)

    @pl.loop(0, 3)
    def _(step):
        work(0, lax.rem(5 - step, 4))

    turn(0, 1, 4)
    work(1, 1)
    wait_band(0)
    turn(0, 0, 1)
    turn(0, 5, 2)

    @pl.loop(0, 3)
    def _(step):
        work(1, lax.rem(step + 2, 4))

    mine = pl.ds(pl.multiple_of(head * HALF, HALF), HALF)
    theirs = pl.ds(pl.multiple_of(other * HALF, HALF), HALF)

    def part(side, chunk):
        return pltpu.make_async_remote_copy(
            src_ref=outgoing.at[side, chunk],
            dst_ref=incoming.at[side, chunk],
            send_sem=part_send.at[side, chunk],
            recv_sem=part_recv.at[side, chunk],
            device_id={"blk": base + swapped, "head": other},
        )

    for side in range(2):
        loads[side].wait()
        for p in range(4):
            landed(gathered.at[side, p], attn_recv.at[side, p])
        rows = jnp.concatenate(
            [
                jnp.concatenate([gathered[side, p, half] for p in range(4)], axis=1)
                for half in (mine, theirs)
            ],
            axis=0,
        )
        for chunk in range(CHUNKS):
            product = jnp.dot(
                rows,
                weights[side, :, chunk * PIECE : (chunk + 1) * PIECE],
                preferred_element_type=F32,
            )
            outgoing[side, chunk] = product[HALF:].astype(BF16)
            part(side, chunk).start()
            own[side, chunk] = product[:HALF]

    for side, out in enumerate((out_a, out_b)):
        for chunk in range(CHUNKS):
            part(side, chunk).wait_recv()
            out[:, chunk * PIECE : (chunk + 1) * PIECE] = (
                own[side, chunk] + incoming[side, chunk].astype(F32)
            ).astype(BF16)

    for side in range(2):
        for p in range(4):
            for t in range(2):
                share(side, p, t).wait_send()
            for copy in attn_copies(side, p):
                copy.wait_send()
        for chunk in range(CHUNKS):
            part(side, chunk).wait_send()
        for t in range(2):
            for index in range(2):
                band(side, t, index).wait_send()


def solution(mesh):
    count = mesh.shape["blk"]

    def shards(ref_a, val_a, ref_b, val_b, w_out_a, w_out_b):
        hbm = pl.BlockSpec(memory_space=pltpu.HBM)
        vmem = pl.BlockSpec(memory_space=pltpu.VMEM)
        out = pltpu.VMEM((HALF, WIDTH), BF16)
        return pl.pallas_call(
            functools.partial(kernel, count),
            out_shape=(out, out),
            in_specs=[hbm] * 6,
            out_specs=(vmem, vmem),
            scratch_shapes=[
                pltpu.VMEM((2, 2, 7, ROWS, PAIR), BF16),
                pltpu.VMEM((2, 7, PAIR, ROWS), BF16),
                pltpu.VMEM((2, WIDTH // 2, WIDTH), BF16),
                pltpu.VMEM((2, 4, ROWS, PAIR), BF16),
                pltpu.VMEM((2, 4, ROWS, PAIR), BF16),
                pltpu.VMEM((2, CHUNKS, HALF, PIECE), BF16),
                pltpu.VMEM((2, CHUNKS, HALF, PIECE), BF16),
                pltpu.VMEM((2, CHUNKS, HALF, PIECE), F32),
                pltpu.SemaphoreType.DMA((2,)),
                pltpu.SemaphoreType.DMA((2, 4, 2)),
                pltpu.SemaphoreType.DMA((2, 4, 2)),
                pltpu.SemaphoreType.DMA((2, 2, 2)),
                pltpu.SemaphoreType.DMA((2, 2, 2)),
                pltpu.SemaphoreType.DMA((2, 4, 2)),
                pltpu.SemaphoreType.DMA((2, 4)),
                pltpu.SemaphoreType.DMA((2, CHUNKS)),
                pltpu.SemaphoreType.DMA((2, CHUNKS)),
            ],
            compiler_params=pltpu.CompilerParams(
                collective_id=0, has_side_effects=True, vmem_limit_bytes=32 * 1024 * 1024
            ),
        )(
            *(
                pltpu.with_memory_space_constraint(array, pltpu.HBM)
                for array in (ref_a, val_a, ref_b, val_b, w_out_a, w_out_b)
            )
        )

    return jax.shard_map(
        shards,
        mesh=mesh,
        in_specs=(
            P("blk", "head"),
            P("blk", "head"),
            P("blk", "head"),
            P("blk", "head"),
            P("head", None),
            P("head", None),
        ),
        out_specs=(P(("blk", "head"), None), P(("blk", "head"), None)),
        check_vma=False,
    )
```

```python
import functools
import math

import jax
import jax.numpy as jnp
from jax import lax
from jax.experimental import pallas as pl
from jax.experimental.pallas import tpu as pltpu
from jax.sharding import PartitionSpec as P


ROWS = 128
HALF = 64
PAIR = 128
WIDTH = 1024
CHUNKS = 2
PIECE = WIDTH // CHUNKS
SCORE = 0.125 * math.log2(math.e)
BF16 = jnp.bfloat16
F32 = jnp.float32


def attend(query, keys, values):
    lane = lax.broadcasted_iota(jnp.int32, (ROWS, PAIR), 1)
    query = query.astype(F32)
    zero = jnp.zeros_like(query)
    both = jnp.concatenate(
        [jnp.where(lane < HALF, query, zero), jnp.where(lane < HALF, zero, query)], axis=0
    ).astype(BF16)
    scores = lax.dot_general(keys, both, (((1,), (1,)), ((), ())), preferred_element_type=F32)
    top = jnp.max(scores, axis=0, keepdims=True)
    expo = jnp.exp2((scores - top) * SCORE)
    total = jnp.sum(expo, axis=0, keepdims=True)
    accum = jnp.dot(values, expo.astype(BF16), preferred_element_type=F32)
    result = jnp.concatenate(
        [
            accum[:HALF, :ROWS] / total[:, :ROWS],
            accum[HALF:, ROWS:] / total[:, ROWS:],
        ],
        axis=0,
    )
    return result.T.astype(BF16)


def kernel(
    count,
    ref_a,
    val_a,
    ref_b,
    val_b,
    w_a,
    w_b,
    out_a,
    out_b,
    staged,
    held,
    turned,
    weights,
    attn,
    gathered,
    outgoing,
    incoming,
    own,
    weight_sem,
    stage_sem,
    share_send,
    share_recv,
    band_send,
    band_recv,
    attn_send,
    attn_recv,
    part_send,
    part_recv,
):
    blk, head = lax.axis_index("blk"), lax.axis_index("head")
    place = lax.rem(blk, 4)
    base = blk - place
    other = 1 - head
    following = lax.rem(blk + 4, count)
    previous = lax.rem(blk + count - 4, count)
    swapped = lax.rem(place, 2) * 2 + place // 2

    barrier = pltpu.get_barrier_semaphore()
    for p in range(4):
        pl.semaphore_signal(barrier, inc=1, device_id={"blk": base + p, "head": other})
    pl.semaphore_signal(barrier, inc=1, device_id={"blk": following})
    pl.semaphore_signal(barrier, inc=1, device_id={"blk": previous})

    loads = [
        pltpu.make_async_copy(w, weights.at[side], weight_sem.at[side])
        for side, w in enumerate((w_a, w_b))
    ]
    for side, pair in enumerate(((ref_a, val_a), (ref_b, val_b))):
        for p in range(4):
            for t in range(2):
                pltpu.make_async_copy(
                    pair[t].at[:, pl.ds(p * PAIR, PAIR)], staged.at[side, p, t], stage_sem.at[side]
                ).start()
    for load in loads:
        load.start()

    pl.semaphore_wait(barrier, 6)

    def share(side, p):
        return pltpu.make_async_remote_copy(
            src_ref=staged.at[side, p],
            dst_ref=held.at[side, place + 1 + side],
            send_sem=share_send.at[side, p],
            recv_sem=share_recv.at[side, place],
            device_id={"blk": base + p, "head": other},
        )

    ahead = place // 2
    for side in (ahead, 1 - ahead):
        pltpu.make_async_copy(staged.at[side], staged.at[side], stage_sem.at[side]).wait()
        for p in range(4):
            share(side, p).start()

    def landed(ref, sem):
        pltpu.make_async_remote_copy(
            src_ref=ref, dst_ref=ref, send_sem=sem, recv_sem=sem, device_id={"head": other}
        ).wait_recv()

    def wait_share(side, blocks):
        for block in blocks:
            landed(held.at[side, block + 1 + side], share_recv.at[side, block])

    bands = ((1, 4, 0, 2, True), (0, 1, 5, 2, False), (0, 4, 0, 1, True), (1, 2, 6, 1, False))

    def band(index):
        side, first, target, blocks, forward = bands[index]
        return pltpu.make_async_remote_copy(
            src_ref=held.at[side, pl.ds(first, blocks)],
            dst_ref=held.at[side, pl.ds(target, blocks)],
            send_sem=band_send.at[index],
            recv_sem=band_recv.at[index],
            device_id={"blk": following if forward else previous},
        )

    def turn(side, first, blocks):
        @pl.loop(first, first + blocks)
        def _(position):
            turned[side, position] = held[side, position, 1].T

    def attn_copies(side, n):
        pieces = (
            (n, pl.ds(pl.multiple_of(other * HALF, HALF), HALF)),
            (lax.rem(n, 2) * 2 + n // 2, pl.ds(pl.multiple_of(head * HALF, HALF), HALF)),
        )
        return [
            pltpu.make_async_remote_copy(
                src_ref=attn.at[side, n, rows],
                dst_ref=gathered.at[side, place, rows],
                send_sem=attn_send.at[side, n, index],
                recv_sem=attn_recv.at[side, place],
                device_id={"blk": base + target, "head": other},
            )
            for index, (target, rows) in enumerate(pieces)
        ]

    def work(*tasks):
        for side, n in tasks:
            keys = held[1 - side, pl.ds(n, 4), 0].reshape(4 * ROWS, PAIR)
            values = jnp.concatenate([turned[1 - side, n + k] for k in range(4)], axis=1)
            attn[side, n] = attend(held[side, n + 1 + side, 0], keys, values)
        for side, n in tasks:
            for copy in attn_copies(side, n):
                copy.start()

    for index, (side, first, _, blocks, _) in enumerate(bands):
        wait_share(side, range(first - 1 - side, first - 1 - side + blocks))
        band(index).start()
    wait_share(0, (2,))
    wait_share(1, (1,))
    turn(0, 1, 4)
    turn(1, 2, 4)
    work((0, 2), (1, 1))
    band(1).wait_recv()
    band(3).wait_recv()
    turn(0, 5, 2)
    turn(1, 6, 1)
    work((0, 3), (1, 2), (1, 3))
    band(0).wait_recv()
    turn(1, 0, 2)
    work((0, 1), (0, 0))
    band(2).wait_recv()
    turn(0, 0, 1)
    work((1, 0),)

    mine = pl.ds(pl.multiple_of(head * HALF, HALF), HALF)
    theirs = pl.ds(pl.multiple_of(other * HALF, HALF), HALF)

    def part(side, chunk):
        return pltpu.make_async_remote_copy(
            src_ref=outgoing.at[side, chunk],
            dst_ref=incoming.at[side, chunk],
            send_sem=part_send.at[side, chunk],
            recv_sem=part_recv.at[side, chunk],
            device_id={"blk": base + swapped, "head": other},
        )

    for side in range(2):
        loads[side].wait()
        for p in range(4):
            landed(gathered.at[side, p], attn_recv.at[side, p])
        rows = jnp.concatenate(
            [
                jnp.concatenate([gathered[side, p, half] for p in range(4)], axis=1)
                for half in (mine, theirs)
            ],
            axis=0,
        )
        for chunk in range(CHUNKS):
            product = jnp.dot(
                rows,
                weights[side, :, chunk * PIECE : (chunk + 1) * PIECE],
                preferred_element_type=F32,
            )
            outgoing[side, chunk] = product[HALF:].astype(BF16)
            part(side, chunk).start()
            own[side, chunk] = product[:HALF]

    for side, out in enumerate((out_a, out_b)):
        for chunk in range(CHUNKS):
            part(side, chunk).wait_recv()
            out[:, chunk * PIECE : (chunk + 1) * PIECE] = (
                own[side, chunk] + incoming[side, chunk].astype(F32)
            ).astype(BF16)

    for side in range(2):
        for p in range(4):
            share(side, p).wait_send()
            for copy in attn_copies(side, p):
                copy.wait_send()
        for chunk in range(CHUNKS):
            part(side, chunk).wait_send()
    for index in range(len(bands)):
        band(index).wait_send()


def solution(mesh):
    count = mesh.shape["blk"]

    def shards(ref_a, val_a, ref_b, val_b, w_out_a, w_out_b):
        hbm = pl.BlockSpec(memory_space=pltpu.HBM)
        vmem = pl.BlockSpec(memory_space=pltpu.VMEM)
        out = pltpu.VMEM((HALF, WIDTH), BF16)
        return pl.pallas_call(
            functools.partial(kernel, count),
            out_shape=(out, out),
            in_specs=[hbm] * 6,
            out_specs=(vmem, vmem),
            scratch_shapes=[
                pltpu.VMEM((2, 4, 2, ROWS, PAIR), BF16),
                pltpu.VMEM((2, 7, 2, ROWS, PAIR), BF16),
                pltpu.VMEM((2, 7, PAIR, ROWS), BF16),
                pltpu.VMEM((2, WIDTH // 2, WIDTH), BF16),
                pltpu.VMEM((2, 4, ROWS, PAIR), BF16),
                pltpu.VMEM((2, 4, ROWS, PAIR), BF16),
                pltpu.VMEM((2, CHUNKS, HALF, PIECE), BF16),
                pltpu.VMEM((2, CHUNKS, HALF, PIECE), BF16),
                pltpu.VMEM((2, CHUNKS, HALF, PIECE), F32),
                pltpu.SemaphoreType.DMA((2,)),
                pltpu.SemaphoreType.DMA((2,)),
                pltpu.SemaphoreType.DMA((2, 4)),
                pltpu.SemaphoreType.DMA((2, 4)),
                pltpu.SemaphoreType.DMA((4,)),
                pltpu.SemaphoreType.DMA((4,)),
                pltpu.SemaphoreType.DMA((2, 4, 2)),
                pltpu.SemaphoreType.DMA((2, 4)),
                pltpu.SemaphoreType.DMA((2, CHUNKS)),
                pltpu.SemaphoreType.DMA((2, CHUNKS)),
            ],
            compiler_params=pltpu.CompilerParams(
                collective_id=0, has_side_effects=True, vmem_limit_bytes=32 * 1024 * 1024
            ),
        )(
            *(
                pltpu.with_memory_space_constraint(array, pltpu.HBM)
                for array in (ref_a, val_a, ref_b, val_b, w_out_a, w_out_b)
            )
        )

    return jax.shard_map(
        shards,
        mesh=mesh,
        in_specs=(
            P("blk", "head"),
            P("blk", "head"),
            P("blk", "head"),
            P("blk", "head"),
            P("head", None),
            P("head", None),
        ),
        out_specs=(P(("blk", "head"), None), P(("blk", "head"), None)),
        check_vma=False,
    )
```

```python
import functools
import math

import jax
import jax.numpy as jnp
from jax import lax
from jax.experimental import pallas as pl
from jax.experimental.pallas import tpu as pltpu
from jax.sharding import PartitionSpec as P


ROWS = 128
HALF = 64
PAIR = 128
WIDTH = 1024
CHUNKS = 2
PIECE = WIDTH // CHUNKS
SCORE = 0.125 * math.log2(math.e)
BF16 = jnp.bfloat16
F32 = jnp.float32


def attend(query, keys, values):
    lane = lax.broadcasted_iota(jnp.int32, (ROWS, PAIR), 1)
    query = query.astype(F32)
    zero = jnp.zeros_like(query)
    both = jnp.concatenate(
        [jnp.where(lane < HALF, query, zero), jnp.where(lane < HALF, zero, query)], axis=0
    ).astype(BF16)
    scores = lax.dot_general(keys, both, (((1,), (1,)), ((), ())), preferred_element_type=F32)
    top = jnp.max(scores, axis=0, keepdims=True)
    expo = jnp.exp2((scores - top) * SCORE)
    total = jnp.sum(expo, axis=0, keepdims=True)
    accum = jnp.dot(values, expo.astype(BF16), preferred_element_type=F32)
    result = jnp.concatenate(
        [
            accum[:HALF, :ROWS] / total[:, :ROWS],
            accum[HALF:, ROWS:] / total[:, ROWS:],
        ],
        axis=0,
    )
    return result.T.astype(BF16)


def kernel(
    count,
    ref_a,
    val_a,
    ref_b,
    val_b,
    w_a,
    w_b,
    out_a,
    out_b,
    staged,
    held,
    turned,
    weights,
    attn,
    gathered,
    outgoing,
    incoming,
    own,
    weight_sem,
    stage_sem,
    share_send,
    share_recv,
    band_send,
    band_recv,
    attn_send,
    attn_recv,
    part_send,
    part_recv,
):
    blk, head = lax.axis_index("blk"), lax.axis_index("head")
    place = lax.rem(blk, 4)
    base = blk - place
    other = 1 - head
    following = lax.rem(blk + 4, count)
    previous = lax.rem(blk + count - 4, count)
    swapped = lax.rem(place, 2) * 2 + place // 2

    barrier = pltpu.get_barrier_semaphore()
    for p in range(4):
        pl.semaphore_signal(barrier, inc=1, device_id={"blk": base + p, "head": other})
    pl.semaphore_signal(barrier, inc=1, device_id={"blk": following})
    pl.semaphore_signal(barrier, inc=1, device_id={"blk": previous})

    loads = [
        pltpu.make_async_copy(w, weights.at[side], weight_sem.at[side])
        for side, w in enumerate((w_a, w_b))
    ]
    for side, pair in enumerate(((ref_a, val_a), (ref_b, val_b))):
        for p in range(4):
            for t in range(2):
                pltpu.make_async_copy(
                    pair[t].at[:, pl.ds(p * PAIR, PAIR)], staged.at[side, p, t], stage_sem.at[side]
                ).start()
    for load in loads:
        load.start()

    pl.semaphore_wait(barrier, 6)

    def landed(ref, sem):
        pltpu.make_async_remote_copy(
            src_ref=ref, dst_ref=ref, send_sem=sem, recv_sem=sem, device_id={"head": other}
        ).wait_recv()

    def left(ref, sem):
        pltpu.make_async_remote_copy(
            src_ref=ref, dst_ref=ref, send_sem=sem, recv_sem=sem, device_id={"head": other}
        ).wait_send()

    def share(side, p):
        return pltpu.make_async_remote_copy(
            src_ref=staged.at[side, p],
            dst_ref=held.at[side, place + 1 + side],
            send_sem=share_send.at[side],
            recv_sem=share_recv.at[side, place],
            device_id={"blk": base + p, "head": other},
        )

    ahead = place // 2
    pltpu.make_async_copy(staged.at[ahead], staged.at[ahead], stage_sem.at[ahead]).wait()
    for p in range(4):
        share(ahead, p).start()
    behind = 1 - ahead
    pltpu.make_async_copy(staged.at[behind], staged.at[behind], stage_sem.at[behind]).wait()
    left(staged.at[ahead], share_send.at[ahead])
    for p in range(4):
        share(behind, p).start()

    def wait_share(side, blocks):
        for block in blocks:
            landed(held.at[side, block + 1 + side], share_recv.at[side, block])

    bands = ((1, 4, 0, 2, True), (0, 1, 5, 2, False), (0, 4, 0, 1, True), (1, 2, 6, 1, False))

    def band(index):
        side, first, target, blocks, forward = bands[index]
        return pltpu.make_async_remote_copy(
            src_ref=held.at[side, pl.ds(first, blocks)],
            dst_ref=held.at[side, pl.ds(target, blocks)],
            send_sem=band_send,
            recv_sem=band_recv.at[index],
            device_id={"blk": following if forward else previous},
        )

    def turn(side, first, blocks):
        @pl.loop(first, first + blocks)
        def _(position):
            turned[side, position] = held[side, position, 1].T

    def attn_copies(side, n):
        if n in (0, 3):
            pieces = ((n, pl.ds(0, ROWS)),)
        else:
            pieces = (
                (n, pl.ds(pl.multiple_of(other * HALF, HALF), HALF)),
                (3 - n, pl.ds(pl.multiple_of(head * HALF, HALF), HALF)),
            )
        return [
            pltpu.make_async_remote_copy(
                src_ref=attn.at[side, n, rows],
                dst_ref=gathered.at[side, place, rows],
                send_sem=attn_send.at[side],
                recv_sem=attn_recv.at[side],
                device_id={"blk": base + target, "head": other},
            )
            for target, rows in pieces
        ]

    def work(*tasks):
        for side, n in tasks:
            keys = held[1 - side, pl.ds(n, 4), 0].reshape(4 * ROWS, PAIR)
            values = jnp.concatenate([turned[1 - side, n + k] for k in range(4)], axis=1)
            attn[side, n] = attend(held[side, n + 1 + side, 0], keys, values)
        for side, n in tasks:
            for copy in attn_copies(side, n):
                copy.start()

    for index, (side, first, _, blocks, _) in enumerate(bands):
        wait_share(side, range(first - 1 - side, first - 1 - side + blocks))
        band(index).start()
    wait_share(0, (2,))
    wait_share(1, (1,))
    turn(0, 1, 4)
    turn(1, 2, 4)
    work((0, 2), (1, 1))
    band(1).wait_recv()
    band(3).wait_recv()
    turn(0, 5, 2)
    turn(1, 6, 1)
    work((0, 3), (1, 2), (1, 3))
    band(0).wait_recv()
    turn(1, 0, 2)
    work((0, 1), (0, 0))
    band(2).wait_recv()
    turn(0, 0, 1)
    work((1, 0),)

    mine = pl.ds(pl.multiple_of(head * HALF, HALF), HALF)
    theirs = pl.ds(pl.multiple_of(other * HALF, HALF), HALF)

    def part(side, chunk):
        return pltpu.make_async_remote_copy(
            src_ref=outgoing.at[side, chunk],
            dst_ref=incoming.at[side, chunk],
            send_sem=part_send.at[side],
            recv_sem=part_recv.at[side, chunk],
            device_id={"blk": base + swapped, "head": other},
        )

    for side in range(2):
        loads[side].wait()
        landed(gathered.at[side], attn_recv.at[side])
        rows = jnp.concatenate(
            [
                jnp.concatenate([gathered[side, p, half] for p in range(4)], axis=1)
                for half in (mine, theirs)
            ],
            axis=0,
        )
        for chunk in range(CHUNKS):
            product = jnp.dot(
                rows,
                weights[side, :, chunk * PIECE : (chunk + 1) * PIECE],
                preferred_element_type=F32,
            )
            outgoing[side, chunk] = product[HALF:].astype(BF16)
            part(side, chunk).start()
            own[side, chunk] = product[:HALF]

    left(staged.at[behind], share_send.at[behind])
    left(held.at[0, pl.ds(0, 6)], band_send)
    for side in range(2):
        left(attn.at[side], attn_send.at[side])
        left(outgoing.at[side], part_send.at[side])

    for side, out in enumerate((out_a, out_b)):
        for chunk in range(CHUNKS):
            part(side, chunk).wait_recv()
            out[:, chunk * PIECE : (chunk + 1) * PIECE] = (
                own[side, chunk] + incoming[side, chunk].astype(F32)
            ).astype(BF16)


def solution(mesh):
    count = mesh.shape["blk"]

    def shards(ref_a, val_a, ref_b, val_b, w_out_a, w_out_b):
        hbm = pl.BlockSpec(memory_space=pltpu.HBM)
        vmem = pl.BlockSpec(memory_space=pltpu.VMEM)
        out = pltpu.VMEM((HALF, WIDTH), BF16)
        return pl.pallas_call(
            functools.partial(kernel, count),
            out_shape=(out, out),
            in_specs=[hbm] * 6,
            out_specs=(vmem, vmem),
            scratch_shapes=[
                pltpu.VMEM((2, 4, 2, ROWS, PAIR), BF16),
                pltpu.VMEM((2, 7, 2, ROWS, PAIR), BF16),
                pltpu.VMEM((2, 7, PAIR, ROWS), BF16),
                pltpu.VMEM((2, WIDTH // 2, WIDTH), BF16),
                pltpu.VMEM((2, 4, ROWS, PAIR), BF16),
                pltpu.VMEM((2, 4, ROWS, PAIR), BF16),
                pltpu.VMEM((2, CHUNKS, HALF, PIECE), BF16),
                pltpu.VMEM((2, CHUNKS, HALF, PIECE), BF16),
                pltpu.VMEM((2, CHUNKS, HALF, PIECE), F32),
                pltpu.SemaphoreType.DMA((2,)),
                pltpu.SemaphoreType.DMA((2,)),
                pltpu.SemaphoreType.DMA((2,)),
                pltpu.SemaphoreType.DMA((2, 4)),
                pltpu.SemaphoreType.DMA,
                pltpu.SemaphoreType.DMA((4,)),
                pltpu.SemaphoreType.DMA((2,)),
                pltpu.SemaphoreType.DMA((2,)),
                pltpu.SemaphoreType.DMA((2,)),
                pltpu.SemaphoreType.DMA((2, CHUNKS)),
            ],
            compiler_params=pltpu.CompilerParams(
                collective_id=0, has_side_effects=True, vmem_limit_bytes=32 * 1024 * 1024
            ),
        )(
            *(
                pltpu.with_memory_space_constraint(array, pltpu.HBM)
                for array in (ref_a, val_a, ref_b, val_b, w_out_a, w_out_b)
            )
        )

    return jax.shard_map(
        shards,
        mesh=mesh,
        in_specs=(
            P("blk", "head"),
            P("blk", "head"),
            P("blk", "head"),
            P("blk", "head"),
            P("head", None),
            P("head", None),
        ),
        out_specs=(P(("blk", "head"), None), P(("blk", "head"), None)),
        check_vma=False,
    )
```

```python
import functools
import math

import jax
import jax.numpy as jnp
from jax import lax
from jax.experimental import pallas as pl
from jax.experimental.pallas import tpu as pltpu
from jax.sharding import PartitionSpec as P


ROWS = 128
HALF = 64
PAIR = 128
WIDTH = 1024
CHUNKS = 2
PIECE = WIDTH // CHUNKS
SCORE = 0.125 * math.log2(math.e)
BF16 = jnp.bfloat16
F32 = jnp.float32


def attend(query, keys, values):
    lane = lax.broadcasted_iota(jnp.int32, (ROWS, PAIR), 1)
    query = query.astype(F32)
    zero = jnp.zeros_like(query)
    both = jnp.concatenate(
        [jnp.where(lane < HALF, query, zero), jnp.where(lane < HALF, zero, query)], axis=0
    ).astype(BF16)
    scores = lax.dot_general(keys, both, (((1,), (1,)), ((), ())), preferred_element_type=F32)
    top = jnp.max(scores, axis=0, keepdims=True)
    expo = jnp.exp2((scores - top) * SCORE)
    total = jnp.sum(expo, axis=0, keepdims=True)
    accum = jnp.dot(values, expo.astype(BF16), preferred_element_type=F32)
    result = jnp.concatenate(
        [
            accum[:HALF, :ROWS] / total[:, :ROWS],
            accum[HALF:, ROWS:] / total[:, ROWS:],
        ],
        axis=0,
    )
    return result.T.astype(BF16)


def kernel(
    count,
    ref_a,
    val_a,
    ref_b,
    val_b,
    w_a,
    w_b,
    out_a,
    out_b,
    staged,
    held,
    turned,
    weights,
    attn,
    gathered,
    outgoing,
    incoming,
    own,
    weight_sem,
    stage_sem,
    share_send,
    share_recv,
    attn_send,
    attn_recv,
    part_send,
    part_recv,
):
    blk, head = lax.axis_index("blk"), lax.axis_index("head")
    place = lax.rem(blk, 4)
    base = blk - place
    other = 1 - head
    following = lax.rem(blk + 4, count)
    previous = lax.rem(blk + count - 4, count)
    swapped = lax.rem(place, 2) * 2 + place // 2

    barrier = pltpu.get_barrier_semaphore()
    for p in range(4):
        near = previous if p >= 2 else following
        pl.semaphore_signal(
            barrier, inc=1, device_id={"blk": near - place + p, "head": other}
        )
        pl.semaphore_signal(barrier, inc=1, device_id={"blk": base + p, "head": other})

    loads = [
        pltpu.make_async_copy(w, weights.at[side], weight_sem.at[side])
        for side, w in enumerate((w_a, w_b))
    ]
    for side, pair in enumerate(((ref_a, val_a), (ref_b, val_b))):
        for p in range(4):
            for t in range(2):
                pltpu.make_async_copy(
                    pair[t].at[:, pl.ds(p * PAIR, PAIR)], staged.at[side, p, t], stage_sem.at[side]
                ).start()
    for load in loads:
        load.start()

    pl.semaphore_wait(barrier, 8)

    def landed(ref, sem):
        pltpu.make_async_remote_copy(
            src_ref=ref, dst_ref=ref, send_sem=sem, recv_sem=sem, device_id={"head": other}
        ).wait_recv()

    def left(ref, sem):
        pltpu.make_async_remote_copy(
            src_ref=ref, dst_ref=ref, send_sem=sem, recv_sem=sem, device_id={"head": other}
        ).wait_send()

    def share(side, p, group, position):
        return pltpu.make_async_remote_copy(
            src_ref=staged.at[side, p],
            dst_ref=held.at[side, position],
            send_sem=share_send.at[side],
            recv_sem=share_recv.at[side, position],
            device_id={"blk": group + p, "head": other},
        )

    def stage_wait(side):
        pltpu.make_async_copy(staged.at[side], staged.at[side], stage_sem.at[side]).wait()

    def own_shares(side):
        for p in range(4):
            share(side, p, base, place + 1 + side).start()

    ends = place // 2
    first_side, second_side = ends, 1 - ends
    group = (1 - ends) * previous + ends * following - place

    def band_shares():
        position = (1 - ends) * (place + 5) + ends * (place - 2)
        for p in range(4):
            share(first_side, p, group, position).start()

    def outer_shares():
        for p in range(4):
            share(second_side, p, group, (1 - ends) * 6).start()

    stage_wait(first_side)

    @pl.when(ends == 1)
    def _():
        band_shares()

    stage_wait(second_side)

    @pl.when(place == 3)
    def _():
        outer_shares()
        left(staged.at[second_side], share_send.at[second_side])

    @pl.when(ends == 1)
    def _():
        left(staged.at[first_side], share_send.at[first_side])

    own_shares(first_side)
    own_shares(second_side)

    @pl.when(ends == 0)
    def _():
        band_shares()

    @pl.when(place == 0)
    def _():
        outer_shares()

    def wait_share(side, first, blocks):
        for position in range(first, first + blocks):
            landed(held.at[side, position], share_recv.at[side, position])

    def turn(side, first, blocks):
        wait_share(side, first, blocks)

        @pl.loop(first, first + blocks)
        def _(position):
            turned[side, position] = held[side, position, 1].T

    def attn_copies(side, n):
        if n in (0, 3):
            pieces = ((n, pl.ds(0, ROWS)),)
        else:
            pieces = (
                (n, pl.ds(pl.multiple_of(other * HALF, HALF), HALF)),
                (3 - n, pl.ds(pl.multiple_of(head * HALF, HALF), HALF)),
            )
        return [
            pltpu.make_async_remote_copy(
                src_ref=attn.at[side, n, rows],
                dst_ref=gathered.at[side, place, rows],
                send_sem=attn_send.at[side],
                recv_sem=attn_recv.at[side],
                device_id={"blk": base + target, "head": other},
            )
            for target, rows in pieces
        ]

    def work(*tasks):
        for side, n in tasks:
            keys = held[1 - side, pl.ds(n, 4), 0].reshape(4 * ROWS, PAIR)
            values = jnp.concatenate([turned[1 - side, n + k] for k in range(4)], axis=1)
            attn[side, n] = attend(held[side, n + 1 + side, 0], keys, values)
        for side, n in tasks:
            for copy in attn_copies(side, n):
                copy.start()

    turn(0, 1, 4)
    turn(1, 2, 4)
    work((0, 2), (1, 1))
    turn(0, 5, 2)
    turn(1, 6, 1)
    work((0, 3), (1, 2), (1, 3))
    turn(1, 0, 2)
    work((0, 1), (0, 0))
    turn(0, 0, 1)
    work((1, 0),)

    mine = pl.ds(pl.multiple_of(head * HALF, HALF), HALF)
    theirs = pl.ds(pl.multiple_of(other * HALF, HALF), HALF)

    def part(side, chunk):
        return pltpu.make_async_remote_copy(
            src_ref=outgoing.at[side, chunk],
            dst_ref=incoming.at[side, chunk],
            send_sem=part_send.at[side],
            recv_sem=part_recv.at[side, chunk],
            device_id={"blk": base + swapped, "head": other},
        )

    for side in range(2):
        loads[side].wait()
        landed(gathered.at[side], attn_recv.at[side])
        rows = jnp.concatenate(
            [
                jnp.concatenate([gathered[side, p, half] for p in range(4)], axis=1)
                for half in (mine, theirs)
            ],
            axis=0,
        )
        for chunk in range(CHUNKS):
            product = jnp.dot(
                rows,
                weights[side, :, chunk * PIECE : (chunk + 1) * PIECE],
                preferred_element_type=F32,
            )
            outgoing[side, chunk] = product[HALF:].astype(BF16)
            part(side, chunk).start()
            own[side, chunk] = product[:HALF]

    @pl.when(ends == 0)
    def _():
        left(staged.at[first_side], share_send.at[first_side])

    @pl.when(place == 0)
    def _():
        left(staged.at[second_side], share_send.at[second_side])

    for side in range(2):
        left(staged.at[side], share_send.at[side])
        left(attn.at[side], attn_send.at[side])
        left(outgoing.at[side], part_send.at[side])

    for side, out in enumerate((out_a, out_b)):
        for chunk in range(CHUNKS):
            part(side, chunk).wait_recv()
            out[:, chunk * PIECE : (chunk + 1) * PIECE] = (
                own[side, chunk] + incoming[side, chunk].astype(F32)
            ).astype(BF16)


def solution(mesh):
    count = mesh.shape["blk"]

    def shards(ref_a, val_a, ref_b, val_b, w_out_a, w_out_b):
        hbm = pl.BlockSpec(memory_space=pltpu.HBM)
        vmem = pl.BlockSpec(memory_space=pltpu.VMEM)
        out = pltpu.VMEM((HALF, WIDTH), BF16)
        return pl.pallas_call(
            functools.partial(kernel, count),
            out_shape=(out, out),
            in_specs=[hbm] * 6,
            out_specs=(vmem, vmem),
            scratch_shapes=[
                pltpu.VMEM((2, 4, 2, ROWS, PAIR), BF16),
                pltpu.VMEM((2, 7, 2, ROWS, PAIR), BF16),
                pltpu.VMEM((2, 7, PAIR, ROWS), BF16),
                pltpu.VMEM((2, WIDTH // 2, WIDTH), BF16),
                pltpu.VMEM((2, 4, ROWS, PAIR), BF16),
                pltpu.VMEM((2, 4, ROWS, PAIR), BF16),
                pltpu.VMEM((2, CHUNKS, HALF, PIECE), BF16),
                pltpu.VMEM((2, CHUNKS, HALF, PIECE), BF16),
                pltpu.VMEM((2, CHUNKS, HALF, PIECE), F32),
                pltpu.SemaphoreType.DMA((2,)),
                pltpu.SemaphoreType.DMA((2,)),
                pltpu.SemaphoreType.DMA((2,)),
                pltpu.SemaphoreType.DMA((2, 7)),
                pltpu.SemaphoreType.DMA((2,)),
                pltpu.SemaphoreType.DMA((2,)),
                pltpu.SemaphoreType.DMA((2,)),
                pltpu.SemaphoreType.DMA((2, CHUNKS)),
            ],
            compiler_params=pltpu.CompilerParams(
                collective_id=0, has_side_effects=True, vmem_limit_bytes=32 * 1024 * 1024
            ),
        )(
            *(
                pltpu.with_memory_space_constraint(array, pltpu.HBM)
                for array in (ref_a, val_a, ref_b, val_b, w_out_a, w_out_b)
            )
        )

    return jax.shard_map(
        shards,
        mesh=mesh,
        in_specs=(
            P("blk", "head"),
            P("blk", "head"),
            P("blk", "head"),
            P("blk", "head"),
            P("head", None),
            P("head", None),
        ),
        out_specs=(P(("blk", "head"), None), P(("blk", "head"), None)),
        check_vma=False,
    )
```

```python
import functools
import math

import jax
import jax.numpy as jnp
from jax import lax
from jax.experimental import pallas as pl
from jax.experimental.pallas import tpu as pltpu
from jax.sharding import PartitionSpec as P


ROWS = 128
HALF = 64
PAIR = 128
WIDTH = 1024
CHUNKS = 2
PIECE = WIDTH // CHUNKS
SCORE = 0.125 * math.log2(math.e)
BF16 = jnp.bfloat16
F32 = jnp.float32


def attend(query, keys, values):
    lane = lax.broadcasted_iota(jnp.int32, (ROWS, PAIR), 1)
    query = query.astype(F32)
    zero = jnp.zeros_like(query)
    both = jnp.concatenate(
        [jnp.where(lane < HALF, query, zero), jnp.where(lane < HALF, zero, query)], axis=0
    ).astype(BF16)
    parts = []
    for key, value in zip(keys, values):
        scores = lax.dot_general(key, both, (((1,), (1,)), ((), ())), preferred_element_type=F32)
        top = jnp.max(scores, axis=0, keepdims=True)
        expo = jnp.exp2((scores - top) * SCORE)
        accum = jnp.dot(value, expo.astype(BF16), preferred_element_type=F32)
        parts.append((top, jnp.sum(expo, axis=0, keepdims=True), accum[:HALF, :ROWS], accum[HALF:, ROWS:]))
    top = functools.reduce(jnp.maximum, [part[0] for part in parts])
    scales = [jnp.exp2((part[0] - top) * SCORE) for part in parts]
    total = sum(scale * part[1] for scale, part in zip(scales, parts))
    first = sum(scale[:, :ROWS] * part[2] for scale, part in zip(scales, parts))
    second = sum(scale[:, ROWS:] * part[3] for scale, part in zip(scales, parts))
    result = jnp.concatenate([first / total[:, :ROWS], second / total[:, ROWS:]], axis=0)
    return result.T.astype(BF16)


def kernel(
    count,
    ref_a,
    val_a,
    ref_b,
    val_b,
    w_a,
    w_b,
    out_a,
    out_b,
    staged,
    held,
    turned,
    weights,
    attn,
    gathered,
    outgoing,
    incoming,
    own,
    weight_sem,
    stage_sem,
    share_send,
    share_recv,
    band_send,
    band_recv,
    attn_send,
    attn_recv,
    part_send,
    part_recv,
):
    blk, head = lax.axis_index("blk"), lax.axis_index("head")
    place = lax.rem(blk, 4)
    base = blk - place
    other = 1 - head
    following = lax.rem(blk + 4, count)
    previous = lax.rem(blk + count - 4, count)
    swapped = lax.rem(place, 2) * 2 + place // 2

    barrier = pltpu.get_barrier_semaphore()
    for p in range(4):
        pl.semaphore_signal(barrier, inc=1, device_id={"blk": base + p, "head": other})
    pl.semaphore_signal(barrier, inc=1, device_id={"blk": following})
    pl.semaphore_signal(barrier, inc=1, device_id={"blk": previous})

    loads = [
        pltpu.make_async_copy(w, weights.at[side], weight_sem.at[side])
        for side, w in enumerate((w_a, w_b))
    ]
    for side, pair in enumerate(((ref_a, val_a), (ref_b, val_b))):
        for p in range(4):
            for t in range(2):
                pltpu.make_async_copy(
                    pair[t].at[:, pl.ds(p * PAIR, PAIR)], staged.at[side, p, t], stage_sem.at[side]
                ).start()
    for load in loads:
        load.start()

    pl.semaphore_wait(barrier, 6)

    def landed(ref, sem):
        pltpu.make_async_remote_copy(
            src_ref=ref, dst_ref=ref, send_sem=sem, recv_sem=sem, device_id={"head": other}
        ).wait_recv()

    def left(ref, sem):
        pltpu.make_async_remote_copy(
            src_ref=ref, dst_ref=ref, send_sem=sem, recv_sem=sem, device_id={"head": other}
        ).wait_send()

    def share(side, p):
        return pltpu.make_async_remote_copy(
            src_ref=staged.at[side, p],
            dst_ref=held.at[side, place + 1 + side],
            send_sem=share_send.at[side],
            recv_sem=share_recv.at[side, place],
            device_id={"blk": base + p, "head": other},
        )

    ahead = place // 2
    pltpu.make_async_copy(staged.at[ahead], staged.at[ahead], stage_sem.at[ahead]).wait()
    for p in range(4):
        share(ahead, p).start()
    behind = 1 - ahead
    pltpu.make_async_copy(staged.at[behind], staged.at[behind], stage_sem.at[behind]).wait()
    left(staged.at[ahead], share_send.at[ahead])
    for p in range(4):
        share(behind, p).start()

    def wait_share(side, blocks):
        for block in blocks:
            landed(held.at[side, block + 1 + side], share_recv.at[side, block])

    bands = ((1, 4, 0, 2, True), (0, 1, 5, 2, False), (0, 4, 0, 1, True), (1, 2, 6, 1, False))

    def band(index):
        side, first, target, blocks, forward = bands[index]
        return pltpu.make_async_remote_copy(
            src_ref=held.at[side, pl.ds(first, blocks)],
            dst_ref=held.at[side, pl.ds(target, blocks)],
            send_sem=band_send,
            recv_sem=band_recv.at[index],
            device_id={"blk": following if forward else previous},
        )

    def turn(side, first, blocks):
        for position in range(first, first + blocks):
            turned[side, position] = held[side, position, 1].T

    def attn_copies(side, n):
        if n in (0, 3):
            pieces = ((n, pl.ds(0, ROWS)),)
        else:
            pieces = (
                (n, pl.ds(pl.multiple_of(other * HALF, HALF), HALF)),
                (3 - n, pl.ds(pl.multiple_of(head * HALF, HALF), HALF)),
            )
        return [
            pltpu.make_async_remote_copy(
                src_ref=attn.at[side, n, rows],
                dst_ref=gathered.at[side, place, rows],
                send_sem=attn_send.at[side],
                recv_sem=attn_recv.at[side],
                device_id={"blk": base + target, "head": other},
            )
            for target, rows in pieces
        ]

    def work(*tasks):
        for side, n in tasks:
            keys = [held[1 - side, n + k, 0] for k in range(4)]
            values = [turned[1 - side, n + k] for k in range(4)]
            attn[side, n] = attend(held[side, n + 1 + side, 0], keys, values)
        for side, n in tasks:
            for copy in attn_copies(side, n):
                copy.start()

    for index, (side, first, _, blocks, _) in enumerate(bands):
        wait_share(side, range(first - 1 - side, first - 1 - side + blocks))
        band(index).start()
    wait_share(0, (2,))
    wait_share(1, (1,))
    turn(0, 1, 4)
    turn(1, 2, 4)
    work((0, 2), (1, 1))
    band(1).wait_recv()
    band(3).wait_recv()
    turn(0, 5, 2)
    turn(1, 6, 1)
    work((0, 3), (1, 2), (1, 3))
    band(0).wait_recv()
    turn(1, 0, 2)
    work((0, 1), (0, 0))
    band(2).wait_recv()
    turn(0, 0, 1)
    work((1, 0),)

    mine = pl.ds(pl.multiple_of(head * HALF, HALF), HALF)
    theirs = pl.ds(pl.multiple_of(other * HALF, HALF), HALF)

    def part(side, chunk):
        return pltpu.make_async_remote_copy(
            src_ref=outgoing.at[side, chunk],
            dst_ref=incoming.at[side, chunk],
            send_sem=part_send.at[side],
            recv_sem=part_recv.at[side, chunk],
            device_id={"blk": base + swapped, "head": other},
        )

    for side in range(2):
        loads[side].wait()
        landed(gathered.at[side], attn_recv.at[side])
        rows = jnp.concatenate(
            [
                jnp.concatenate([gathered[side, p, half] for p in range(4)], axis=1)
                for half in (mine, theirs)
            ],
            axis=0,
        )
        for chunk in range(CHUNKS):
            product = jnp.dot(
                rows,
                weights[side, :, chunk * PIECE : (chunk + 1) * PIECE],
                preferred_element_type=F32,
            )
            outgoing[side, chunk] = product[HALF:].astype(BF16)
            part(side, chunk).start()
            own[side, chunk] = product[:HALF]

    left(staged.at[behind], share_send.at[behind])
    left(held.at[0, pl.ds(0, 6)], band_send)
    for side in range(2):
        left(attn.at[side], attn_send.at[side])
        left(outgoing.at[side], part_send.at[side])

    for side, out in enumerate((out_a, out_b)):
        for chunk in range(CHUNKS):
            part(side, chunk).wait_recv()
            out[:, chunk * PIECE : (chunk + 1) * PIECE] = (
                own[side, chunk] + incoming[side, chunk].astype(F32)
            ).astype(BF16)


def solution(mesh):
    count = mesh.shape["blk"]

    def shards(ref_a, val_a, ref_b, val_b, w_out_a, w_out_b):
        hbm = pl.BlockSpec(memory_space=pltpu.HBM)
        vmem = pl.BlockSpec(memory_space=pltpu.VMEM)
        out = pltpu.VMEM((HALF, WIDTH), BF16)
        return pl.pallas_call(
            functools.partial(kernel, count),
            out_shape=(out, out),
            in_specs=[hbm] * 6,
            out_specs=(vmem, vmem),
            scratch_shapes=[
                pltpu.VMEM((2, 4, 2, ROWS, PAIR), BF16),
                pltpu.VMEM((2, 7, 2, ROWS, PAIR), BF16),
                pltpu.VMEM((2, 7, PAIR, ROWS), BF16),
                pltpu.VMEM((2, WIDTH // 2, WIDTH), BF16),
                pltpu.VMEM((2, 4, ROWS, PAIR), BF16),
                pltpu.VMEM((2, 4, ROWS, PAIR), BF16),
                pltpu.VMEM((2, CHUNKS, HALF, PIECE), BF16),
                pltpu.VMEM((2, CHUNKS, HALF, PIECE), BF16),
                pltpu.VMEM((2, CHUNKS, HALF, PIECE), F32),
                pltpu.SemaphoreType.DMA((2,)),
                pltpu.SemaphoreType.DMA((2,)),
                pltpu.SemaphoreType.DMA((2,)),
                pltpu.SemaphoreType.DMA((2, 4)),
                pltpu.SemaphoreType.DMA,
                pltpu.SemaphoreType.DMA((4,)),
                pltpu.SemaphoreType.DMA((2,)),
                pltpu.SemaphoreType.DMA((2,)),
                pltpu.SemaphoreType.DMA((2,)),
                pltpu.SemaphoreType.DMA((2, CHUNKS)),
            ],
            compiler_params=pltpu.CompilerParams(
                collective_id=0, has_side_effects=True, vmem_limit_bytes=32 * 1024 * 1024
            ),
        )(
            *(
                pltpu.with_memory_space_constraint(array, pltpu.HBM)
                for array in (ref_a, val_a, ref_b, val_b, w_out_a, w_out_b)
            )
        )

    return jax.shard_map(
        shards,
        mesh=mesh,
        in_specs=(
            P("blk", "head"),
            P("blk", "head"),
            P("blk", "head"),
            P("blk", "head"),
            P("head", None),
            P("head", None),
        ),
        out_specs=(P(("blk", "head"), None), P(("blk", "head"), None)),
        check_vma=False,
    )
```

```python
import functools
import math

import jax
import jax.numpy as jnp
from jax import lax
from jax.experimental import pallas as pl
from jax.experimental.pallas import tpu as pltpu
from jax.sharding import PartitionSpec as P


ROWS = 128
HALF = 64
PAIR = 128
WIDTH = 1024
CHUNKS = 2
PIECE = WIDTH // CHUNKS
SCORE = 0.125 * math.log2(math.e)
BF16 = jnp.bfloat16
F32 = jnp.float32


def split_heads(query):
    lane = lax.broadcasted_iota(jnp.int32, (ROWS, PAIR), 1)
    query = query.astype(F32)
    zero = jnp.zeros_like(query)
    return jnp.concatenate(
        [jnp.where(lane < HALF, query, zero), jnp.where(lane < HALF, zero, query)], axis=0
    ).astype(BF16)


def pair_part(both, key, value):
    scores = lax.dot_general(key, both, (((1,), (1,)), ((), ())), preferred_element_type=F32)
    top = jnp.max(scores, axis=0, keepdims=True)
    expo = jnp.exp2((scores - top) * SCORE)
    accum = jnp.dot(value, expo.astype(BF16), preferred_element_type=F32)
    return top, jnp.sum(expo, axis=0, keepdims=True), accum[:HALF, :ROWS], accum[HALF:, ROWS:]


def merge_parts(parts):
    top = functools.reduce(jnp.maximum, [part[0] for part in parts])
    scales = [jnp.exp2((part[0] - top) * SCORE) for part in parts]
    return (
        top,
        sum(scale * part[1] for scale, part in zip(scales, parts)),
        sum(scale[:, :ROWS] * part[2] for scale, part in zip(scales, parts)),
        sum(scale[:, ROWS:] * part[3] for scale, part in zip(scales, parts)),
    )


def finish(part):
    _, total, first, second = part
    result = jnp.concatenate([first / total[:, :ROWS], second / total[:, ROWS:]], axis=0)
    return result.T.astype(BF16)


def kernel(
    count,
    ref_a,
    val_a,
    ref_b,
    val_b,
    w_a,
    w_b,
    out,
    staged,
    held,
    turned,
    weights,
    stats,
    sums,
    attn,
    gathered,
    outgoing,
    incoming,
    own,
    weight_sem,
    stage_sem,
    share_send,
    share_recv,
    band_send,
    band_recv,
    attn_send,
    attn_recv,
    part_send,
    part_recv,
):
    blk, head = lax.axis_index("blk"), lax.axis_index("head")
    place = lax.rem(blk, 4)
    base = blk - place
    other = 1 - head
    following = lax.rem(blk + 4, count)
    previous = lax.rem(blk + count - 4, count)
    swapped = lax.rem(place, 2) * 2 + place // 2

    barrier = pltpu.get_barrier_semaphore()
    for p in range(4):
        pl.semaphore_signal(barrier, inc=1, device_id={"blk": base + p, "head": other})
    pl.semaphore_signal(barrier, inc=1, device_id={"blk": following})
    pl.semaphore_signal(barrier, inc=1, device_id={"blk": previous})

    loads = [
        pltpu.make_async_copy(w, weights.at[side], weight_sem.at[side])
        for side, w in enumerate((w_a, w_b))
    ]
    for side, pair in enumerate(((ref_a, val_a), (ref_b, val_b))):
        for p in range(4):
            for t in range(2):
                pltpu.make_async_copy(
                    pair[t].at[:, pl.ds(p * PAIR, PAIR)], staged.at[side, p, t], stage_sem.at[side]
                ).start()
    for load in loads:
        load.start()

    pl.semaphore_wait(barrier, 6)

    def landed(ref, sem):
        pltpu.make_async_remote_copy(
            src_ref=ref, dst_ref=ref, send_sem=sem, recv_sem=sem, device_id={"head": other}
        ).wait_recv()

    def left(ref, sem):
        pltpu.make_async_remote_copy(
            src_ref=ref, dst_ref=ref, send_sem=sem, recv_sem=sem, device_id={"head": other}
        ).wait_send()

    def share(side, p):
        return pltpu.make_async_remote_copy(
            src_ref=staged.at[side, p],
            dst_ref=held.at[side, place + 1 + side],
            send_sem=share_send.at[side],
            recv_sem=share_recv.at[side, place],
            device_id={"blk": base + p, "head": other},
        )

    ahead = place // 2
    pltpu.make_async_copy(staged.at[ahead], staged.at[ahead], stage_sem.at[ahead]).wait()
    for p in range(4):
        share(ahead, p).start()
    behind = 1 - ahead
    pltpu.make_async_copy(staged.at[behind], staged.at[behind], stage_sem.at[behind]).wait()

    @pl.when((place == 1) | (place == 2))
    def _():
        left(staged.at[ahead], share_send.at[ahead])

    for p in range(4):
        share(behind, p).start()

    def wait_share(side, blocks):
        for block in blocks:
            landed(held.at[side, block + 1 + side], share_recv.at[side, block])

    bands = ((1, 4, 0, 2, True), (0, 1, 5, 2, False), (0, 4, 0, 1, True), (1, 2, 6, 1, False))

    def band(index):
        side, first, target, blocks, forward = bands[index]
        return pltpu.make_async_remote_copy(
            src_ref=held.at[side, pl.ds(first, blocks)],
            dst_ref=held.at[side, pl.ds(target, blocks)],
            send_sem=band_send,
            recv_sem=band_recv.at[index],
            device_id={"blk": following if forward else previous},
        )

    def turn(side, first, blocks):
        for position in range(first, first + blocks):
            turned[side, position] = held[side, position, 1].T

    def attn_copies(side, n):
        if n in (0, 3):
            pieces = ((n, pl.ds(0, ROWS)),)
        else:
            pieces = (
                (n, pl.ds(pl.multiple_of(other * HALF, HALF), HALF)),
                (3 - n, pl.ds(pl.multiple_of(head * HALF, HALF), HALF)),
            )
        return [
            pltpu.make_async_remote_copy(
                src_ref=attn.at[side, n, rows],
                dst_ref=gathered.at[side, place, rows],
                send_sem=attn_send.at[side],
                recv_sem=attn_recv.at[side],
                device_id={"blk": base + target, "head": other},
            )
            for target, rows in pieces
        ]

    def pairs(side, n, positions):
        both = split_heads(held[side, n + 1 + side, 0])
        return [
            pair_part(both, held[1 - side, position, 0], turned[1 - side, position])
            for position in positions
        ]

    def ready(side, n, part):
        attn[side, n] = finish(part)

    def begin(side, n, positions):
        part = merge_parts(pairs(side, n, positions))
        if len(positions) == 4:
            ready(side, n, part)
        else:
            stats[side, n, 0:1], stats[side, n, 1:2] = part[0], part[1]
            sums[side, n, :HALF], sums[side, n, HALF:] = part[2], part[3]

    def complete(side, n, positions):
        state = (
            stats[side, n, 0:1],
            stats[side, n, 1:2],
            sums[side, n, :HALF],
            sums[side, n, HALF:],
        )
        ready(side, n, merge_parts([state] + pairs(side, n, positions)))

    def give(*tasks):
        for side, n in tasks:
            for copy in attn_copies(side, n):
                copy.start()

    for index, (side, first, _, blocks, _) in enumerate(bands):
        wait_share(side, range(first - 1 - side, first - 1 - side + blocks))
        band(index).start()
    wait_share(0, (2,))
    wait_share(1, (1,))
    turn(0, 1, 4)
    turn(1, 2, 4)
    begin(0, 2, (2, 3, 4, 5))
    begin(1, 1, (1, 2, 3, 4))
    give((0, 2), (1, 1))
    begin(0, 3, (3, 4, 5))
    begin(1, 2, (2, 3, 4))
    begin(1, 3, (3, 4))
    begin(0, 1, (2, 3, 4))
    begin(0, 0, (2, 3))
    begin(1, 0, (1, 2, 3))
    band(1).wait_recv()
    band(3).wait_recv()
    turn(0, 5, 2)
    turn(1, 6, 1)
    complete(0, 3, (6,))
    complete(1, 2, (5,))
    complete(1, 3, (5, 6))
    give((0, 3), (1, 2), (1, 3))
    band(0).wait_recv()
    turn(1, 0, 2)
    complete(0, 1, (1,))
    complete(0, 0, (0, 1))
    give((0, 1), (0, 0))
    band(2).wait_recv()
    turn(0, 0, 1)
    complete(1, 0, (0,))
    give((1, 0),)

    mine = pl.ds(pl.multiple_of(head * HALF, HALF), HALF)
    theirs = pl.ds(pl.multiple_of(other * HALF, HALF), HALF)

    def part(side, chunk):
        return pltpu.make_async_remote_copy(
            src_ref=outgoing.at[side, chunk],
            dst_ref=incoming.at[side, chunk],
            send_sem=part_send.at[side],
            recv_sem=part_recv.at[side, chunk],
            device_id={"blk": base + swapped, "head": other},
        )

    for side in range(2):
        loads[side].wait()
        landed(gathered.at[side], attn_recv.at[side])
        rows = jnp.concatenate(
            [
                jnp.concatenate([gathered[side, p, half] for p in range(4)], axis=1)
                for half in (mine, theirs)
            ],
            axis=0,
        )
        for chunk in range(CHUNKS):
            product = jnp.dot(
                rows,
                weights[side, :, chunk * PIECE : (chunk + 1) * PIECE],
                preferred_element_type=F32,
            )
            outgoing[side, chunk] = product[HALF:].astype(BF16)
            part(side, chunk).start()
            own[side, chunk] = product[:HALF]

    @pl.when((place == 0) | (place == 3))
    def _():
        left(staged.at[ahead], share_send.at[ahead])

    left(staged.at[behind], share_send.at[behind])
    left(held.at[0, pl.ds(0, 6)], band_send)
    for side in range(2):
        left(attn.at[side], attn_send.at[side])
        left(outgoing.at[side], part_send.at[side])

    for side in range(2):
        for chunk in range(CHUNKS):
            part(side, chunk).wait_recv()
            out[side, :, chunk * PIECE : (chunk + 1) * PIECE] = (
                own[side, chunk] + incoming[side, chunk].astype(F32)
            ).astype(BF16)


def solution(mesh):
    count = mesh.shape["blk"]

    def shards(ref_a, val_a, ref_b, val_b, w_out_a, w_out_b):
        hbm = pl.BlockSpec(memory_space=pltpu.HBM)
        vmem = pl.BlockSpec(memory_space=pltpu.VMEM)
        out = pltpu.VMEM((2, HALF, WIDTH), BF16)
        results = pl.pallas_call(
            functools.partial(kernel, count),
            out_shape=out,
            in_specs=[hbm] * 6,
            out_specs=vmem,
            scratch_shapes=[
                pltpu.VMEM((2, 4, 2, ROWS, PAIR), BF16),
                pltpu.VMEM((2, 7, 2, ROWS, PAIR), BF16),
                pltpu.VMEM((2, 7, PAIR, ROWS), BF16),
                pltpu.VMEM((2, WIDTH // 2, WIDTH), BF16),
                pltpu.VMEM((2, 4, 8, 2 * ROWS), F32),
                pltpu.VMEM((2, 4, PAIR, ROWS), F32),
                pltpu.VMEM((2, 4, ROWS, PAIR), BF16),
                pltpu.VMEM((2, 4, ROWS, PAIR), BF16),
                pltpu.VMEM((2, CHUNKS, HALF, PIECE), BF16),
                pltpu.VMEM((2, CHUNKS, HALF, PIECE), BF16),
                pltpu.VMEM((2, CHUNKS, HALF, PIECE), F32),
                pltpu.SemaphoreType.DMA((2,)),
                pltpu.SemaphoreType.DMA((2,)),
                pltpu.SemaphoreType.DMA((2,)),
                pltpu.SemaphoreType.DMA((2, 4)),
                pltpu.SemaphoreType.DMA,
                pltpu.SemaphoreType.DMA((4,)),
                pltpu.SemaphoreType.DMA((2,)),
                pltpu.SemaphoreType.DMA((2,)),
                pltpu.SemaphoreType.DMA((2,)),
                pltpu.SemaphoreType.DMA((2, CHUNKS)),
            ],
            compiler_params=pltpu.CompilerParams(
                collective_id=0, has_side_effects=True, vmem_limit_bytes=32 * 1024 * 1024
            ),
        )(
            *(
                pltpu.with_memory_space_constraint(array, pltpu.HBM)
                for array in (ref_a, val_a, ref_b, val_b, w_out_a, w_out_b)
            )
        )
        return results[0], results[1]

    return jax.shard_map(
        shards,
        mesh=mesh,
        in_specs=(
            P("blk", "head"),
            P("blk", "head"),
            P("blk", "head"),
            P("blk", "head"),
            P("head", None),
            P("head", None),
        ),
        out_specs=(P(("blk", "head"), None), P(("blk", "head"), None)),
        check_vma=False,
    )
```

```python
import functools
import math

import jax
import jax.numpy as jnp
from jax import lax
from jax.experimental import pallas as pl
from jax.experimental.pallas import tpu as pltpu
from jax.sharding import PartitionSpec as P


ROWS = 128
HALF = 64
PAIR = 128
WIDTH = 1024
CHUNKS = 2
PIECE = WIDTH // CHUNKS
SCORE = 0.125 * math.log2(math.e)
BF16 = jnp.bfloat16
F32 = jnp.float32


def split_heads(query):
    lane = lax.broadcasted_iota(jnp.int32, (ROWS, PAIR), 1)
    query = query.astype(F32)
    zero = jnp.zeros_like(query)
    return jnp.concatenate(
        [jnp.where(lane < HALF, query, zero), jnp.where(lane < HALF, zero, query)], axis=0
    ).astype(BF16)


def pair_part(both, key, value):
    scores = lax.dot_general(key, both, (((1,), (1,)), ((), ())), preferred_element_type=F32)
    top = jnp.max(scores, axis=0, keepdims=True)
    expo = jnp.exp2((scores - top) * SCORE)
    accum = jnp.dot(value, expo.astype(BF16), preferred_element_type=F32)
    return top, jnp.sum(expo, axis=0, keepdims=True), accum[:HALF, :ROWS], accum[HALF:, ROWS:]


def merge_parts(parts):
    top = functools.reduce(jnp.maximum, [part[0] for part in parts])
    scales = [jnp.exp2((part[0] - top) * SCORE) for part in parts]
    return (
        top,
        sum(scale * part[1] for scale, part in zip(scales, parts)),
        sum(scale[:, :ROWS] * part[2] for scale, part in zip(scales, parts)),
        sum(scale[:, ROWS:] * part[3] for scale, part in zip(scales, parts)),
    )


def finish(part):
    _, total, first, second = part
    result = jnp.concatenate([first / total[:, :ROWS], second / total[:, ROWS:]], axis=0)
    return result.T.astype(BF16)


def kernel(
    count,
    ref_a,
    val_a,
    ref_b,
    val_b,
    w_a,
    w_b,
    out,
    staged,
    held,
    turned,
    weights,
    stats,
    sums,
    attn,
    gathered,
    outgoing,
    incoming,
    own,
    weight_sem,
    stage_sem,
    share_send,
    share_recv,
    band_send,
    band_recv,
    attn_send,
    attn_recv,
    part_send,
    part_recv,
):
    blk, head = lax.axis_index("blk"), lax.axis_index("head")
    place = lax.rem(blk, 4)
    base = blk - place
    other = 1 - head
    following = lax.rem(blk + 4, count)
    previous = lax.rem(blk + count - 4, count)
    swapped = lax.rem(place, 2) * 2 + place // 2

    barrier = pltpu.get_barrier_semaphore()
    for p in range(4):
        pl.semaphore_signal(barrier, inc=1, device_id={"blk": base + p, "head": other})
    pl.semaphore_signal(barrier, inc=1, device_id={"blk": following})
    pl.semaphore_signal(barrier, inc=1, device_id={"blk": previous})

    loads = [
        pltpu.make_async_copy(w, weights.at[side], weight_sem.at[side])
        for side, w in enumerate((w_a, w_b))
    ]
    for side, pair in enumerate(((ref_a, val_a), (ref_b, val_b))):
        for p in range(4):
            for t in range(2):
                pltpu.make_async_copy(
                    pair[t].at[:, pl.ds(p * PAIR, PAIR)], staged.at[side, p, t], stage_sem.at[side]
                ).start()
    for load in loads:
        load.start()

    pl.semaphore_wait(barrier, 6)

    def landed(ref, sem):
        pltpu.make_async_remote_copy(
            src_ref=ref, dst_ref=ref, send_sem=sem, recv_sem=sem, device_id={"head": other}
        ).wait_recv()

    def left(ref, sem):
        pltpu.make_async_remote_copy(
            src_ref=ref, dst_ref=ref, send_sem=sem, recv_sem=sem, device_id={"head": other}
        ).wait_send()

    def share(side, p):
        return pltpu.make_async_remote_copy(
            src_ref=staged.at[side, p],
            dst_ref=held.at[side, place + 1 + side],
            send_sem=share_send.at[side],
            recv_sem=share_recv.at[side, place],
            device_id={"blk": base + p, "head": other},
        )

    ahead = place // 2
    pltpu.make_async_copy(staged.at[ahead], staged.at[ahead], stage_sem.at[ahead]).wait()
    for p in range(4):
        share(ahead, p).start()
    behind = 1 - ahead
    pltpu.make_async_copy(staged.at[behind], staged.at[behind], stage_sem.at[behind]).wait()
    left(staged.at[ahead], share_send.at[ahead])
    for p in range(4):
        share(behind, p).start()

    def wait_share(side, blocks):
        for block in blocks:
            landed(held.at[side, block + 1 + side], share_recv.at[side, block])

    bands = ((1, 4, 0, 2, True), (0, 1, 5, 2, False), (0, 4, 0, 1, True), (1, 2, 6, 1, False))

    def band(index):
        side, first, target, blocks, forward = bands[index]
        return pltpu.make_async_remote_copy(
            src_ref=held.at[side, pl.ds(first, blocks)],
            dst_ref=held.at[side, pl.ds(target, blocks)],
            send_sem=band_send,
            recv_sem=band_recv.at[index],
            device_id={"blk": following if forward else previous},
        )

    def turn(side, first, blocks):
        for position in range(first, first + blocks):
            turned[side, position] = held[side, position, 1].T

    def attn_copies(side, n):
        if n in (0, 3):
            pieces = ((n, pl.ds(0, ROWS)),)
        else:
            pieces = (
                (n, pl.ds(pl.multiple_of(other * HALF, HALF), HALF)),
                (3 - n, pl.ds(pl.multiple_of(head * HALF, HALF), HALF)),
            )
        return [
            pltpu.make_async_remote_copy(
                src_ref=attn.at[side, n, rows],
                dst_ref=gathered.at[side, place, rows],
                send_sem=attn_send.at[side],
                recv_sem=attn_recv.at[side],
                device_id={"blk": base + target, "head": other},
            )
            for target, rows in pieces
        ]

    def pairs(side, n, positions):
        both = split_heads(held[side, n + 1 + side, 0])
        return [
            pair_part(both, held[1 - side, position, 0], turned[1 - side, position])
            for position in positions
        ]

    def ready(side, n, part):
        attn[side, n] = finish(part)

    def begin(side, n, positions):
        part = merge_parts(pairs(side, n, positions))
        if len(positions) == 4:
            ready(side, n, part)
        else:
            stats[side, n, 0:1], stats[side, n, 1:2] = part[0], part[1]
            sums[side, n, :HALF], sums[side, n, HALF:] = part[2], part[3]

    def complete(side, n, positions):
        state = (
            stats[side, n, 0:1],
            stats[side, n, 1:2],
            sums[side, n, :HALF],
            sums[side, n, HALF:],
        )
        ready(side, n, merge_parts([state] + pairs(side, n, positions)))

    def give(*tasks):
        for side, n in tasks:
            for copy in attn_copies(side, n):
                copy.start()

    for index, (side, first, _, blocks, _) in enumerate(bands):
        wait_share(side, range(first - 1 - side, first - 1 - side + blocks))
        band(index).start()
    wait_share(0, (2,))
    wait_share(1, (1,))
    turn(0, 1, 4)
    turn(1, 2, 4)
    begin(0, 2, (2, 3, 4, 5))
    begin(1, 1, (1, 2, 3, 4))
    give((0, 2), (1, 1))
    begin(0, 3, (3, 4, 5))
    begin(1, 2, (2, 3, 4))
    begin(1, 3, (3, 4))
    begin(0, 1, (2, 3, 4))
    begin(0, 0, (2, 3))
    begin(1, 0, (1, 2, 3))
    band(1).wait_recv()
    band(3).wait_recv()
    turn(0, 5, 2)
    turn(1, 6, 1)
    complete(0, 3, (6,))
    complete(1, 2, (5,))
    complete(1, 3, (5, 6))
    give((0, 3), (1, 2), (1, 3))
    band(0).wait_recv()
    turn(1, 0, 2)
    complete(0, 1, (1,))
    complete(0, 0, (0, 1))
    give((0, 1), (0, 0))
    band(2).wait_recv()
    turn(0, 0, 1)
    complete(1, 0, (0,))
    give((1, 0),)

    mine = pl.ds(pl.multiple_of(head * HALF, HALF), HALF)
    theirs = pl.ds(pl.multiple_of(other * HALF, HALF), HALF)

    def part(side, chunk):
        return pltpu.make_async_remote_copy(
            src_ref=outgoing.at[side, chunk],
            dst_ref=incoming.at[side, chunk],
            send_sem=part_send.at[side],
            recv_sem=part_recv.at[side, chunk],
            device_id={"blk": base + swapped, "head": other},
        )

    for side in range(2):
        loads[side].wait()
        landed(gathered.at[side], attn_recv.at[side])
        rows = jnp.concatenate(
            [
                jnp.concatenate([gathered[side, p, half] for p in range(4)], axis=1)
                for half in (mine, theirs)
            ],
            axis=0,
        )
        for chunk in range(CHUNKS):
            product = jnp.dot(
                rows,
                weights[side, :, chunk * PIECE : (chunk + 1) * PIECE],
                preferred_element_type=F32,
            )
            outgoing[side, chunk] = product[HALF:].astype(BF16)
            part(side, chunk).start()
            own[side, chunk] = product[:HALF]

    left(staged.at[behind], share_send.at[behind])
    left(held.at[0, pl.ds(0, 6)], band_send)
    for side in range(2):
        left(attn.at[side], attn_send.at[side])
        left(outgoing.at[side], part_send.at[side])

    for side in range(2):
        for chunk in range(CHUNKS):
            part(side, chunk).wait_recv()
            out[side, :, chunk * PIECE : (chunk + 1) * PIECE] = (
                own[side, chunk] + incoming[side, chunk].astype(F32)
            ).astype(BF16)


def solution(mesh):
    count = mesh.shape["blk"]

    def shards(ref_a, val_a, ref_b, val_b, w_out_a, w_out_b):
        hbm = pl.BlockSpec(memory_space=pltpu.HBM)
        vmem = pl.BlockSpec(memory_space=pltpu.VMEM)
        out = pltpu.VMEM((2, HALF, WIDTH), BF16)
        results = pl.pallas_call(
            functools.partial(kernel, count),
            out_shape=out,
            in_specs=[hbm] * 6,
            out_specs=vmem,
            scratch_shapes=[
                pltpu.VMEM((2, 4, 2, ROWS, PAIR), BF16),
                pltpu.VMEM((2, 7, 2, ROWS, PAIR), BF16),
                pltpu.VMEM((2, 7, PAIR, ROWS), BF16),
                pltpu.VMEM((2, WIDTH // 2, WIDTH), BF16),
                pltpu.VMEM((2, 4, 8, 2 * ROWS), F32),
                pltpu.VMEM((2, 4, PAIR, ROWS), F32),
                pltpu.VMEM((2, 4, ROWS, PAIR), BF16),
                pltpu.VMEM((2, 4, ROWS, PAIR), BF16),
                pltpu.VMEM((2, CHUNKS, HALF, PIECE), BF16),
                pltpu.VMEM((2, CHUNKS, HALF, PIECE), BF16),
                pltpu.VMEM((2, CHUNKS, HALF, PIECE), F32),
                pltpu.SemaphoreType.DMA((2,)),
                pltpu.SemaphoreType.DMA((2,)),
                pltpu.SemaphoreType.DMA((2,)),
                pltpu.SemaphoreType.DMA((2, 4)),
                pltpu.SemaphoreType.DMA,
                pltpu.SemaphoreType.DMA((4,)),
                pltpu.SemaphoreType.DMA((2,)),
                pltpu.SemaphoreType.DMA((2,)),
                pltpu.SemaphoreType.DMA((2,)),
                pltpu.SemaphoreType.DMA((2, CHUNKS)),
            ],
            compiler_params=pltpu.CompilerParams(
                collective_id=0, has_side_effects=True, vmem_limit_bytes=32 * 1024 * 1024
            ),
        )(
            *(
                pltpu.with_memory_space_constraint(array, pltpu.HBM)
                for array in (ref_a, val_a, ref_b, val_b, w_out_a, w_out_b)
            )
        )
        return results[0], results[1]

    return jax.shard_map(
        shards,
        mesh=mesh,
        in_specs=(
            P("blk", "head"),
            P("blk", "head"),
            P("blk", "head"),
            P("blk", "head"),
            P("head", None),
            P("head", None),
        ),
        out_specs=(P(("blk", "head"), None), P(("blk", "head"), None)),
        check_vma=False,
    )
```

```python
import functools
import math

import jax
import jax.numpy as jnp
from jax import lax
from jax.experimental import pallas as pl
from jax.experimental.pallas import tpu as pltpu
from jax.sharding import PartitionSpec as P


ROWS = 128
HALF = 64
PAIR = 128
WIDTH = 1024
CHUNKS = 2
PIECE = WIDTH // CHUNKS
SCORE = 0.125 * math.log2(math.e)
BF16 = jnp.bfloat16
F32 = jnp.float32


def split_heads(query):
    lane = lax.broadcasted_iota(jnp.int32, (ROWS, PAIR), 1)
    query = query.astype(F32)
    zero = jnp.zeros_like(query)
    return jnp.concatenate(
        [jnp.where(lane < HALF, query, zero), jnp.where(lane < HALF, zero, query)], axis=0
    ).astype(BF16)


def pair_part(both, key, value):
    scores = lax.dot_general(key, both, (((1,), (1,)), ((), ())), preferred_element_type=F32)
    top = jnp.max(scores, axis=0, keepdims=True)
    expo = jnp.exp2((scores - top) * SCORE)
    accum = jnp.dot(value, expo.astype(BF16), preferred_element_type=F32)
    return top, jnp.sum(expo, axis=0, keepdims=True), accum[:HALF, :ROWS], accum[HALF:, ROWS:]


def merge_parts(parts):
    top = functools.reduce(jnp.maximum, [part[0] for part in parts])
    scales = [jnp.exp2((part[0] - top) * SCORE) for part in parts]
    return (
        top,
        sum(scale * part[1] for scale, part in zip(scales, parts)),
        sum(scale[:, :ROWS] * part[2] for scale, part in zip(scales, parts)),
        sum(scale[:, ROWS:] * part[3] for scale, part in zip(scales, parts)),
    )


def finish(part):
    _, total, first, second = part
    result = jnp.concatenate([first / total[:, :ROWS], second / total[:, ROWS:]], axis=0)
    return result.T.astype(BF16)


def kernel(
    count,
    ref_a,
    val_a,
    ref_b,
    val_b,
    w_a,
    w_b,
    out,
    staged,
    held,
    turned,
    weights,
    stats,
    sums,
    attn,
    gathered,
    outgoing,
    incoming,
    own,
    weight_sem,
    stage_sem,
    share_send,
    share_recv,
    band_send,
    band_recv,
    attn_send,
    attn_recv,
    part_send,
    part_recv,
):
    blk, head = lax.axis_index("blk"), lax.axis_index("head")
    place = lax.rem(blk, 4)
    base = blk - place
    other = 1 - head
    following = lax.rem(blk + 4, count)
    previous = lax.rem(blk + count - 4, count)
    swapped = lax.rem(place, 2) * 2 + place // 2

    barrier = pltpu.get_barrier_semaphore()
    for p in range(4):
        pl.semaphore_signal(barrier, inc=1, device_id={"blk": base + p, "head": other})
    pl.semaphore_signal(barrier, inc=1, device_id={"blk": following})
    pl.semaphore_signal(barrier, inc=1, device_id={"blk": previous})

    loads = [
        pltpu.make_async_copy(w, weights.at[side], weight_sem.at[side])
        for side, w in enumerate((w_a, w_b))
    ]
    for side, pair in enumerate(((ref_a, val_a), (ref_b, val_b))):
        for p in range(4):
            for t in range(2):
                pltpu.make_async_copy(
                    pair[t].at[:, pl.ds(p * PAIR, PAIR)], staged.at[side, p, t], stage_sem.at[side]
                ).start()
    for load in loads:
        load.start()

    pl.semaphore_wait(barrier, 6)

    def landed(ref, sem):
        pltpu.make_async_remote_copy(
            src_ref=ref, dst_ref=ref, send_sem=sem, recv_sem=sem, device_id={"head": other}
        ).wait_recv()

    def left(ref, sem):
        pltpu.make_async_remote_copy(
            src_ref=ref, dst_ref=ref, send_sem=sem, recv_sem=sem, device_id={"head": other}
        ).wait_send()

    def share(side, p):
        return pltpu.make_async_remote_copy(
            src_ref=staged.at[side, p],
            dst_ref=held.at[side, place + 1 + side],
            send_sem=share_send.at[side],
            recv_sem=share_recv.at[side, place],
            device_id={"blk": base + p, "head": other},
        )

    pltpu.make_async_copy(staged.at[1], staged.at[1], stage_sem.at[1]).wait()
    for p in range(4):
        share(1, p).start()
    pltpu.make_async_copy(staged.at[0], staged.at[0], stage_sem.at[0]).wait()
    left(staged.at[1], share_send.at[1])
    for p in range(4):
        share(0, p).start()

    def wait_share(side, blocks):
        for block in blocks:
            landed(held.at[side, block + 1 + side], share_recv.at[side, block])

    bands = ((1, 4, 0, 2, True), (1, 2, 6, 1, False), (0, 4, 0, 1, True), (0, 1, 5, 2, False))

    def band(index):
        side, first, target, blocks, forward = bands[index]
        return pltpu.make_async_remote_copy(
            src_ref=held.at[side, pl.ds(first, blocks)],
            dst_ref=held.at[side, pl.ds(target, blocks)],
            send_sem=band_send,
            recv_sem=band_recv.at[index],
            device_id={"blk": following if forward else previous},
        )

    def turn(side, first, blocks):
        for position in range(first, first + blocks):
            turned[side, position] = held[side, position, 1].T

    def attn_copies(side, n):
        if n in (0, 3):
            pieces = ((n, pl.ds(0, ROWS)),)
        else:
            pieces = (
                (n, pl.ds(pl.multiple_of(other * HALF, HALF), HALF)),
                (3 - n, pl.ds(pl.multiple_of(head * HALF, HALF), HALF)),
            )
        return [
            pltpu.make_async_remote_copy(
                src_ref=attn.at[side, n, rows],
                dst_ref=gathered.at[side, place, rows],
                send_sem=attn_send.at[side],
                recv_sem=attn_recv.at[side],
                device_id={"blk": base + target, "head": other},
            )
            for target, rows in pieces
        ]

    def pairs(side, n, positions):
        both = split_heads(held[side, n + 1 + side, 0])
        return [
            pair_part(both, held[1 - side, position, 0], turned[1 - side, position])
            for position in positions
        ]

    def ready(side, n, part):
        attn[side, n] = finish(part)

    def begin(side, n, positions):
        part = merge_parts(pairs(side, n, positions))
        if len(positions) == 4:
            ready(side, n, part)
        else:
            stats[side, n, 0:1], stats[side, n, 1:2] = part[0], part[1]
            sums[side, n, :HALF], sums[side, n, HALF:] = part[2], part[3]

    def complete(side, n, positions):
        state = (
            stats[side, n, 0:1],
            stats[side, n, 1:2],
            sums[side, n, :HALF],
            sums[side, n, HALF:],
        )
        ready(side, n, merge_parts([state] + pairs(side, n, positions)))

    def give(*tasks):
        for side, n in tasks:
            for copy in attn_copies(side, n):
                copy.start()

    def pass_on(index):
        side, first, _, blocks, _ = bands[index]
        wait_share(side, range(first - 1 - side, first - 1 - side + blocks))
        band(index).start()

    pass_on(0)
    pass_on(1)
    wait_share(1, (1,))
    turn(1, 2, 4)
    pass_on(2)
    pass_on(3)
    wait_share(0, (2,))
    begin(0, 2, (2, 3, 4, 5))
    give((0, 2),)
    begin(0, 3, (3, 4, 5))
    begin(0, 1, (2, 3, 4))
    begin(0, 0, (2, 3))
    band(0).wait_recv()
    band(1).wait_recv()
    turn(1, 0, 2)
    turn(1, 6, 1)
    complete(0, 3, (6,))
    complete(0, 1, (1,))
    complete(0, 0, (0, 1))
    give((0, 3), (0, 1), (0, 0))
    turn(0, 1, 4)
    begin(1, 1, (1, 2, 3, 4))
    give((1, 1),)
    begin(1, 2, (2, 3, 4))
    begin(1, 3, (3, 4))
    begin(1, 0, (1, 2, 3))
    band(3).wait_recv()
    turn(0, 5, 2)
    complete(1, 2, (5,))
    complete(1, 3, (5, 6))
    give((1, 2), (1, 3))
    band(2).wait_recv()
    turn(0, 0, 1)
    complete(1, 0, (0,))
    give((1, 0),)

    mine = pl.ds(pl.multiple_of(head * HALF, HALF), HALF)
    theirs = pl.ds(pl.multiple_of(other * HALF, HALF), HALF)

    def part(side, chunk):
        return pltpu.make_async_remote_copy(
            src_ref=outgoing.at[side, chunk],
            dst_ref=incoming.at[side, chunk],
            send_sem=part_send.at[side],
            recv_sem=part_recv.at[side, chunk],
            device_id={"blk": base + swapped, "head": other},
        )

    for side in range(2):
        loads[side].wait()
        landed(gathered.at[side], attn_recv.at[side])
        rows = jnp.concatenate(
            [
                jnp.concatenate([gathered[side, p, half] for p in range(4)], axis=1)
                for half in (mine, theirs)
            ],
            axis=0,
        )
        for chunk in range(CHUNKS):
            product = jnp.dot(
                rows,
                weights[side, :, chunk * PIECE : (chunk + 1) * PIECE],
                preferred_element_type=F32,
            )
            outgoing[side, chunk] = product[HALF:].astype(BF16)
            part(side, chunk).start()
            own[side, chunk] = product[:HALF]

    left(staged.at[0], share_send.at[0])
    left(held.at[0, pl.ds(0, 6)], band_send)
    for side in range(2):
        left(attn.at[side], attn_send.at[side])
        left(outgoing.at[side], part_send.at[side])

    for side in range(2):
        for chunk in range(CHUNKS):
            part(side, chunk).wait_recv()
            out[side, :, chunk * PIECE : (chunk + 1) * PIECE] = (
                own[side, chunk] + incoming[side, chunk].astype(F32)
            ).astype(BF16)


def solution(mesh):
    count = mesh.shape["blk"]

    def shards(ref_a, val_a, ref_b, val_b, w_out_a, w_out_b):
        hbm = pl.BlockSpec(memory_space=pltpu.HBM)
        vmem = pl.BlockSpec(memory_space=pltpu.VMEM)
        out = pltpu.VMEM((2, HALF, WIDTH), BF16)
        results = pl.pallas_call(
            functools.partial(kernel, count),
            out_shape=out,
            in_specs=[hbm] * 6,
            out_specs=vmem,
            scratch_shapes=[
                pltpu.VMEM((2, 4, 2, ROWS, PAIR), BF16),
                pltpu.VMEM((2, 7, 2, ROWS, PAIR), BF16),
                pltpu.VMEM((2, 7, PAIR, ROWS), BF16),
                pltpu.VMEM((2, WIDTH // 2, WIDTH), BF16),
                pltpu.VMEM((2, 4, 8, 2 * ROWS), F32),
                pltpu.VMEM((2, 4, PAIR, ROWS), F32),
                pltpu.VMEM((2, 4, ROWS, PAIR), BF16),
                pltpu.VMEM((2, 4, ROWS, PAIR), BF16),
                pltpu.VMEM((2, CHUNKS, HALF, PIECE), BF16),
                pltpu.VMEM((2, CHUNKS, HALF, PIECE), BF16),
                pltpu.VMEM((2, CHUNKS, HALF, PIECE), F32),
                pltpu.SemaphoreType.DMA((2,)),
                pltpu.SemaphoreType.DMA((2,)),
                pltpu.SemaphoreType.DMA((2,)),
                pltpu.SemaphoreType.DMA((2, 4)),
                pltpu.SemaphoreType.DMA,
                pltpu.SemaphoreType.DMA((4,)),
                pltpu.SemaphoreType.DMA((2,)),
                pltpu.SemaphoreType.DMA((2,)),
                pltpu.SemaphoreType.DMA((2,)),
                pltpu.SemaphoreType.DMA((2, CHUNKS)),
            ],
            compiler_params=pltpu.CompilerParams(
                collective_id=0, has_side_effects=True, vmem_limit_bytes=32 * 1024 * 1024
            ),
        )(
            *(
                pltpu.with_memory_space_constraint(array, pltpu.HBM)
                for array in (ref_a, val_a, ref_b, val_b, w_out_a, w_out_b)
            )
        )
        return results[0], results[1]

    return jax.shard_map(
        shards,
        mesh=mesh,
        in_specs=(
            P("blk", "head"),
            P("blk", "head"),
            P("blk", "head"),
            P("blk", "head"),
            P("head", None),
            P("head", None),
        ),
        out_specs=(P(("blk", "head"), None), P(("blk", "head"), None)),
        check_vma=False,
    )
```

```python
import functools
import math

import jax
import jax.numpy as jnp
from jax import lax
from jax.experimental import pallas as pl
from jax.experimental.pallas import tpu as pltpu
from jax.sharding import PartitionSpec as P


ROWS = 128
HALF = 64
PAIR = 128
WIDTH = 1024
CHUNKS = 2
PIECE = WIDTH // CHUNKS
SCORE = 0.125 * math.log2(math.e)
BF16 = jnp.bfloat16
F32 = jnp.float32


def split_heads(query):
    lane = lax.broadcasted_iota(jnp.int32, (ROWS, PAIR), 1)
    query = query.astype(F32)
    zero = jnp.zeros_like(query)
    return jnp.concatenate(
        [jnp.where(lane < HALF, query, zero), jnp.where(lane < HALF, zero, query)], axis=0
    ).astype(BF16)


def pair_part(both, key, value):
    scores = lax.dot_general(key, both, (((1,), (1,)), ((), ())), preferred_element_type=F32)
    top = jnp.max(scores, axis=0, keepdims=True)
    expo = jnp.exp2((scores - top) * SCORE)
    accum = jnp.dot(value, expo.astype(BF16), preferred_element_type=F32)
    return top, jnp.sum(expo, axis=0, keepdims=True), accum[:HALF, :ROWS], accum[HALF:, ROWS:]


def merge_parts(parts):
    top = functools.reduce(jnp.maximum, [part[0] for part in parts])
    scales = [jnp.exp2((part[0] - top) * SCORE) for part in parts]
    return (
        top,
        sum(scale * part[1] for scale, part in zip(scales, parts)),
        sum(scale[:, :ROWS] * part[2] for scale, part in zip(scales, parts)),
        sum(scale[:, ROWS:] * part[3] for scale, part in zip(scales, parts)),
    )


def finish(part):
    _, total, first, second = part
    result = jnp.concatenate([first / total[:, :ROWS], second / total[:, ROWS:]], axis=0)
    return result.T.astype(BF16)


def kernel(
    count,
    ref_a,
    val_a,
    ref_b,
    val_b,
    w_a,
    w_b,
    out,
    staged,
    held,
    turned,
    weights,
    stats,
    sums,
    attn,
    gathered,
    outgoing,
    incoming,
    own,
    here_sem,
    near_sem,
    weight_sem,
    stage_sem,
    share_send,
    share_recv,
    band_send,
    band_recv,
    attn_send,
    attn_recv,
    part_send,
    part_recv,
):
    blk, head = lax.axis_index("blk"), lax.axis_index("head")
    place = lax.rem(blk, 4)
    base = blk - place
    other = 1 - head
    following = lax.rem(blk + 4, count)
    previous = lax.rem(blk + count - 4, count)
    swapped = lax.rem(place, 2) * 2 + place // 2

    herald = (place == 1) & (head == 1)
    barrier = pltpu.get_barrier_semaphore()
    for p in (0, 2, 3):
        pl.semaphore_signal(barrier, inc=1, device_id={"blk": base + p, "head": other})

    @pl.when(head == 1)
    def _():
        pl.semaphore_signal(barrier, inc=1, device_id={"blk": base + 1, "head": other})

    loads = [
        pltpu.make_async_copy(w, weights.at[side], weight_sem.at[side])
        for side, w in enumerate((w_a, w_b))
    ]
    for side, pair in enumerate(((ref_a, val_a), (ref_b, val_b))):
        for p in range(4):
            for t in range(2):
                pltpu.make_async_copy(
                    pair[t].at[:, pl.ds(p * PAIR, PAIR)], staged.at[side, p, t], stage_sem.at[side]
                ).start()
    for load in loads:
        load.start()

    @pl.when(jnp.logical_not(herald))
    def _():
        pl.semaphore_wait(barrier, 4)

    @pl.when(head == 0)
    def _():
        pl.semaphore_signal(here_sem, inc=1, device_id={"blk": base + 1, "head": other})

    @pl.when(herald)
    def _():
        pl.semaphore_wait(here_sem, 4)
        for near in (previous, following):
            pl.semaphore_signal(barrier, inc=1, device_id={"blk": near})


    def landed(ref, sem):
        pltpu.make_async_remote_copy(
            src_ref=ref, dst_ref=ref, send_sem=sem, recv_sem=sem, device_id={"head": other}
        ).wait_recv()

    def left(ref, sem):
        pltpu.make_async_remote_copy(
            src_ref=ref, dst_ref=ref, send_sem=sem, recv_sem=sem, device_id={"head": other}
        ).wait_send()

    def share(side, p):
        return pltpu.make_async_remote_copy(
            src_ref=staged.at[side, p],
            dst_ref=held.at[side, place + 1 + side],
            send_sem=share_send.at[side],
            recv_sem=share_recv.at[side, place],
            device_id={"blk": base + p, "head": other},
        )

    pltpu.make_async_copy(staged.at[1], staged.at[1], stage_sem.at[1]).wait()
    for p in range(4):
        share(1, p).start()
    pltpu.make_async_copy(staged.at[0], staged.at[0], stage_sem.at[0]).wait()

    @pl.when(jnp.logical_not(herald))
    def _():
        left(staged.at[1], share_send.at[1])

    for p in range(4):
        share(0, p).start()

    @pl.when(herald)
    def _():
        pl.semaphore_wait(barrier, 2)
        for p in range(4):
            pl.semaphore_signal(near_sem, inc=1, device_id={"blk": base + p, "head": other})
        for p in (0, 2, 3):
            pl.semaphore_signal(near_sem, inc=1, device_id={"blk": base + p})

    def wait_share(side, blocks):
        for block in blocks:
            landed(held.at[side, block + 1 + side], share_recv.at[side, block])

    bands = ((1, 4, 0, 2, True), (1, 2, 6, 1, False), (0, 4, 0, 1, True), (0, 1, 5, 2, False))

    def band(index):
        side, first, target, blocks, forward = bands[index]
        return pltpu.make_async_remote_copy(
            src_ref=held.at[side, pl.ds(first, blocks)],
            dst_ref=held.at[side, pl.ds(target, blocks)],
            send_sem=band_send,
            recv_sem=band_recv.at[index],
            device_id={"blk": following if forward else previous},
        )

    def turn(side, first, blocks):
        for position in range(first, first + blocks):
            turned[side, position] = held[side, position, 1].T

    def attn_copies(side, n):
        if n in (0, 3):
            pieces = ((n, pl.ds(0, ROWS)),)
        else:
            pieces = (
                (n, pl.ds(pl.multiple_of(other * HALF, HALF), HALF)),
                (3 - n, pl.ds(pl.multiple_of(head * HALF, HALF), HALF)),
            )
        return [
            pltpu.make_async_remote_copy(
                src_ref=attn.at[side, n, rows],
                dst_ref=gathered.at[side, place, rows],
                send_sem=attn_send.at[side],
                recv_sem=attn_recv.at[side],
                device_id={"blk": base + target, "head": other},
            )
            for target, rows in pieces
        ]

    def pairs(side, n, positions):
        both = split_heads(held[side, n + 1 + side, 0])
        return [
            pair_part(both, held[1 - side, position, 0], turned[1 - side, position])
            for position in positions
        ]

    def ready(side, n, part):
        attn[side, n] = finish(part)

    def begin(side, n, positions):
        part = merge_parts(pairs(side, n, positions))
        if len(positions) == 4:
            ready(side, n, part)
        else:
            stats[side, n, 0:1], stats[side, n, 1:2] = part[0], part[1]
            sums[side, n, :HALF], sums[side, n, HALF:] = part[2], part[3]

    def complete(side, n, positions):
        state = (
            stats[side, n, 0:1],
            stats[side, n, 1:2],
            sums[side, n, :HALF],
            sums[side, n, HALF:],
        )
        ready(side, n, merge_parts([state] + pairs(side, n, positions)))

    def give(*tasks):
        for side, n in tasks:
            for copy in attn_copies(side, n):
                copy.start()

    def pass_on(index):
        side, first, _, blocks, _ = bands[index]
        wait_share(side, range(first - 1 - side, first - 1 - side + blocks))
        band(index).start()

    @pl.when(jnp.logical_not(herald))
    def _():
        pl.semaphore_wait(near_sem, 1)

    pass_on(0)
    pass_on(1)
    wait_share(1, (1,))
    turn(1, 2, 4)
    pass_on(2)
    pass_on(3)
    wait_share(0, (2,))
    begin(0, 2, (2, 3, 4, 5))
    give((0, 2),)
    begin(0, 3, (3, 4, 5))
    begin(0, 1, (2, 3, 4))
    begin(0, 0, (2, 3))
    turn(0, 1, 4)
    begin(1, 1, (1, 2, 3, 4))
    give((1, 1),)
    begin(1, 2, (2, 3, 4))
    begin(1, 3, (3, 4))
    begin(1, 0, (1, 2, 3))
    band(1).wait_recv()
    turn(1, 6, 1)
    complete(0, 3, (6,))
    give((0, 3),)
    band(0).wait_recv()
    turn(1, 0, 2)
    complete(0, 1, (1,))
    complete(0, 0, (0, 1))
    give((0, 1), (0, 0))
    band(3).wait_recv()
    turn(0, 5, 2)
    complete(1, 2, (5,))
    complete(1, 3, (5, 6))
    give((1, 2), (1, 3))
    band(2).wait_recv()
    turn(0, 0, 1)
    complete(1, 0, (0,))
    give((1, 0),)

    mine = pl.ds(pl.multiple_of(head * HALF, HALF), HALF)
    theirs = pl.ds(pl.multiple_of(other * HALF, HALF), HALF)

    def part(side, chunk):
        return pltpu.make_async_remote_copy(
            src_ref=outgoing.at[side, chunk],
            dst_ref=incoming.at[side, chunk],
            send_sem=part_send.at[side],
            recv_sem=part_recv.at[side, chunk],
            device_id={"blk": base + swapped, "head": other},
        )

    for side in range(2):
        loads[side].wait()
        landed(gathered.at[side], attn_recv.at[side])
        rows = jnp.concatenate(
            [
                jnp.concatenate([gathered[side, p, half] for p in range(4)], axis=1)
                for half in (mine, theirs)
            ],
            axis=0,
        )
        for chunk in range(CHUNKS):
            product = jnp.dot(
                rows,
                weights[side, :, chunk * PIECE : (chunk + 1) * PIECE],
                preferred_element_type=F32,
            )
            outgoing[side, chunk] = product[HALF:].astype(BF16)
            part(side, chunk).start()
            own[side, chunk] = product[:HALF]

    @pl.when(herald)
    def _():
        left(staged.at[1], share_send.at[1])

    left(staged.at[0], share_send.at[0])
    left(held.at[0, pl.ds(0, 6)], band_send)
    for side in range(2):
        left(attn.at[side], attn_send.at[side])
        left(outgoing.at[side], part_send.at[side])

    for side in range(2):
        for chunk in range(CHUNKS):
            part(side, chunk).wait_recv()
            out[side, :, chunk * PIECE : (chunk + 1) * PIECE] = (
                own[side, chunk] + incoming[side, chunk].astype(F32)
            ).astype(BF16)


def solution(mesh):
    count = mesh.shape["blk"]

    def shards(ref_a, val_a, ref_b, val_b, w_out_a, w_out_b):
        hbm = pl.BlockSpec(memory_space=pltpu.HBM)
        vmem = pl.BlockSpec(memory_space=pltpu.VMEM)
        out = pltpu.VMEM((2, HALF, WIDTH), BF16)
        results = pl.pallas_call(
            functools.partial(kernel, count),
            out_shape=out,
            in_specs=[hbm] * 6,
            out_specs=vmem,
            scratch_shapes=[
                pltpu.VMEM((2, 4, 2, ROWS, PAIR), BF16),
                pltpu.VMEM((2, 7, 2, ROWS, PAIR), BF16),
                pltpu.VMEM((2, 7, PAIR, ROWS), BF16),
                pltpu.VMEM((2, WIDTH // 2, WIDTH), BF16),
                pltpu.VMEM((2, 4, 8, 2 * ROWS), F32),
                pltpu.VMEM((2, 4, PAIR, ROWS), F32),
                pltpu.VMEM((2, 4, ROWS, PAIR), BF16),
                pltpu.VMEM((2, 4, ROWS, PAIR), BF16),
                pltpu.VMEM((2, CHUNKS, HALF, PIECE), BF16),
                pltpu.VMEM((2, CHUNKS, HALF, PIECE), BF16),
                pltpu.VMEM((2, CHUNKS, HALF, PIECE), F32),
                pltpu.SemaphoreType.REGULAR,
                pltpu.SemaphoreType.REGULAR,
                pltpu.SemaphoreType.DMA((2,)),
                pltpu.SemaphoreType.DMA((2,)),
                pltpu.SemaphoreType.DMA((2,)),
                pltpu.SemaphoreType.DMA((2, 4)),
                pltpu.SemaphoreType.DMA,
                pltpu.SemaphoreType.DMA((4,)),
                pltpu.SemaphoreType.DMA((2,)),
                pltpu.SemaphoreType.DMA((2,)),
                pltpu.SemaphoreType.DMA((2,)),
                pltpu.SemaphoreType.DMA((2, CHUNKS)),
            ],
            compiler_params=pltpu.CompilerParams(
                collective_id=0, has_side_effects=True, vmem_limit_bytes=32 * 1024 * 1024
            ),
        )(
            *(
                pltpu.with_memory_space_constraint(array, pltpu.HBM)
                for array in (ref_a, val_a, ref_b, val_b, w_out_a, w_out_b)
            )
        )
        return results[0], results[1]

    return jax.shard_map(
        shards,
        mesh=mesh,
        in_specs=(
            P("blk", "head"),
            P("blk", "head"),
            P("blk", "head"),
            P("blk", "head"),
            P("head", None),
            P("head", None),
        ),
        out_specs=(P(("blk", "head"), None), P(("blk", "head"), None)),
        check_vma=False,
    )
```

```python
import functools
import math

import jax
import jax.numpy as jnp
from jax import lax
from jax.experimental import pallas as pl
from jax.experimental.pallas import tpu as pltpu
from jax.sharding import PartitionSpec as P


ROWS = 128
HALF = 64
PAIR = 128
WIDTH = 1024
CHUNKS = 2
PIECE = WIDTH // CHUNKS
SCORE = 0.125 * math.log2(math.e)
BF16 = jnp.bfloat16
F32 = jnp.float32


def split_heads(query):
    lane = lax.broadcasted_iota(jnp.int32, (ROWS, PAIR), 1)
    query = query.astype(F32)
    zero = jnp.zeros_like(query)
    return jnp.concatenate(
        [jnp.where(lane < HALF, query, zero), jnp.where(lane < HALF, zero, query)], axis=0
    ).astype(BF16)


def pair_part(both, key, value):
    scores = lax.dot_general(key, both, (((1,), (1,)), ((), ())), preferred_element_type=F32)
    top = jnp.max(scores, axis=0, keepdims=True)
    expo = jnp.exp2((scores - top) * SCORE)
    accum = jnp.dot(value, expo.astype(BF16), preferred_element_type=F32)
    return top, jnp.sum(expo, axis=0, keepdims=True), accum[:HALF, :ROWS], accum[HALF:, ROWS:]


def merge_parts(parts):
    top = functools.reduce(jnp.maximum, [part[0] for part in parts])
    scales = [jnp.exp2((part[0] - top) * SCORE) for part in parts]
    return (
        top,
        sum(scale * part[1] for scale, part in zip(scales, parts)),
        sum(scale[:, :ROWS] * part[2] for scale, part in zip(scales, parts)),
        sum(scale[:, ROWS:] * part[3] for scale, part in zip(scales, parts)),
    )


def finish(part):
    _, total, first, second = part
    result = jnp.concatenate([first / total[:, :ROWS], second / total[:, ROWS:]], axis=0)
    return result.T.astype(BF16)


def kernel(
    count,
    ref_a,
    val_a,
    ref_b,
    val_b,
    w_a,
    w_b,
    out,
    staged,
    held,
    turned,
    weights,
    stats,
    sums,
    attn,
    gathered,
    outgoing,
    incoming,
    own,
    here_sem,
    near_sem,
    weight_sem,
    stage_sem,
    share_send,
    share_recv,
    band_send,
    band_recv,
    attn_send,
    attn_recv,
    part_send,
    part_recv,
):
    blk, head = lax.axis_index("blk"), lax.axis_index("head")
    place = lax.rem(blk, 4)
    base = blk - place
    other = 1 - head
    following = lax.rem(blk + 4, count)
    previous = lax.rem(blk + count - 4, count)
    swapped = lax.rem(place, 2) * 2 + place // 2

    herald = (place == 1) & (head == 1)
    barrier = pltpu.get_barrier_semaphore()
    for p in (0, 2, 3):
        pl.semaphore_signal(barrier, inc=1, device_id={"blk": base + p, "head": other})

    @pl.when(head == 1)
    def _():
        pl.semaphore_signal(barrier, inc=1, device_id={"blk": base + 1, "head": other})

    loads = [
        pltpu.make_async_copy(w, weights.at[side], weight_sem.at[side])
        for side, w in enumerate((w_a, w_b))
    ]
    for side, pair in ((1, (ref_b, val_b)), (0, (ref_a, val_a))):
        for t in range(2):
            for p in range(4):
                pltpu.make_async_copy(
                    pair[t].at[:, pl.ds(p * PAIR, PAIR)], staged.at[side, t, p], stage_sem.at[side, t]
                ).start()
    for load in loads:
        load.start()

    @pl.when(jnp.logical_not(herald))
    def _():
        pl.semaphore_wait(barrier, 4)

    @pl.when(head == 0)
    def _():
        pl.semaphore_signal(here_sem, inc=1, device_id={"blk": base + 1, "head": other})

    @pl.when(herald)
    def _():
        pl.semaphore_wait(here_sem, 4)
        for near in (previous, following):
            pl.semaphore_signal(barrier, inc=1, device_id={"blk": near})


    def landed(ref, sem):
        pltpu.make_async_remote_copy(
            src_ref=ref, dst_ref=ref, send_sem=sem, recv_sem=sem, device_id={"head": other}
        ).wait_recv()

    def left(ref, sem):
        pltpu.make_async_remote_copy(
            src_ref=ref, dst_ref=ref, send_sem=sem, recv_sem=sem, device_id={"head": other}
        ).wait_send()

    def share(side, t, p):
        return pltpu.make_async_remote_copy(
            src_ref=staged.at[side, t, p],
            dst_ref=held.at[side, t, place + 1 + side],
            send_sem=share_send.at[side, t],
            recv_sem=share_recv.at[side, t, place],
            device_id={"blk": base + p, "head": other},
        )

    def shares(side, t):
        pltpu.make_async_copy(staged.at[side, t], staged.at[side, t], stage_sem.at[side, t]).wait()
        for p in range(4):
            share(side, t, p).start()

    shares(1, 0)
    shares(1, 1)
    for t in range(2):

        @pl.when(jnp.logical_not(herald))
        def _():
            left(staged.at[1, t], share_send.at[1, t])

        shares(0, t)

    @pl.when(herald)
    def _():
        pl.semaphore_wait(barrier, 2)
        for p in range(4):
            pl.semaphore_signal(near_sem, inc=1, device_id={"blk": base + p, "head": other})
        for p in (0, 2, 3):
            pl.semaphore_signal(near_sem, inc=1, device_id={"blk": base + p})

    def wait_share(side, t, blocks):
        for block in blocks:
            landed(held.at[side, t, block + 1 + side], share_recv.at[side, t, block])

    bands = ((1, 4, 0, 2, True), (1, 2, 6, 1, False), (0, 4, 0, 1, True), (0, 1, 5, 2, False))

    def band(index, t):
        side, first, target, blocks, forward = bands[index]
        return pltpu.make_async_remote_copy(
            src_ref=held.at[side, t, pl.ds(first, blocks)],
            dst_ref=held.at[side, t, pl.ds(target, blocks)],
            send_sem=band_send.at[t],
            recv_sem=band_recv.at[index, t],
            device_id={"blk": following if forward else previous},
        )

    def turn(side, first, blocks):
        for position in range(first, first + blocks):
            turned[side, position] = held[side, 1, position].T

    def pass_on(t, *indices):
        for index in indices:
            side, first, _, blocks, _ = bands[index]
            wait_share(side, t, range(first - 1 - side, first - 1 - side + blocks))
            band(index, t).start()

    def wait_band(index):
        for t in range(2):
            band(index, t).wait_recv()

    def attn_copies(side, n):
        if n in (0, 3):
            pieces = ((n, pl.ds(0, ROWS)),)
        else:
            pieces = (
                (n, pl.ds(pl.multiple_of(other * HALF, HALF), HALF)),
                (3 - n, pl.ds(pl.multiple_of(head * HALF, HALF), HALF)),
            )
        return [
            pltpu.make_async_remote_copy(
                src_ref=attn.at[side, n, rows],
                dst_ref=gathered.at[side, place, rows],
                send_sem=attn_send.at[side],
                recv_sem=attn_recv.at[side],
                device_id={"blk": base + target, "head": other},
            )
            for target, rows in pieces
        ]

    def pairs(side, n, positions):
        both = split_heads(held[side, 0, n + 1 + side])
        return [
            pair_part(both, held[1 - side, 0, position], turned[1 - side, position])
            for position in positions
        ]

    def ready(side, n, part):
        attn[side, n] = finish(part)

    def begin(side, n, positions):
        part = merge_parts(pairs(side, n, positions))
        if len(positions) == 4:
            ready(side, n, part)
        else:
            stats[side, n, 0:1], stats[side, n, 1:2] = part[0], part[1]
            sums[side, n, :HALF], sums[side, n, HALF:] = part[2], part[3]

    def complete(side, n, positions):
        state = (
            stats[side, n, 0:1],
            stats[side, n, 1:2],
            sums[side, n, :HALF],
            sums[side, n, HALF:],
        )
        ready(side, n, merge_parts([state] + pairs(side, n, positions)))

    def give(*tasks):
        for side, n in tasks:
            for copy in attn_copies(side, n):
                copy.start()

    @pl.when(jnp.logical_not(herald))
    def _():
        pl.semaphore_wait(near_sem, 1)

    pass_on(0, 0, 1)
    pass_on(1, 0, 1)
    for t in range(2):
        wait_share(1, t, (1,))
    turn(1, 2, 4)
    pass_on(0, 2, 3)
    pass_on(1, 2, 3)
    for t in range(2):
        wait_share(0, t, (2,))
    begin(0, 2, (2, 3, 4, 5))
    give((0, 2),)
    begin(0, 3, (3, 4, 5))
    begin(0, 1, (2, 3, 4))
    begin(0, 0, (2, 3))
    turn(0, 1, 4)
    begin(1, 1, (1, 2, 3, 4))
    give((1, 1),)
    begin(1, 2, (2, 3, 4))
    begin(1, 3, (3, 4))
    begin(1, 0, (1, 2, 3))
    wait_band(1)
    turn(1, 6, 1)
    complete(0, 3, (6,))
    give((0, 3),)
    wait_band(0)
    turn(1, 0, 2)
    complete(0, 1, (1,))
    complete(0, 0, (0, 1))
    give((0, 1), (0, 0))
    wait_band(3)
    turn(0, 5, 2)
    complete(1, 2, (5,))
    complete(1, 3, (5, 6))
    give((1, 2), (1, 3))
    wait_band(2)
    turn(0, 0, 1)
    complete(1, 0, (0,))
    give((1, 0),)

    mine = pl.ds(pl.multiple_of(head * HALF, HALF), HALF)
    theirs = pl.ds(pl.multiple_of(other * HALF, HALF), HALF)

    def part(side, chunk):
        return pltpu.make_async_remote_copy(
            src_ref=outgoing.at[side, chunk],
            dst_ref=incoming.at[side, chunk],
            send_sem=part_send.at[side],
            recv_sem=part_recv.at[side, chunk],
            device_id={"blk": base + swapped, "head": other},
        )

    for side in range(2):
        loads[side].wait()
        landed(gathered.at[side], attn_recv.at[side])
        rows = jnp.concatenate(
            [
                jnp.concatenate([gathered[side, p, half] for p in range(4)], axis=1)
                for half in (mine, theirs)
            ],
            axis=0,
        )
        for chunk in range(CHUNKS):
            product = jnp.dot(
                rows,
                weights[side, :, chunk * PIECE : (chunk + 1) * PIECE],
                preferred_element_type=F32,
            )
            outgoing[side, chunk] = product[HALF:].astype(BF16)
            part(side, chunk).start()
            own[side, chunk] = product[:HALF]

    @pl.when(herald)
    def _():
        for t in range(2):
            left(staged.at[1, t], share_send.at[1, t])

    for t in range(2):
        left(staged.at[0, t], share_send.at[0, t])
        left(held.at[0, 0, pl.ds(0, 6)], band_send.at[t])
    for side in range(2):
        left(attn.at[side], attn_send.at[side])
        left(outgoing.at[side], part_send.at[side])

    for side in range(2):
        for chunk in range(CHUNKS):
            part(side, chunk).wait_recv()
            out[side, :, chunk * PIECE : (chunk + 1) * PIECE] = (
                own[side, chunk] + incoming[side, chunk].astype(F32)
            ).astype(BF16)


def solution(mesh):
    count = mesh.shape["blk"]

    def shards(ref_a, val_a, ref_b, val_b, w_out_a, w_out_b):
        hbm = pl.BlockSpec(memory_space=pltpu.HBM)
        vmem = pl.BlockSpec(memory_space=pltpu.VMEM)
        out = pltpu.VMEM((2, HALF, WIDTH), BF16)
        results = pl.pallas_call(
            functools.partial(kernel, count),
            out_shape=out,
            in_specs=[hbm] * 6,
            out_specs=vmem,
            scratch_shapes=[
                pltpu.VMEM((2, 2, 4, ROWS, PAIR), BF16),
                pltpu.VMEM((2, 2, 7, ROWS, PAIR), BF16),
                pltpu.VMEM((2, 7, PAIR, ROWS), BF16),
                pltpu.VMEM((2, WIDTH // 2, WIDTH), BF16),
                pltpu.VMEM((2, 4, 8, 2 * ROWS), F32),
                pltpu.VMEM((2, 4, PAIR, ROWS), F32),
                pltpu.VMEM((2, 4, ROWS, PAIR), BF16),
                pltpu.VMEM((2, 4, ROWS, PAIR), BF16),
                pltpu.VMEM((2, CHUNKS, HALF, PIECE), BF16),
                pltpu.VMEM((2, CHUNKS, HALF, PIECE), BF16),
                pltpu.VMEM((2, CHUNKS, HALF, PIECE), F32),
                pltpu.SemaphoreType.REGULAR,
                pltpu.SemaphoreType.REGULAR,
                pltpu.SemaphoreType.DMA((2,)),
                pltpu.SemaphoreType.DMA((2, 2)),
                pltpu.SemaphoreType.DMA((2, 2)),
                pltpu.SemaphoreType.DMA((2, 2, 4)),
                pltpu.SemaphoreType.DMA((2,)),
                pltpu.SemaphoreType.DMA((4, 2)),
                pltpu.SemaphoreType.DMA((2,)),
                pltpu.SemaphoreType.DMA((2,)),
                pltpu.SemaphoreType.DMA((2,)),
                pltpu.SemaphoreType.DMA((2, CHUNKS)),
            ],
            compiler_params=pltpu.CompilerParams(
                collective_id=0, has_side_effects=True, vmem_limit_bytes=32 * 1024 * 1024
            ),
        )(
            *(
                pltpu.with_memory_space_constraint(array, pltpu.HBM)
                for array in (ref_a, val_a, ref_b, val_b, w_out_a, w_out_b)
            )
        )
        return results[0], results[1]

    return jax.shard_map(
        shards,
        mesh=mesh,
        in_specs=(
            P("blk", "head"),
            P("blk", "head"),
            P("blk", "head"),
            P("blk", "head"),
            P("head", None),
            P("head", None),
        ),
        out_specs=(P(("blk", "head"), None), P(("blk", "head"), None)),
        check_vma=False,
    )
```

```python
import functools
import math

import jax
import jax.numpy as jnp
from jax import lax
from jax.experimental import pallas as pl
from jax.experimental.pallas import tpu as pltpu
from jax.sharding import PartitionSpec as P


ROWS = 128
HALF = 64
PAIR = 128
WIDTH = 1024
CHUNKS = 2
PIECE = WIDTH // CHUNKS
SCORE = 0.125 * math.log2(math.e)
BF16 = jnp.bfloat16
F32 = jnp.float32


def split_heads(query):
    lane = lax.broadcasted_iota(jnp.int32, (ROWS, PAIR), 1)
    query = query.astype(F32)
    zero = jnp.zeros_like(query)
    return jnp.concatenate(
        [jnp.where(lane < HALF, query, zero), jnp.where(lane < HALF, zero, query)], axis=0
    ).astype(BF16)


def pair_part(both, key, value):
    scores = lax.dot_general(key, both, (((1,), (1,)), ((), ())), preferred_element_type=F32)
    top = jnp.max(scores, axis=0, keepdims=True)
    expo = jnp.exp2((scores - top) * SCORE)
    accum = jnp.dot(value, expo.astype(BF16), preferred_element_type=F32)
    return top, jnp.sum(expo, axis=0, keepdims=True), accum[:HALF, :ROWS], accum[HALF:, ROWS:]


def merge_parts(parts):
    top = functools.reduce(jnp.maximum, [part[0] for part in parts])
    scales = [jnp.exp2((part[0] - top) * SCORE) for part in parts]
    return (
        top,
        sum(scale * part[1] for scale, part in zip(scales, parts)),
        sum(scale[:, :ROWS] * part[2] for scale, part in zip(scales, parts)),
        sum(scale[:, ROWS:] * part[3] for scale, part in zip(scales, parts)),
    )


def finish(part):
    _, total, first, second = part
    result = jnp.concatenate([first / total[:, :ROWS], second / total[:, ROWS:]], axis=0)
    return result.T.astype(BF16)


def kernel(
    count,
    ref_a,
    val_a,
    ref_b,
    val_b,
    w_a,
    w_b,
    out,
    staged,
    held,
    turned,
    weights,
    stats,
    sums,
    attn,
    gathered,
    outgoing,
    incoming,
    own,
    here_sem,
    near_sem,
    weight_sem,
    stage_sem,
    share_send,
    share_recv,
    band_send,
    band_recv,
    attn_send,
    attn_recv,
    part_send,
    part_recv,
):
    blk, head = lax.axis_index("blk"), lax.axis_index("head")
    place = lax.rem(blk, 4)
    base = blk - place
    other = 1 - head
    following = lax.rem(blk + 4, count)
    previous = lax.rem(blk + count - 4, count)
    swapped = lax.rem(place, 2) * 2 + place // 2

    herald = (place == 1) & (head == 1)
    barrier = pltpu.get_barrier_semaphore()
    for p in (0, 2, 3):
        pl.semaphore_signal(barrier, inc=1, device_id={"blk": base + p, "head": other})

    @pl.when(head == 1)
    def _():
        pl.semaphore_signal(barrier, inc=1, device_id={"blk": base + 1, "head": other})

    loads = [
        pltpu.make_async_copy(w, weights.at[side], weight_sem.at[side])
        for side, w in enumerate((w_a, w_b))
    ]
    for side, pair in ((1, (ref_b, val_b)), (0, (ref_a, val_a))):
        for t in range(2):
            for p in range(4):
                pltpu.make_async_copy(
                    pair[t].at[:, pl.ds(p * PAIR, PAIR)], staged.at[side, t, p], stage_sem.at[side, t]
                ).start()
    for load in loads:
        load.start()

    @pl.when(jnp.logical_not(herald))
    def _():
        pl.semaphore_wait(barrier, 4)

    @pl.when(head == 0)
    def _():
        pl.semaphore_signal(here_sem, inc=1, device_id={"blk": base + 1, "head": other})

    @pl.when(herald)
    def _():
        pl.semaphore_wait(here_sem, 4)
        for near in (previous, following):
            pl.semaphore_signal(barrier, inc=1, device_id={"blk": near})


    def landed(ref, sem):
        pltpu.make_async_remote_copy(
            src_ref=ref, dst_ref=ref, send_sem=sem, recv_sem=sem, device_id={"head": other}
        ).wait_recv()

    def left(ref, sem):
        pltpu.make_async_remote_copy(
            src_ref=ref, dst_ref=ref, send_sem=sem, recv_sem=sem, device_id={"head": other}
        ).wait_send()

    def share(side, t, p):
        return pltpu.make_async_remote_copy(
            src_ref=staged.at[side, t, p],
            dst_ref=held.at[side, t, place + 1 + side],
            send_sem=share_send.at[side, t],
            recv_sem=share_recv.at[side, t, place],
            device_id={"blk": base + p, "head": other},
        )

    def shares(side, t):
        pltpu.make_async_copy(staged.at[side, t], staged.at[side, t], stage_sem.at[side, t]).wait()
        for p in range(4):
            share(side, t, p).start()

    shares(1, 0)
    shares(1, 1)
    for t in range(2):

        @pl.when(jnp.logical_not(herald))
        def _():
            left(staged.at[1, t], share_send.at[1, t])

        @pl.when(place != 2)
        def _():
            shares(0, t)

    @pl.when(herald)
    def _():
        pl.semaphore_wait(barrier, 2)
        for p in range(4):
            pl.semaphore_signal(near_sem, inc=1, device_id={"blk": base + p, "head": other})
        for p in (0, 2, 3):
            pl.semaphore_signal(near_sem, inc=1, device_id={"blk": base + p})

    def wait_share(side, t, blocks):
        for block in blocks:
            landed(held.at[side, t, block + 1 + side], share_recv.at[side, t, block])

    bands = ((1, 4, 0, 2, True), (1, 2, 6, 1, False), (0, 4, 0, 1, True), (0, 1, 5, 2, False))

    def band(index, t):
        side, first, target, blocks, forward = bands[index]
        return pltpu.make_async_remote_copy(
            src_ref=held.at[side, t, pl.ds(first, blocks)],
            dst_ref=held.at[side, t, pl.ds(target, blocks)],
            send_sem=band_send.at[t],
            recv_sem=band_recv.at[index, t],
            device_id={"blk": following if forward else previous},
        )

    def turn(side, first, blocks):
        for position in range(first, first + blocks):
            turned[side, position] = held[side, 1, position].T

    def pass_on(t, *indices):
        for index in indices:
            side, first, _, blocks, _ = bands[index]
            wait_share(side, t, range(first - 1 - side, first - 1 - side + blocks))
            band(index, t).start()

    def wait_band(index):
        for t in range(2):
            band(index, t).wait_recv()

    def attn_copies(side, n):
        if n in (0, 3):
            pieces = ((n, pl.ds(0, ROWS)),)
        else:
            pieces = (
                (n, pl.ds(pl.multiple_of(other * HALF, HALF), HALF)),
                (3 - n, pl.ds(pl.multiple_of(head * HALF, HALF), HALF)),
            )
        return [
            pltpu.make_async_remote_copy(
                src_ref=attn.at[side, n, rows],
                dst_ref=gathered.at[side, place, rows],
                send_sem=attn_send.at[side],
                recv_sem=attn_recv.at[side],
                device_id={"blk": base + target, "head": other},
            )
            for target, rows in pieces
        ]

    def pairs(side, n, positions):
        both = split_heads(held[side, 0, n + 1 + side])
        return [
            pair_part(both, held[1 - side, 0, position], turned[1 - side, position])
            for position in positions
        ]

    def ready(side, n, part):
        attn[side, n] = finish(part)

    def begin(side, n, positions):
        part = merge_parts(pairs(side, n, positions))
        if len(positions) == 4:
            ready(side, n, part)
        else:
            stats[side, n, 0:1], stats[side, n, 1:2] = part[0], part[1]
            sums[side, n, :HALF], sums[side, n, HALF:] = part[2], part[3]

    def complete(side, n, positions):
        state = (
            stats[side, n, 0:1],
            stats[side, n, 1:2],
            sums[side, n, :HALF],
            sums[side, n, HALF:],
        )
        ready(side, n, merge_parts([state] + pairs(side, n, positions)))

    def give(*tasks):
        for side, n in tasks:
            for copy in attn_copies(side, n):
                copy.start()

    @pl.when(jnp.logical_not(herald))
    def _():
        pl.semaphore_wait(near_sem, 1)

    pass_on(0, 0, 1)
    pass_on(1, 0, 1)
    pass_on(0, 2, 3)
    pass_on(1, 2, 3)

    @pl.when(place == 2)
    def _():
        for t in range(2):
            shares(0, t)

    for t in range(2):
        wait_share(1, t, (1,))
    turn(1, 2, 4)
    for t in range(2):
        wait_share(0, t, (2,))
    begin(0, 2, (2, 3, 4, 5))
    give((0, 2),)
    begin(0, 3, (3, 4, 5))
    begin(0, 1, (2, 3, 4))
    begin(0, 0, (2, 3))
    turn(0, 1, 4)
    begin(1, 1, (1, 2, 3, 4))
    give((1, 1),)
    begin(1, 2, (2, 3, 4))
    begin(1, 3, (3, 4))
    begin(1, 0, (1, 2, 3))
    wait_band(1)
    turn(1, 6, 1)
    complete(0, 3, (6,))
    wait_band(3)
    turn(0, 5, 2)
    complete(1, 2, (5,))
    complete(1, 3, (5, 6))
    give((0, 3), (1, 2), (1, 3))
    wait_band(0)
    turn(1, 0, 2)
    complete(0, 1, (1,))
    complete(0, 0, (0, 1))
    give((0, 1), (0, 0))
    wait_band(2)
    turn(0, 0, 1)
    complete(1, 0, (0,))
    give((1, 0),)

    mine = pl.ds(pl.multiple_of(head * HALF, HALF), HALF)
    theirs = pl.ds(pl.multiple_of(other * HALF, HALF), HALF)

    def part(side, chunk):
        return pltpu.make_async_remote_copy(
            src_ref=outgoing.at[side, chunk],
            dst_ref=incoming.at[side, chunk],
            send_sem=part_send.at[side],
            recv_sem=part_recv.at[side, chunk],
            device_id={"blk": base + swapped, "head": other},
        )

    for side in range(2):
        loads[side].wait()
        landed(gathered.at[side], attn_recv.at[side])
        rows = jnp.concatenate(
            [
                jnp.concatenate([gathered[side, p, half] for p in range(4)], axis=1)
                for half in (mine, theirs)
            ],
            axis=0,
        )
        for chunk in range(CHUNKS):
            product = jnp.dot(
                rows,
                weights[side, :, chunk * PIECE : (chunk + 1) * PIECE],
                preferred_element_type=F32,
            )
            outgoing[side, chunk] = product[HALF:].astype(BF16)
            part(side, chunk).start()
            own[side, chunk] = product[:HALF]

    @pl.when(herald)
    def _():
        for t in range(2):
            left(staged.at[1, t], share_send.at[1, t])

    for t in range(2):
        left(staged.at[0, t], share_send.at[0, t])
        left(held.at[0, 0, pl.ds(0, 6)], band_send.at[t])
    for side in range(2):
        left(attn.at[side], attn_send.at[side])
        left(outgoing.at[side], part_send.at[side])

    for side in range(2):
        for chunk in range(CHUNKS):
            part(side, chunk).wait_recv()
            out[side, :, chunk * PIECE : (chunk + 1) * PIECE] = (
                own[side, chunk] + incoming[side, chunk].astype(F32)
            ).astype(BF16)


def solution(mesh):
    count = mesh.shape["blk"]

    def shards(ref_a, val_a, ref_b, val_b, w_out_a, w_out_b):
        hbm = pl.BlockSpec(memory_space=pltpu.HBM)
        vmem = pl.BlockSpec(memory_space=pltpu.VMEM)
        out = pltpu.VMEM((2, HALF, WIDTH), BF16)
        results = pl.pallas_call(
            functools.partial(kernel, count),
            out_shape=out,
            in_specs=[hbm] * 6,
            out_specs=vmem,
            scratch_shapes=[
                pltpu.VMEM((2, 2, 4, ROWS, PAIR), BF16),
                pltpu.VMEM((2, 2, 7, ROWS, PAIR), BF16),
                pltpu.VMEM((2, 7, PAIR, ROWS), BF16),
                pltpu.VMEM((2, WIDTH // 2, WIDTH), BF16),
                pltpu.VMEM((2, 4, 8, 2 * ROWS), F32),
                pltpu.VMEM((2, 4, PAIR, ROWS), F32),
                pltpu.VMEM((2, 4, ROWS, PAIR), BF16),
                pltpu.VMEM((2, 4, ROWS, PAIR), BF16),
                pltpu.VMEM((2, CHUNKS, HALF, PIECE), BF16),
                pltpu.VMEM((2, CHUNKS, HALF, PIECE), BF16),
                pltpu.VMEM((2, CHUNKS, HALF, PIECE), F32),
                pltpu.SemaphoreType.REGULAR,
                pltpu.SemaphoreType.REGULAR,
                pltpu.SemaphoreType.DMA((2,)),
                pltpu.SemaphoreType.DMA((2, 2)),
                pltpu.SemaphoreType.DMA((2, 2)),
                pltpu.SemaphoreType.DMA((2, 2, 4)),
                pltpu.SemaphoreType.DMA((2,)),
                pltpu.SemaphoreType.DMA((4, 2)),
                pltpu.SemaphoreType.DMA((2,)),
                pltpu.SemaphoreType.DMA((2,)),
                pltpu.SemaphoreType.DMA((2,)),
                pltpu.SemaphoreType.DMA((2, CHUNKS)),
            ],
            compiler_params=pltpu.CompilerParams(
                collective_id=0, has_side_effects=True, vmem_limit_bytes=32 * 1024 * 1024
            ),
        )(
            *(
                pltpu.with_memory_space_constraint(array, pltpu.HBM)
                for array in (ref_a, val_a, ref_b, val_b, w_out_a, w_out_b)
            )
        )
        return results[0], results[1]

    return jax.shard_map(
        shards,
        mesh=mesh,
        in_specs=(
            P("blk", "head"),
            P("blk", "head"),
            P("blk", "head"),
            P("blk", "head"),
            P("head", None),
            P("head", None),
        ),
        out_specs=(P(("blk", "head"), None), P(("blk", "head"), None)),
        check_vma=False,
    )
```

```python
import functools
import math

import jax
import jax.numpy as jnp
from jax import lax
from jax.experimental import pallas as pl
from jax.experimental.pallas import tpu as pltpu
from jax.sharding import PartitionSpec as P


ROWS = 128
HALF = 64
PAIR = 128
WIDTH = 1024
CHUNKS = 2
PIECE = WIDTH // CHUNKS
SCORE = 0.125 * math.log2(math.e)
BF16 = jnp.bfloat16
F32 = jnp.float32


def split_heads(query):
    lane = lax.broadcasted_iota(jnp.int32, (ROWS, PAIR), 1)
    query = query.astype(F32)
    zero = jnp.zeros_like(query)
    return jnp.concatenate(
        [jnp.where(lane < HALF, query, zero), jnp.where(lane < HALF, zero, query)], axis=0
    ).astype(BF16)


def pair_part(both, key, value):
    scores = lax.dot_general(key, both, (((1,), (1,)), ((), ())), preferred_element_type=F32)
    top = jnp.max(scores, axis=0, keepdims=True)
    expo = jnp.exp2((scores - top) * SCORE)
    accum = jnp.dot(value, expo.astype(BF16), preferred_element_type=F32)
    return top, jnp.sum(expo, axis=0, keepdims=True), accum[:HALF, :ROWS], accum[HALF:, ROWS:]


def merge_parts(parts):
    top = functools.reduce(jnp.maximum, [part[0] for part in parts])
    scales = [jnp.exp2((part[0] - top) * SCORE) for part in parts]
    return (
        top,
        sum(scale * part[1] for scale, part in zip(scales, parts)),
        sum(scale[:, :ROWS] * part[2] for scale, part in zip(scales, parts)),
        sum(scale[:, ROWS:] * part[3] for scale, part in zip(scales, parts)),
    )


def finish(part):
    _, total, first, second = part
    result = jnp.concatenate([first / total[:, :ROWS], second / total[:, ROWS:]], axis=0)
    return result.T.astype(BF16)


def kernel(
    count,
    ref_a,
    val_a,
    ref_b,
    val_b,
    w_a,
    w_b,
    out,
    staged,
    held,
    turned,
    weights,
    stats,
    sums,
    attn,
    gathered,
    outgoing,
    incoming,
    own,
    here_sem,
    near_sem,
    weight_sem,
    stage_sem,
    share_send,
    share_recv,
    band_send,
    band_recv,
    attn_send,
    attn_recv,
    part_send,
    part_recv,
):
    blk, head = lax.axis_index("blk"), lax.axis_index("head")
    place = lax.rem(blk, 4)
    base = blk - place
    other = 1 - head
    following = lax.rem(blk + 4, count)
    previous = lax.rem(blk + count - 4, count)
    swapped = lax.rem(place, 2) * 2 + place // 2

    herald = (place == 1) & (head == 1)
    later = base > 0
    holds_back = (place == 2) & (base + 4 == count)
    barrier = pltpu.get_barrier_semaphore()
    for p in (0, 2, 3):
        pl.semaphore_signal(barrier, inc=1, device_id={"blk": base + p, "head": other})

    @pl.when(head == 1)
    def _():
        pl.semaphore_signal(barrier, inc=1, device_id={"blk": base + 1, "head": other})

    loads = [
        pltpu.make_async_copy(w, weights.at[side], weight_sem.at[side])
        for side, w in enumerate((w_a, w_b))
    ]
    for side, pair in ((1, (ref_b, val_b)), (0, (ref_a, val_a))):
        for t in range(2):
            for p in range(4):
                pltpu.make_async_copy(
                    pair[t].at[:, pl.ds(p * PAIR, PAIR)], staged.at[side, t, p], stage_sem.at[side, t]
                ).start()
    for load in loads:
        load.start()

    @pl.when(jnp.logical_not(herald))
    def _():
        pl.semaphore_wait(barrier, 4)

    @pl.when(head == 0)
    def _():
        pl.semaphore_signal(here_sem, inc=1, device_id={"blk": base + 1, "head": other})

    @pl.when(herald)
    def _():
        pl.semaphore_wait(here_sem, 4)
        for near in (previous, following):
            pl.semaphore_signal(barrier, inc=1, device_id={"blk": near})


    def landed(ref, sem):
        pltpu.make_async_remote_copy(
            src_ref=ref, dst_ref=ref, send_sem=sem, recv_sem=sem, device_id={"head": other}
        ).wait_recv()

    def left(ref, sem):
        pltpu.make_async_remote_copy(
            src_ref=ref, dst_ref=ref, send_sem=sem, recv_sem=sem, device_id={"head": other}
        ).wait_send()

    def share(side, t, p):
        return pltpu.make_async_remote_copy(
            src_ref=staged.at[side, t, p],
            dst_ref=held.at[side, t, place + 1 + side],
            send_sem=share_send.at[side, t],
            recv_sem=share_recv.at[side, t, place],
            device_id={"blk": base + p, "head": other},
        )

    def shares(side, t):
        pltpu.make_async_copy(staged.at[side, t], staged.at[side, t], stage_sem.at[side, t]).wait()
        for p in range(4):
            share(side, t, p).start()

    shares(1, 0)
    shares(1, 1)
    for t in range(2):

        @pl.when(jnp.logical_not(herald))
        def _():
            left(staged.at[1, t], share_send.at[1, t])

        @pl.when(jnp.logical_not(holds_back))
        def _():
            shares(0, t)

    def tell():
        pl.semaphore_wait(barrier, 2)
        for p in range(4):
            pl.semaphore_signal(near_sem, inc=1, device_id={"blk": base + p, "head": other})
        for p in (0, 2, 3):
            pl.semaphore_signal(near_sem, inc=1, device_id={"blk": base + p})

    @pl.when(herald & later)
    def _():
        tell()

    def wait_share(side, t, blocks):
        for block in blocks:
            landed(held.at[side, t, block + 1 + side], share_recv.at[side, t, block])

    bands = ((1, 4, 0, 2, True), (1, 2, 6, 1, False), (0, 4, 0, 1, True), (0, 1, 5, 2, False))

    def band(index, t):
        side, first, target, blocks, forward = bands[index]
        return pltpu.make_async_remote_copy(
            src_ref=held.at[side, t, pl.ds(first, blocks)],
            dst_ref=held.at[side, t, pl.ds(target, blocks)],
            send_sem=band_send.at[t],
            recv_sem=band_recv.at[index, t],
            device_id={"blk": following if forward else previous},
        )

    def turn(side, first, blocks):
        for position in range(first, first + blocks):
            turned[side, position] = held[side, 1, position].T

    def pass_on(t, *indices):
        for index in indices:
            side, first, _, blocks, _ = bands[index]
            wait_share(side, t, range(first - 1 - side, first - 1 - side + blocks))
            band(index, t).start()

    def wait_word():
        @pl.when(jnp.logical_not(herald))
        def _():
            pl.semaphore_wait(near_sem, 1)

    def wait_band(index):
        for t in range(2):
            band(index, t).wait_recv()

    def attn_copies(side, n):
        if n in (0, 3):
            pieces = ((n, pl.ds(0, ROWS)),)
        else:
            pieces = (
                (n, pl.ds(pl.multiple_of(other * HALF, HALF), HALF)),
                (3 - n, pl.ds(pl.multiple_of(head * HALF, HALF), HALF)),
            )
        return [
            pltpu.make_async_remote_copy(
                src_ref=attn.at[side, n, rows],
                dst_ref=gathered.at[side, place, rows],
                send_sem=attn_send.at[side],
                recv_sem=attn_recv.at[side],
                device_id={"blk": base + target, "head": other},
            )
            for target, rows in pieces
        ]

    def pairs(side, n, positions):
        both = split_heads(held[side, 0, n + 1 + side])
        return [
            pair_part(both, held[1 - side, 0, position], turned[1 - side, position])
            for position in positions
        ]

    def ready(side, n, part):
        attn[side, n] = finish(part)

    def begin(side, n, positions):
        part = merge_parts(pairs(side, n, positions))
        if len(positions) == 4:
            ready(side, n, part)
        else:
            stats[side, n, 0:1], stats[side, n, 1:2] = part[0], part[1]
            sums[side, n, :HALF], sums[side, n, HALF:] = part[2], part[3]

    def complete(side, n, positions):
        state = (
            stats[side, n, 0:1],
            stats[side, n, 1:2],
            sums[side, n, :HALF],
            sums[side, n, HALF:],
        )
        ready(side, n, merge_parts([state] + pairs(side, n, positions)))

    def give(*tasks):
        for side, n in tasks:
            for copy in attn_copies(side, n):
                copy.start()

    @pl.when(later)
    def _():
        wait_word()
        pass_on(0, 0, 1)
        pass_on(1, 0, 1)
        pass_on(0, 2, 3)
        pass_on(1, 2, 3)

    @pl.when(holds_back)
    def _():
        for t in range(2):
            shares(0, t)

    @pl.when(jnp.logical_not(later))
    def _():
        for t in range(2):
            wait_share(1, t, (0, 2, 3))
            wait_share(0, t, (0, 1, 3))

    for t in range(2):
        wait_share(1, t, (1,))
        wait_share(0, t, (2,))
    turn(1, 2, 4)
    begin(0, 2, (2, 3, 4, 5))
    give((0, 2),)
    begin(0, 3, (3, 4, 5))
    begin(0, 1, (2, 3, 4))
    begin(0, 0, (2, 3))
    turn(0, 1, 4)
    begin(1, 1, (1, 2, 3, 4))
    give((1, 1),)
    begin(1, 2, (2, 3, 4))
    begin(1, 3, (3, 4))
    begin(1, 0, (1, 2, 3))

    @pl.when(jnp.logical_not(later))
    def _():
        @pl.when(herald)
        def _():
            tell()

        wait_word()
        for t in range(2):
            for index in range(4):
                band(index, t).start()

    wait_band(1)
    turn(1, 6, 1)
    complete(0, 3, (6,))
    wait_band(3)
    turn(0, 5, 2)
    complete(1, 2, (5,))
    complete(1, 3, (5, 6))
    give((0, 3), (1, 2), (1, 3))
    wait_band(0)
    turn(1, 0, 2)
    complete(0, 1, (1,))
    complete(0, 0, (0, 1))
    give((0, 1), (0, 0))
    wait_band(2)
    turn(0, 0, 1)
    complete(1, 0, (0,))
    give((1, 0),)

    mine = pl.ds(pl.multiple_of(head * HALF, HALF), HALF)
    theirs = pl.ds(pl.multiple_of(other * HALF, HALF), HALF)

    def part(side, chunk):
        return pltpu.make_async_remote_copy(
            src_ref=outgoing.at[side, chunk],
            dst_ref=incoming.at[side, chunk],
            send_sem=part_send.at[side],
            recv_sem=part_recv.at[side, chunk],
            device_id={"blk": base + swapped, "head": other},
        )

    for side in range(2):
        loads[side].wait()
        landed(gathered.at[side], attn_recv.at[side])
        rows = jnp.concatenate(
            [
                jnp.concatenate([gathered[side, p, half] for p in range(4)], axis=1)
                for half in (mine, theirs)
            ],
            axis=0,
        )
        for chunk in range(CHUNKS):
            product = jnp.dot(
                rows,
                weights[side, :, chunk * PIECE : (chunk + 1) * PIECE],
                preferred_element_type=F32,
            )
            outgoing[side, chunk] = product[HALF:].astype(BF16)
            part(side, chunk).start()
            own[side, chunk] = product[:HALF]

    @pl.when(herald)
    def _():
        for t in range(2):
            left(staged.at[1, t], share_send.at[1, t])

    for t in range(2):
        left(staged.at[0, t], share_send.at[0, t])
        left(held.at[0, 0, pl.ds(0, 6)], band_send.at[t])
    for side in range(2):
        left(attn.at[side], attn_send.at[side])
        left(outgoing.at[side], part_send.at[side])

    for side in range(2):
        for chunk in range(CHUNKS):
            part(side, chunk).wait_recv()
            out[side, :, chunk * PIECE : (chunk + 1) * PIECE] = (
                own[side, chunk] + incoming[side, chunk].astype(F32)
            ).astype(BF16)


def solution(mesh):
    count = mesh.shape["blk"]

    def shards(ref_a, val_a, ref_b, val_b, w_out_a, w_out_b):
        hbm = pl.BlockSpec(memory_space=pltpu.HBM)
        vmem = pl.BlockSpec(memory_space=pltpu.VMEM)
        out = pltpu.VMEM((2, HALF, WIDTH), BF16)
        results = pl.pallas_call(
            functools.partial(kernel, count),
            out_shape=out,
            in_specs=[hbm] * 6,
            out_specs=vmem,
            scratch_shapes=[
                pltpu.VMEM((2, 2, 4, ROWS, PAIR), BF16),
                pltpu.VMEM((2, 2, 7, ROWS, PAIR), BF16),
                pltpu.VMEM((2, 7, PAIR, ROWS), BF16),
                pltpu.VMEM((2, WIDTH // 2, WIDTH), BF16),
                pltpu.VMEM((2, 4, 8, 2 * ROWS), F32),
                pltpu.VMEM((2, 4, PAIR, ROWS), F32),
                pltpu.VMEM((2, 4, ROWS, PAIR), BF16),
                pltpu.VMEM((2, 4, ROWS, PAIR), BF16),
                pltpu.VMEM((2, CHUNKS, HALF, PIECE), BF16),
                pltpu.VMEM((2, CHUNKS, HALF, PIECE), BF16),
                pltpu.VMEM((2, CHUNKS, HALF, PIECE), F32),
                pltpu.SemaphoreType.REGULAR,
                pltpu.SemaphoreType.REGULAR,
                pltpu.SemaphoreType.DMA((2,)),
                pltpu.SemaphoreType.DMA((2, 2)),
                pltpu.SemaphoreType.DMA((2, 2)),
                pltpu.SemaphoreType.DMA((2, 2, 4)),
                pltpu.SemaphoreType.DMA((2,)),
                pltpu.SemaphoreType.DMA((4, 2)),
                pltpu.SemaphoreType.DMA((2,)),
                pltpu.SemaphoreType.DMA((2,)),
                pltpu.SemaphoreType.DMA((2,)),
                pltpu.SemaphoreType.DMA((2, CHUNKS)),
            ],
            compiler_params=pltpu.CompilerParams(
                collective_id=0, has_side_effects=True, vmem_limit_bytes=32 * 1024 * 1024
            ),
        )(
            *(
                pltpu.with_memory_space_constraint(array, pltpu.HBM)
                for array in (ref_a, val_a, ref_b, val_b, w_out_a, w_out_b)
            )
        )
        return results[0], results[1]

    return jax.shard_map(
        shards,
        mesh=mesh,
        in_specs=(
            P("blk", "head"),
            P("blk", "head"),
            P("blk", "head"),
            P("blk", "head"),
            P("head", None),
            P("head", None),
        ),
        out_specs=(P(("blk", "head"), None), P(("blk", "head"), None)),
        check_vma=False,
    )
```

```python
import functools
import math

import jax
import jax.numpy as jnp
from jax import lax
from jax.experimental import pallas as pl
from jax.experimental.pallas import tpu as pltpu
from jax.sharding import PartitionSpec as P


ROWS = 128
HALF = 64
PAIR = 128
WIDTH = 1024
CHUNKS = 2
PIECE = WIDTH // CHUNKS
SCORE = 0.125 * math.log2(math.e)
BF16 = jnp.bfloat16
F32 = jnp.float32


def split_heads(query):
    lane = lax.broadcasted_iota(jnp.int32, (ROWS, PAIR), 1)
    query = query.astype(F32)
    zero = jnp.zeros_like(query)
    return jnp.concatenate(
        [jnp.where(lane < HALF, query, zero), jnp.where(lane < HALF, zero, query)], axis=0
    ).astype(BF16)


def pair_part(both, key, value):
    scores = lax.dot_general(key, both, (((1,), (1,)), ((), ())), preferred_element_type=F32)
    top = jnp.max(scores, axis=0, keepdims=True)
    expo = jnp.exp2((scores - top) * SCORE)
    accum = jnp.dot(value, expo.astype(BF16), preferred_element_type=F32)
    return top, jnp.sum(expo, axis=0, keepdims=True), accum[:HALF, :ROWS], accum[HALF:, ROWS:]


def merge_parts(parts):
    top = functools.reduce(jnp.maximum, [part[0] for part in parts])
    scales = [jnp.exp2((part[0] - top) * SCORE) for part in parts]
    return (
        top,
        sum(scale * part[1] for scale, part in zip(scales, parts)),
        sum(scale[:, :ROWS] * part[2] for scale, part in zip(scales, parts)),
        sum(scale[:, ROWS:] * part[3] for scale, part in zip(scales, parts)),
    )


def finish(part):
    _, total, first, second = part
    result = jnp.concatenate([first / total[:, :ROWS], second / total[:, ROWS:]], axis=0)
    return result.T.astype(BF16)


def kernel(
    count,
    ref_a,
    val_a,
    ref_b,
    val_b,
    w_a,
    w_b,
    out,
    staged,
    held,
    turned,
    weights,
    stats,
    sums,
    attn,
    gathered,
    outgoing,
    incoming,
    own,
    here_sem,
    near_sem,
    weight_sem,
    stage_sem,
    share_send,
    share_recv,
    band_send,
    band_recv,
    attn_send,
    attn_recv,
    part_send,
    part_recv,
):
    blk, head = lax.axis_index("blk"), lax.axis_index("head")
    place = lax.rem(blk, 4)
    base = blk - place
    other = 1 - head
    following = lax.rem(blk + 4, count)
    previous = lax.rem(blk + count - 4, count)
    swapped = lax.rem(place, 2) * 2 + place // 2

    herald = (place == 1) & (head == 1)
    barrier = pltpu.get_barrier_semaphore()
    for p in (0, 2, 3):
        pl.semaphore_signal(barrier, inc=1, device_id={"blk": base + p, "head": other})

    @pl.when(head == 1)
    def _():
        pl.semaphore_signal(barrier, inc=1, device_id={"blk": base + 1, "head": other})

    loads = [
        pltpu.make_async_copy(w, weights.at[side], weight_sem.at[side])
        for side, w in enumerate((w_a, w_b))
    ]
    for t, source in enumerate((ref_a, val_a)):
        for p in range(4):
            pltpu.make_async_copy(
                source.at[:, pl.ds(p * PAIR, PAIR)], staged.at[t, p], stage_sem.at[t]
            ).start()
    for load in loads:
        load.start()

    @pl.when(jnp.logical_not(herald))
    def _():
        pl.semaphore_wait(barrier, 4)

    @pl.when(head == 0)
    def _():
        pl.semaphore_signal(here_sem, inc=1, device_id={"blk": base + 1, "head": other})

    @pl.when(herald)
    def _():
        pl.semaphore_wait(here_sem, 4)
        for near in (previous, following):
            pl.semaphore_signal(barrier, inc=1, device_id={"blk": near})


    def landed(ref, sem):
        pltpu.make_async_remote_copy(
            src_ref=ref, dst_ref=ref, send_sem=sem, recv_sem=sem, device_id={"head": other}
        ).wait_recv()

    def left(ref, sem):
        pltpu.make_async_remote_copy(
            src_ref=ref, dst_ref=ref, send_sem=sem, recv_sem=sem, device_id={"head": other}
        ).wait_send()

    def share(side, t, p):
        return pltpu.make_async_remote_copy(
            src_ref=(ref_b, val_b)[t].at[:, pl.ds(p * PAIR, PAIR)] if side else staged.at[t, p],
            dst_ref=held.at[side, t, place + 1 + side],
            send_sem=share_send.at[side, t],
            recv_sem=share_recv.at[side, t, place],
            device_id={"blk": base + p, "head": other},
        )

    def shares(side, t):
        for p in range(4):
            share(side, t, p).start()

    shares(1, 0)
    shares(1, 1)
    for t in range(2):

        @pl.when(jnp.logical_not(herald))
        def _():
            left(staged.at[t], share_send.at[1, t])

        pltpu.make_async_copy(staged.at[t], staged.at[t], stage_sem.at[t]).wait()
        shares(0, t)

    @pl.when(herald)
    def _():
        pl.semaphore_wait(barrier, 2)
        for p in range(4):
            pl.semaphore_signal(near_sem, inc=1, device_id={"blk": base + p, "head": other})
        for p in (0, 2, 3):
            pl.semaphore_signal(near_sem, inc=1, device_id={"blk": base + p})

    def wait_share(side, t, blocks):
        for block in blocks:
            landed(held.at[side, t, block + 1 + side], share_recv.at[side, t, block])

    bands = ((1, 4, 0, 2, True), (1, 2, 6, 1, False), (0, 4, 0, 1, True), (0, 1, 5, 2, False))

    def band(index, t):
        side, first, target, blocks, forward = bands[index]
        return pltpu.make_async_remote_copy(
            src_ref=held.at[side, t, pl.ds(first, blocks)],
            dst_ref=held.at[side, t, pl.ds(target, blocks)],
            send_sem=band_send.at[t],
            recv_sem=band_recv.at[index, t],
            device_id={"blk": following if forward else previous},
        )

    def turn(side, first, blocks):
        for position in range(first, first + blocks):
            turned[side, position] = held[side, 1, position].T

    def pass_on(t, *indices):
        for index in indices:
            side, first, _, blocks, _ = bands[index]
            wait_share(side, t, range(first - 1 - side, first - 1 - side + blocks))
            band(index, t).start()

    def wait_band(index):
        for t in range(2):
            band(index, t).wait_recv()

    def attn_copies(side, n):
        if n in (0, 3):
            pieces = ((n, pl.ds(0, ROWS)),)
        else:
            pieces = (
                (n, pl.ds(pl.multiple_of(other * HALF, HALF), HALF)),
                (3 - n, pl.ds(pl.multiple_of(head * HALF, HALF), HALF)),
            )
        return [
            pltpu.make_async_remote_copy(
                src_ref=attn.at[side, n, rows],
                dst_ref=gathered.at[side, place, rows],
                send_sem=attn_send.at[side],
                recv_sem=attn_recv.at[side],
                device_id={"blk": base + target, "head": other},
            )
            for target, rows in pieces
        ]

    def pairs(side, n, positions):
        both = split_heads(held[side, 0, n + 1 + side])
        return [
            pair_part(both, held[1 - side, 0, position], turned[1 - side, position])
            for position in positions
        ]

    def ready(side, n, part):
        attn[side, n] = finish(part)

    def begin(side, n, positions):
        part = merge_parts(pairs(side, n, positions))
        if len(positions) == 4:
            ready(side, n, part)
        else:
            stats[side, n, 0:1], stats[side, n, 1:2] = part[0], part[1]
            sums[side, n, :HALF], sums[side, n, HALF:] = part[2], part[3]

    def complete(side, n, positions):
        state = (
            stats[side, n, 0:1],
            stats[side, n, 1:2],
            sums[side, n, :HALF],
            sums[side, n, HALF:],
        )
        ready(side, n, merge_parts([state] + pairs(side, n, positions)))

    def give(*tasks):
        for side, n in tasks:
            for copy in attn_copies(side, n):
                copy.start()

    @pl.when(jnp.logical_not(herald))
    def _():
        pl.semaphore_wait(near_sem, 1)

    pass_on(0, 0, 1)
    pass_on(1, 0, 1)
    for t in range(2):
        wait_share(1, t, (1,))
    turn(1, 2, 4)
    pass_on(0, 2, 3)
    pass_on(1, 2, 3)
    for t in range(2):
        wait_share(0, t, (2,))
    begin(0, 2, (2, 3, 4, 5))
    give((0, 2),)
    begin(0, 3, (3, 4, 5))
    begin(0, 1, (2, 3, 4))
    begin(0, 0, (2, 3))
    turn(0, 1, 4)
    begin(1, 1, (1, 2, 3, 4))
    give((1, 1),)
    begin(1, 2, (2, 3, 4))
    begin(1, 3, (3, 4))
    begin(1, 0, (1, 2, 3))
    wait_band(1)
    turn(1, 6, 1)
    complete(0, 3, (6,))
    give((0, 3),)
    wait_band(0)
    turn(1, 0, 2)
    complete(0, 1, (1,))
    complete(0, 0, (0, 1))
    give((0, 1), (0, 0))
    wait_band(3)
    turn(0, 5, 2)
    complete(1, 2, (5,))
    complete(1, 3, (5, 6))
    give((1, 2), (1, 3))
    wait_band(2)
    turn(0, 0, 1)
    complete(1, 0, (0,))
    give((1, 0),)

    mine = pl.ds(pl.multiple_of(head * HALF, HALF), HALF)
    theirs = pl.ds(pl.multiple_of(other * HALF, HALF), HALF)

    def part(side, chunk):
        return pltpu.make_async_remote_copy(
            src_ref=outgoing.at[side, chunk],
            dst_ref=incoming.at[side, chunk],
            send_sem=part_send.at[side],
            recv_sem=part_recv.at[side, chunk],
            device_id={"blk": base + swapped, "head": other},
        )

    for side in range(2):
        loads[side].wait()
        landed(gathered.at[side], attn_recv.at[side])
        rows = jnp.concatenate(
            [
                jnp.concatenate([gathered[side, p, half] for p in range(4)], axis=1)
                for half in (mine, theirs)
            ],
            axis=0,
        )
        for chunk in range(CHUNKS):
            product = jnp.dot(
                rows,
                weights[side, :, chunk * PIECE : (chunk + 1) * PIECE],
                preferred_element_type=F32,
            )
            outgoing[side, chunk] = product[HALF:].astype(BF16)
            part(side, chunk).start()
            own[side, chunk] = product[:HALF]

    @pl.when(herald)
    def _():
        for t in range(2):
            left(staged.at[t], share_send.at[1, t])

    for t in range(2):
        left(staged.at[t], share_send.at[0, t])
        left(held.at[0, 0, pl.ds(0, 6)], band_send.at[t])
    for side in range(2):
        left(attn.at[side], attn_send.at[side])
        left(outgoing.at[side], part_send.at[side])

    for side in range(2):
        for chunk in range(CHUNKS):
            part(side, chunk).wait_recv()
            out[side, :, chunk * PIECE : (chunk + 1) * PIECE] = (
                own[side, chunk] + incoming[side, chunk].astype(F32)
            ).astype(BF16)


def solution(mesh):
    count = mesh.shape["blk"]

    def shards(ref_a, val_a, ref_b, val_b, w_out_a, w_out_b):
        hbm = pl.BlockSpec(memory_space=pltpu.HBM)
        vmem = pl.BlockSpec(memory_space=pltpu.VMEM)
        out = pltpu.VMEM((2, HALF, WIDTH), BF16)
        results = pl.pallas_call(
            functools.partial(kernel, count),
            out_shape=out,
            in_specs=[hbm] * 6,
            out_specs=vmem,
            scratch_shapes=[
                pltpu.VMEM((2, 4, ROWS, PAIR), BF16),
                pltpu.VMEM((2, 2, 7, ROWS, PAIR), BF16),
                pltpu.VMEM((2, 7, PAIR, ROWS), BF16),
                pltpu.VMEM((2, WIDTH // 2, WIDTH), BF16),
                pltpu.VMEM((2, 4, 8, 2 * ROWS), F32),
                pltpu.VMEM((2, 4, PAIR, ROWS), F32),
                pltpu.VMEM((2, 4, ROWS, PAIR), BF16),
                pltpu.VMEM((2, 4, ROWS, PAIR), BF16),
                pltpu.VMEM((2, CHUNKS, HALF, PIECE), BF16),
                pltpu.VMEM((2, CHUNKS, HALF, PIECE), BF16),
                pltpu.VMEM((2, CHUNKS, HALF, PIECE), F32),
                pltpu.SemaphoreType.REGULAR,
                pltpu.SemaphoreType.REGULAR,
                pltpu.SemaphoreType.DMA((2,)),
                pltpu.SemaphoreType.DMA((2,)),
                pltpu.SemaphoreType.DMA((2, 2)),
                pltpu.SemaphoreType.DMA((2, 2, 4)),
                pltpu.SemaphoreType.DMA((2,)),
                pltpu.SemaphoreType.DMA((4, 2)),
                pltpu.SemaphoreType.DMA((2,)),
                pltpu.SemaphoreType.DMA((2,)),
                pltpu.SemaphoreType.DMA((2,)),
                pltpu.SemaphoreType.DMA((2, CHUNKS)),
            ],
            compiler_params=pltpu.CompilerParams(
                collective_id=0, has_side_effects=True, vmem_limit_bytes=32 * 1024 * 1024
            ),
        )(
            *(
                pltpu.with_memory_space_constraint(array, pltpu.HBM)
                for array in (ref_a, val_a, ref_b, val_b, w_out_a, w_out_b)
            )
        )
        return results[0], results[1]

    return jax.shard_map(
        shards,
        mesh=mesh,
        in_specs=(
            P("blk", "head"),
            P("blk", "head"),
            P("blk", "head"),
            P("blk", "head"),
            P("head", None),
            P("head", None),
        ),
        out_specs=(P(("blk", "head"), None), P(("blk", "head"), None)),
        check_vma=False,
    )
```

```python
import functools
import math

import jax
import jax.numpy as jnp
from jax import lax
from jax.experimental import pallas as pl
from jax.experimental.pallas import tpu as pltpu
from jax.sharding import PartitionSpec as P


ROWS = 128
HALF = 64
QUARTER = 32
PAIR = 128
WIDTH = 1024
CHUNKS = 2
PIECE = WIDTH // CHUNKS
SCORE = 0.125 * math.log2(math.e)
BF16 = jnp.bfloat16
F32 = jnp.float32


def split_heads(query):
    lane = lax.broadcasted_iota(jnp.int32, (ROWS, PAIR), 1)
    query = query.astype(F32)
    zero = jnp.zeros_like(query)
    return jnp.concatenate(
        [jnp.where(lane < HALF, query, zero), jnp.where(lane < HALF, zero, query)], axis=0
    ).astype(BF16)


def pair_part(both, key, value):
    scores = lax.dot_general(key, both, (((1,), (1,)), ((), ())), preferred_element_type=F32)
    top = jnp.max(scores, axis=0, keepdims=True)
    expo = jnp.exp2((scores - top) * SCORE)
    accum = jnp.dot(value, expo.astype(BF16), preferred_element_type=F32)
    return top, jnp.sum(expo, axis=0, keepdims=True), accum[:HALF, :ROWS], accum[HALF:, ROWS:]


def merge_parts(parts):
    top = functools.reduce(jnp.maximum, [part[0] for part in parts])
    scales = [jnp.exp2((part[0] - top) * SCORE) for part in parts]
    return (
        top,
        sum(scale * part[1] for scale, part in zip(scales, parts)),
        sum(scale[:, :ROWS] * part[2] for scale, part in zip(scales, parts)),
        sum(scale[:, ROWS:] * part[3] for scale, part in zip(scales, parts)),
    )


def finish(part):
    _, total, first, second = part
    result = jnp.concatenate([first / total[:, :ROWS], second / total[:, ROWS:]], axis=0)
    return result.T.astype(BF16)


def kernel(
    count,
    ref_a,
    val_a,
    ref_b,
    val_b,
    w_a,
    w_b,
    out,
    staged,
    held,
    turned,
    weights,
    stats,
    sums,
    attn,
    gathered,
    outgoing,
    incoming,
    own,
    here_sem,
    near_sem,
    weight_sem,
    stage_sem,
    share_send,
    share_recv,
    band_send,
    band_recv,
    attn_send,
    attn_recv,
    part_send,
    part_recv,
):
    blk, head = lax.axis_index("blk"), lax.axis_index("head")
    place = lax.rem(blk, 4)
    base = blk - place
    other = 1 - head
    following = lax.rem(blk + 4, count)
    previous = lax.rem(blk + count - 4, count)

    herald = (place == 1) & (head == 1)
    barrier = pltpu.get_barrier_semaphore()
    for p in (0, 2, 3):
        pl.semaphore_signal(barrier, inc=1, device_id={"blk": base + p, "head": other})

    @pl.when(head == 1)
    def _():
        pl.semaphore_signal(barrier, inc=1, device_id={"blk": base + 1, "head": other})

    loads = [
        pltpu.make_async_copy(w, weights.at[side], weight_sem.at[side])
        for side, w in enumerate((w_a, w_b))
    ]
    for side, pair in ((1, (ref_b, val_b)), (0, (ref_a, val_a))):
        for t in range(2):
            for p in range(4):
                pltpu.make_async_copy(
                    pair[t].at[:, pl.ds(p * PAIR, PAIR)], staged.at[side, t, p], stage_sem.at[side, t]
                ).start()
    for load in loads:
        load.start()

    @pl.when(jnp.logical_not(herald))
    def _():
        pl.semaphore_wait(barrier, 4)

    @pl.when(head == 0)
    def _():
        pl.semaphore_signal(here_sem, inc=1, device_id={"blk": base + 1, "head": other})

    @pl.when(herald)
    def _():
        pl.semaphore_wait(here_sem, 4)
        for near in (previous, following):
            pl.semaphore_signal(barrier, inc=1, device_id={"blk": near})


    def landed(ref, sem):
        pltpu.make_async_remote_copy(
            src_ref=ref, dst_ref=ref, send_sem=sem, recv_sem=sem, device_id={"head": other}
        ).wait_recv()

    def left(ref, sem):
        pltpu.make_async_remote_copy(
            src_ref=ref, dst_ref=ref, send_sem=sem, recv_sem=sem, device_id={"head": other}
        ).wait_send()

    def share(side, t, p):
        return pltpu.make_async_remote_copy(
            src_ref=staged.at[side, t, p],
            dst_ref=held.at[side, t, place + 1 + side],
            send_sem=share_send.at[side, t],
            recv_sem=share_recv.at[side, t, place],
            device_id={"blk": base + p, "head": other},
        )

    def shares(side, t):
        pltpu.make_async_copy(staged.at[side, t], staged.at[side, t], stage_sem.at[side, t]).wait()
        for p in range(4):
            share(side, t, p).start()

    shares(1, 0)
    shares(1, 1)
    for t in range(2):

        @pl.when(jnp.logical_not(herald))
        def _():
            left(staged.at[1, t], share_send.at[1, t])

        shares(0, t)

    @pl.when(herald)
    def _():
        pl.semaphore_wait(barrier, 2)
        for p in range(4):
            pl.semaphore_signal(near_sem, inc=1, device_id={"blk": base + p, "head": other})
        for p in (0, 2, 3):
            pl.semaphore_signal(near_sem, inc=1, device_id={"blk": base + p})

    def wait_share(side, t, blocks):
        for block in blocks:
            landed(held.at[side, t, block + 1 + side], share_recv.at[side, t, block])

    bands = ((1, 4, 0, 2, True), (1, 2, 6, 1, False), (0, 4, 0, 1, True), (0, 1, 5, 2, False))

    def band(index, t):
        side, first, target, blocks, forward = bands[index]
        return pltpu.make_async_remote_copy(
            src_ref=held.at[side, t, pl.ds(first, blocks)],
            dst_ref=held.at[side, t, pl.ds(target, blocks)],
            send_sem=band_send.at[t],
            recv_sem=band_recv.at[index, t],
            device_id={"blk": following if forward else previous},
        )

    def turn(side, first, blocks):
        for position in range(first, first + blocks):
            turned[side, position] = held[side, 1, position].T

    def pass_on(t, *indices):
        for index in indices:
            side, first, _, blocks, _ = bands[index]
            wait_share(side, t, range(first - 1 - side, first - 1 - side + blocks))
            band(index, t).start()

    def wait_band(index):
        for t in range(2):
            band(index, t).wait_recv()

    def attn_copies(side, n):
        start, last = divmod(n, 2)
        pieces = [(n, other * HALF, 0, HALF)] + [
            (2 * part + last, head * HALF + part * QUARTER, HALF + start * QUARTER, QUARTER)
            for part in range(2)
        ]
        return [
            pltpu.make_async_remote_copy(
                src_ref=attn.at[side, n, pl.ds(pl.multiple_of(first, QUARTER), rows)],
                dst_ref=gathered.at[side, place, pl.ds(target, rows)],
                send_sem=attn_send.at[side],
                recv_sem=attn_recv.at[side],
                device_id={"blk": base + owner, "head": other},
            )
            for owner, first, target, rows in pieces
        ]

    def pairs(side, n, positions):
        both = split_heads(held[side, 0, n + 1 + side])
        return [
            pair_part(both, held[1 - side, 0, position], turned[1 - side, position])
            for position in positions
        ]

    def ready(side, n, part):
        attn[side, n] = finish(part)

    def begin(side, n, positions):
        part = merge_parts(pairs(side, n, positions))
        if len(positions) == 4:
            ready(side, n, part)
        else:
            stats[side, n, 0:1], stats[side, n, 1:2] = part[0], part[1]
            sums[side, n, :HALF], sums[side, n, HALF:] = part[2], part[3]

    def complete(side, n, positions):
        state = (
            stats[side, n, 0:1],
            stats[side, n, 1:2],
            sums[side, n, :HALF],
            sums[side, n, HALF:],
        )
        ready(side, n, merge_parts([state] + pairs(side, n, positions)))

    def give(*tasks):
        for side, n in tasks:
            for copy in attn_copies(side, n):
                copy.start()

    @pl.when(jnp.logical_not(herald))
    def _():
        pl.semaphore_wait(near_sem, 1)

    pass_on(0, 0, 1)
    pass_on(1, 0, 1)
    for t in range(2):
        wait_share(1, t, (1,))
    turn(1, 2, 4)
    pass_on(0, 2, 3)
    pass_on(1, 2, 3)
    for t in range(2):
        wait_share(0, t, (2,))
    begin(0, 2, (2, 3, 4, 5))
    give((0, 2),)
    begin(0, 3, (3, 4, 5))
    begin(0, 1, (2, 3, 4))
    begin(0, 0, (2, 3))
    turn(0, 1, 4)
    begin(1, 1, (1, 2, 3, 4))
    give((1, 1),)
    begin(1, 2, (2, 3, 4))
    begin(1, 3, (3, 4))
    begin(1, 0, (1, 2, 3))
    wait_band(1)
    turn(1, 6, 1)
    complete(0, 3, (6,))
    give((0, 3),)
    wait_band(0)
    turn(1, 0, 2)
    complete(0, 1, (1,))
    complete(0, 0, (0, 1))
    give((0, 1), (0, 0))
    wait_band(3)
    turn(0, 5, 2)
    complete(1, 2, (5,))
    complete(1, 3, (5, 6))
    give((1, 2), (1, 3))
    wait_band(2)
    turn(0, 0, 1)
    complete(1, 0, (0,))
    give((1, 0),)

    start, last = place // 2, lax.rem(place, 2)

    def part(side, chunk, piece):
        return pltpu.make_async_remote_copy(
            src_ref=outgoing.at[side, chunk, pl.ds(piece * QUARTER, QUARTER)],
            dst_ref=incoming.at[
                side, chunk, pl.ds(pl.multiple_of(start * QUARTER, QUARTER), QUARTER)
            ],
            send_sem=part_send.at[side],
            recv_sem=part_recv.at[side, chunk],
            device_id={"blk": base + 2 * piece + last, "head": other},
        )

    for side in range(2):
        loads[side].wait()
        landed(gathered.at[side], attn_recv.at[side])
        rows = jnp.concatenate([gathered[side, p] for p in range(4)], axis=1)
        for chunk in range(CHUNKS):
            product = jnp.dot(
                rows,
                weights[side, :, chunk * PIECE : (chunk + 1) * PIECE],
                preferred_element_type=F32,
            )
            outgoing[side, chunk] = product[HALF:].astype(BF16)
            for piece in range(2):
                part(side, chunk, piece).start()
            own[side, chunk] = product[:HALF]

    @pl.when(herald)
    def _():
        for t in range(2):
            left(staged.at[1, t], share_send.at[1, t])

    for t in range(2):
        left(staged.at[0, t], share_send.at[0, t])
        left(held.at[0, 0, pl.ds(0, 6)], band_send.at[t])
    for side in range(2):
        left(attn.at[side], attn_send.at[side])
        left(outgoing.at[side], part_send.at[side])

    for side in range(2):
        for chunk in range(CHUNKS):
            landed(incoming.at[side, chunk], part_recv.at[side, chunk])
            out[side, :, chunk * PIECE : (chunk + 1) * PIECE] = (
                own[side, chunk] + incoming[side, chunk].astype(F32)
            ).astype(BF16)


def solution(mesh):
    count = mesh.shape["blk"]

    def shards(ref_a, val_a, ref_b, val_b, w_out_a, w_out_b):
        hbm = pl.BlockSpec(memory_space=pltpu.HBM)
        vmem = pl.BlockSpec(memory_space=pltpu.VMEM)
        out = pltpu.VMEM((2, HALF, WIDTH), BF16)
        results = pl.pallas_call(
            functools.partial(kernel, count),
            out_shape=out,
            in_specs=[hbm] * 6,
            out_specs=vmem,
            scratch_shapes=[
                pltpu.VMEM((2, 2, 4, ROWS, PAIR), BF16),
                pltpu.VMEM((2, 2, 7, ROWS, PAIR), BF16),
                pltpu.VMEM((2, 7, PAIR, ROWS), BF16),
                pltpu.VMEM((2, WIDTH // 2, WIDTH), BF16),
                pltpu.VMEM((2, 4, 8, 2 * ROWS), F32),
                pltpu.VMEM((2, 4, PAIR, ROWS), F32),
                pltpu.VMEM((2, 4, ROWS, PAIR), BF16),
                pltpu.VMEM((2, 4, ROWS, PAIR), BF16),
                pltpu.VMEM((2, CHUNKS, HALF, PIECE), BF16),
                pltpu.VMEM((2, CHUNKS, HALF, PIECE), BF16),
                pltpu.VMEM((2, CHUNKS, HALF, PIECE), F32),
                pltpu.SemaphoreType.REGULAR,
                pltpu.SemaphoreType.REGULAR,
                pltpu.SemaphoreType.DMA((2,)),
                pltpu.SemaphoreType.DMA((2, 2)),
                pltpu.SemaphoreType.DMA((2, 2)),
                pltpu.SemaphoreType.DMA((2, 2, 4)),
                pltpu.SemaphoreType.DMA((2,)),
                pltpu.SemaphoreType.DMA((4, 2)),
                pltpu.SemaphoreType.DMA((2,)),
                pltpu.SemaphoreType.DMA((2,)),
                pltpu.SemaphoreType.DMA((2,)),
                pltpu.SemaphoreType.DMA((2, CHUNKS)),
            ],
            compiler_params=pltpu.CompilerParams(
                collective_id=0, has_side_effects=True, vmem_limit_bytes=32 * 1024 * 1024
            ),
        )(
            *(
                pltpu.with_memory_space_constraint(array, pltpu.HBM)
                for array in (ref_a, val_a, ref_b, val_b, w_out_a, w_out_b)
            )
        )
        return results[0], results[1]

    return jax.shard_map(
        shards,
        mesh=mesh,
        in_specs=(
            P("blk", "head"),
            P("blk", "head"),
            P("blk", "head"),
            P("blk", "head"),
            P("head", None),
            P("head", None),
        ),
        out_specs=(P(("blk", "head"), None), P(("blk", "head"), None)),
        check_vma=False,
    )
```

```python
import functools
import math

import jax
import jax.numpy as jnp
from jax import lax
from jax.experimental import pallas as pl
from jax.experimental.pallas import tpu as pltpu
from jax.sharding import PartitionSpec as P


ROWS = 128
HALF = 64
QUARTER = 32
PAIR = 128
WIDTH = 1024
CHUNKS = 2
PIECE = WIDTH // CHUNKS
SCORE = 0.125 * math.log2(math.e)
BF16 = jnp.bfloat16
F32 = jnp.float32


def split_heads(query):
    lane = lax.broadcasted_iota(jnp.int32, (ROWS, PAIR), 1)
    query = query.astype(F32)
    zero = jnp.zeros_like(query)
    return jnp.concatenate(
        [jnp.where(lane < HALF, query, zero), jnp.where(lane < HALF, zero, query)], axis=0
    ).astype(BF16)


def pair_part(both, key, value):
    scores = lax.dot_general(key, both, (((1,), (1,)), ((), ())), preferred_element_type=F32)
    top = jnp.max(scores, axis=0, keepdims=True)
    expo = jnp.exp2((scores - top) * SCORE)
    accum = jnp.dot(value, expo.astype(BF16), preferred_element_type=F32)
    return top, jnp.sum(expo, axis=0, keepdims=True), accum[:HALF, :ROWS], accum[HALF:, ROWS:]


def merge_parts(parts):
    top = functools.reduce(jnp.maximum, [part[0] for part in parts])
    scales = [jnp.exp2((part[0] - top) * SCORE) for part in parts]
    return (
        top,
        sum(scale * part[1] for scale, part in zip(scales, parts)),
        sum(scale[:, :ROWS] * part[2] for scale, part in zip(scales, parts)),
        sum(scale[:, ROWS:] * part[3] for scale, part in zip(scales, parts)),
    )


def finish(part):
    _, total, first, second = part
    result = jnp.concatenate([first / total[:, :ROWS], second / total[:, ROWS:]], axis=0)
    return result.T.astype(BF16)


def kernel(
    count,
    ref_a,
    val_a,
    ref_b,
    val_b,
    w_a,
    w_b,
    out,
    staged,
    held,
    turned,
    weights,
    stats,
    sums,
    attn,
    gathered,
    outgoing,
    incoming,
    own,
    here_sem,
    near_sem,
    weight_sem,
    stage_sem,
    share_send,
    share_recv,
    band_send,
    band_recv,
    attn_send,
    attn_recv,
    part_send,
    part_recv,
):
    blk, head = lax.axis_index("blk"), lax.axis_index("head")
    place = lax.rem(blk, 4)
    base = blk - place
    other = 1 - head
    following = lax.rem(blk + 4, count)
    previous = lax.rem(blk + count - 4, count)

    herald = (place == 1) & (head == 1)
    barrier = pltpu.get_barrier_semaphore()
    for p in (0, 2, 3):
        pl.semaphore_signal(barrier, inc=1, device_id={"blk": base + p, "head": other})

    @pl.when(head == 1)
    def _():
        pl.semaphore_signal(barrier, inc=1, device_id={"blk": base + 1, "head": other})

    loads = [
        pltpu.make_async_copy(w, weights.at[side], weight_sem.at[side])
        for side, w in enumerate((w_a, w_b))
    ]
    for side, pair in ((1, (ref_b, val_b)), (0, (ref_a, val_a))):
        for t in range(2):
            for p in range(4):
                pltpu.make_async_copy(
                    pair[t].at[:, pl.ds(p * PAIR, PAIR)], staged.at[side, t, p], stage_sem.at[side, t]
                ).start()
    for load in loads:
        load.start()

    @pl.when(jnp.logical_not(herald))
    def _():
        pl.semaphore_wait(barrier, 4)

    @pl.when(head == 0)
    def _():
        pl.semaphore_signal(here_sem, inc=1, device_id={"blk": base + 1, "head": other})

    @pl.when(herald)
    def _():
        pl.semaphore_wait(here_sem, 4)
        for near in (previous, following):
            pl.semaphore_signal(barrier, inc=1, device_id={"blk": near})


    def landed(ref, sem):
        pltpu.make_async_remote_copy(
            src_ref=ref, dst_ref=ref, send_sem=sem, recv_sem=sem, device_id={"head": other}
        ).wait_recv()

    def left(ref, sem):
        pltpu.make_async_remote_copy(
            src_ref=ref, dst_ref=ref, send_sem=sem, recv_sem=sem, device_id={"head": other}
        ).wait_send()

    def share(side, t, p):
        return pltpu.make_async_remote_copy(
            src_ref=staged.at[side, t, p],
            dst_ref=held.at[side, t, place + 1 + side],
            send_sem=share_send.at[side, t],
            recv_sem=share_recv.at[side, t, place],
            device_id={"blk": base + p, "head": other},
        )

    def shares(side, t):
        pltpu.make_async_copy(staged.at[side, t], staged.at[side, t], stage_sem.at[side, t]).wait()
        for p in range(4):
            share(side, t, p).start()

    shares(1, 0)
    shares(1, 1)
    for t in range(2):

        @pl.when(jnp.logical_not(herald))
        def _():
            left(staged.at[1, t], share_send.at[1, t])

        shares(0, t)

    @pl.when(herald)
    def _():
        pl.semaphore_wait(barrier, 2)
        for p in range(4):
            pl.semaphore_signal(near_sem, inc=1, device_id={"blk": base + p, "head": other})
        for p in (0, 2, 3):
            pl.semaphore_signal(near_sem, inc=1, device_id={"blk": base + p})

    def wait_share(side, t, blocks):
        for block in blocks:
            landed(held.at[side, t, block + 1 + side], share_recv.at[side, t, block])

    bands = ((1, 4, 0, 2, True), (1, 2, 6, 1, False), (0, 4, 0, 1, True), (0, 1, 5, 2, False))

    def band(index, t):
        side, first, target, blocks, forward = bands[index]
        return pltpu.make_async_remote_copy(
            src_ref=held.at[side, t, pl.ds(first, blocks)],
            dst_ref=held.at[side, t, pl.ds(target, blocks)],
            send_sem=band_send.at[t],
            recv_sem=band_recv.at[index, t],
            device_id={"blk": following if forward else previous},
        )

    def turn(side, first, blocks):
        for position in range(first, first + blocks):
            turned[side, position] = held[side, 1, position].T

    def pass_on(t, *indices):
        for index in indices:
            side, first, _, blocks, _ = bands[index]
            wait_share(side, t, range(first - 1 - side, first - 1 - side + blocks))
            band(index, t).start()

    def wait_band(index):
        for t in range(2):
            band(index, t).wait_recv()

    def attn_copies(side, n):
        start, last = divmod(n, 2)
        pieces = [(n, other * HALF, 0, HALF)] + [
            (2 * part + last, head * HALF + part * QUARTER, HALF + start * QUARTER, QUARTER)
            for part in range(2)
        ]
        return [
            pltpu.make_async_remote_copy(
                src_ref=attn.at[side, n, pl.ds(pl.multiple_of(first, QUARTER), rows)],
                dst_ref=gathered.at[side, place, pl.ds(target, rows)],
                send_sem=attn_send.at[side],
                recv_sem=attn_recv.at[side],
                device_id={"blk": base + owner, "head": other},
            )
            for owner, first, target, rows in pieces
        ]

    def pairs(side, n, positions):
        both = split_heads(held[side, 0, n + 1 + side])
        return [
            pair_part(both, held[1 - side, 0, position], turned[1 - side, position])
            for position in positions
        ]

    def ready(side, n, part):
        attn[side, n] = finish(part)

    def begin(side, n, positions):
        part = merge_parts(pairs(side, n, positions))
        if len(positions) == 4:
            ready(side, n, part)
        else:
            stats[side, n, 0:1], stats[side, n, 1:2] = part[0], part[1]
            sums[side, n, :HALF], sums[side, n, HALF:] = part[2], part[3]

    def complete(side, n, positions):
        state = (
            stats[side, n, 0:1],
            stats[side, n, 1:2],
            sums[side, n, :HALF],
            sums[side, n, HALF:],
        )
        ready(side, n, merge_parts([state] + pairs(side, n, positions)))

    def give(*tasks):
        for side, n in tasks:
            for copy in attn_copies(side, n):
                copy.start()

    @pl.when(jnp.logical_not(herald))
    def _():
        pl.semaphore_wait(near_sem, 1)

    pass_on(0, 0, 1)
    pass_on(1, 0, 1)
    for t in range(2):
        wait_share(1, t, (1,))
    turn(1, 2, 4)
    pass_on(0, 2, 3)
    pass_on(1, 2, 3)
    for t in range(2):
        wait_share(0, t, (2,))
    begin(0, 2, (2, 3, 4, 5))
    give((0, 2),)
    begin(0, 3, (3, 4, 5))
    begin(0, 1, (2, 3, 4))
    begin(0, 0, (2, 3))
    turn(0, 1, 4)
    begin(1, 1, (1, 2, 3, 4))
    give((1, 1),)
    begin(1, 2, (2, 3, 4))
    begin(1, 3, (3, 4))
    begin(1, 0, (1, 2, 3))
    start, last = place // 2, lax.rem(place, 2)

    def part(side, chunk, piece):
        return pltpu.make_async_remote_copy(
            src_ref=outgoing.at[side, chunk, pl.ds(piece * QUARTER, QUARTER)],
            dst_ref=incoming.at[
                side, chunk, pl.ds(pl.multiple_of(start * QUARTER, QUARTER), QUARTER)
            ],
            send_sem=part_send.at[side],
            recv_sem=part_recv.at[side, chunk],
            device_id={"blk": base + 2 * piece + last, "head": other},
        )

    def project(side):
        loads[side].wait()
        landed(gathered.at[side], attn_recv.at[side])
        rows = jnp.concatenate([gathered[side, p] for p in range(4)], axis=1)
        for chunk in range(CHUNKS):
            product = jnp.dot(
                rows,
                weights[side, :, chunk * PIECE : (chunk + 1) * PIECE],
                preferred_element_type=F32,
            )
            outgoing[side, chunk] = product[HALF:].astype(BF16)
            for piece in range(2):
                part(side, chunk, piece).start()
            own[side, chunk] = product[:HALF]

    wait_band(1)
    turn(1, 6, 1)
    complete(0, 3, (6,))
    wait_band(3)
    turn(0, 5, 2)
    complete(1, 2, (5,))
    complete(1, 3, (5, 6))
    give((0, 3), (1, 2), (1, 3))
    wait_band(0)
    turn(1, 1, 1)
    complete(0, 1, (1,))
    give((0, 1),)
    turn(1, 0, 1)
    complete(0, 0, (0, 1))
    give((0, 0),)

    @pl.when(last == 1)
    def _():
        project(1)

    wait_band(2)
    turn(0, 0, 1)
    complete(1, 0, (0,))
    give((1, 0),)
    project(0)

    @pl.when(last == 0)
    def _():
        project(1)

    @pl.when(herald)
    def _():
        for t in range(2):
            left(staged.at[1, t], share_send.at[1, t])

    for t in range(2):
        left(staged.at[0, t], share_send.at[0, t])
        left(held.at[0, 0, pl.ds(0, 6)], band_send.at[t])
    for side in range(2):
        left(attn.at[side], attn_send.at[side])
        left(outgoing.at[side], part_send.at[side])

    for side in range(2):
        for chunk in range(CHUNKS):
            landed(incoming.at[side, chunk], part_recv.at[side, chunk])
            out[side, :, chunk * PIECE : (chunk + 1) * PIECE] = (
                own[side, chunk] + incoming[side, chunk].astype(F32)
            ).astype(BF16)


def solution(mesh):
    count = mesh.shape["blk"]

    def shards(ref_a, val_a, ref_b, val_b, w_out_a, w_out_b):
        hbm = pl.BlockSpec(memory_space=pltpu.HBM)
        vmem = pl.BlockSpec(memory_space=pltpu.VMEM)
        out = pltpu.VMEM((2, HALF, WIDTH), BF16)
        results = pl.pallas_call(
            functools.partial(kernel, count),
            out_shape=out,
            in_specs=[hbm] * 6,
            out_specs=vmem,
            scratch_shapes=[
                pltpu.VMEM((2, 2, 4, ROWS, PAIR), BF16),
                pltpu.VMEM((2, 2, 7, ROWS, PAIR), BF16),
                pltpu.VMEM((2, 7, PAIR, ROWS), BF16),
                pltpu.VMEM((2, WIDTH // 2, WIDTH), BF16),
                pltpu.VMEM((2, 4, 8, 2 * ROWS), F32),
                pltpu.VMEM((2, 4, PAIR, ROWS), F32),
                pltpu.VMEM((2, 4, ROWS, PAIR), BF16),
                pltpu.VMEM((2, 4, ROWS, PAIR), BF16),
                pltpu.VMEM((2, CHUNKS, HALF, PIECE), BF16),
                pltpu.VMEM((2, CHUNKS, HALF, PIECE), BF16),
                pltpu.VMEM((2, CHUNKS, HALF, PIECE), F32),
                pltpu.SemaphoreType.REGULAR,
                pltpu.SemaphoreType.REGULAR,
                pltpu.SemaphoreType.DMA((2,)),
                pltpu.SemaphoreType.DMA((2, 2)),
                pltpu.SemaphoreType.DMA((2, 2)),
                pltpu.SemaphoreType.DMA((2, 2, 4)),
                pltpu.SemaphoreType.DMA((2,)),
                pltpu.SemaphoreType.DMA((4, 2)),
                pltpu.SemaphoreType.DMA((2,)),
                pltpu.SemaphoreType.DMA((2,)),
                pltpu.SemaphoreType.DMA((2,)),
                pltpu.SemaphoreType.DMA((2, CHUNKS)),
            ],
            compiler_params=pltpu.CompilerParams(
                collective_id=0, has_side_effects=True, vmem_limit_bytes=32 * 1024 * 1024
            ),
        )(
            *(
                pltpu.with_memory_space_constraint(array, pltpu.HBM)
                for array in (ref_a, val_a, ref_b, val_b, w_out_a, w_out_b)
            )
        )
        return results[0], results[1]

    return jax.shard_map(
        shards,
        mesh=mesh,
        in_specs=(
            P("blk", "head"),
            P("blk", "head"),
            P("blk", "head"),
            P("blk", "head"),
            P("head", None),
            P("head", None),
        ),
        out_specs=(P(("blk", "head"), None), P(("blk", "head"), None)),
        check_vma=False,
    )
```

```python
import functools
import math

import jax
import jax.numpy as jnp
from jax import lax
from jax.experimental import pallas as pl
from jax.experimental.pallas import tpu as pltpu
from jax.sharding import PartitionSpec as P


ROWS = 128
HALF = 64
QUARTER = 32
PAIR = 128
WIDTH = 1024
CHUNKS = 2
PIECE = WIDTH // CHUNKS
SCORE = 0.125 * math.log2(math.e)
BF16 = jnp.bfloat16
F32 = jnp.float32


def split_heads(query):
    lane = lax.broadcasted_iota(jnp.int32, (ROWS, PAIR), 1)
    query = query.astype(F32)
    zero = jnp.zeros_like(query)
    return jnp.concatenate(
        [jnp.where(lane < HALF, query, zero), jnp.where(lane < HALF, zero, query)], axis=0
    ).astype(BF16)


def pair_part(both, key, value):
    scores = lax.dot_general(key, both, (((1,), (1,)), ((), ())), preferred_element_type=F32)
    top = jnp.max(scores, axis=0, keepdims=True)
    expo = jnp.exp2((scores - top) * SCORE)
    accum = jnp.dot(value, expo.astype(BF16), preferred_element_type=F32)
    return top, jnp.sum(expo, axis=0, keepdims=True), accum[:HALF, :ROWS], accum[HALF:, ROWS:]


def merge_parts(parts):
    top = functools.reduce(jnp.maximum, [part[0] for part in parts])
    scales = [jnp.exp2((part[0] - top) * SCORE) for part in parts]
    return (
        top,
        sum(scale * part[1] for scale, part in zip(scales, parts)),
        sum(scale[:, :ROWS] * part[2] for scale, part in zip(scales, parts)),
        sum(scale[:, ROWS:] * part[3] for scale, part in zip(scales, parts)),
    )


def finish(part):
    _, total, first, second = part
    result = jnp.concatenate([first / total[:, :ROWS], second / total[:, ROWS:]], axis=0)
    return result.T.astype(BF16)


def kernel(
    count,
    ref_a,
    val_a,
    ref_b,
    val_b,
    w_a,
    w_b,
    out,
    staged,
    held,
    turned,
    weights,
    stats,
    sums,
    attn,
    gathered,
    outgoing,
    incoming,
    own,
    here_sem,
    after_sem,
    before_sem,
    weight_sem,
    stage_sem,
    share_send,
    share_recv,
    band_send,
    band_recv,
    attn_send,
    attn_recv,
    part_send,
    part_recv,
):
    blk, head = lax.axis_index("blk"), lax.axis_index("head")
    place = lax.rem(blk, 4)
    base = blk - place
    other = 1 - head
    following = lax.rem(blk + 4, count)
    previous = lax.rem(blk + count - 4, count)

    fore = (place == 1) & (head == 1)
    aft = (place == 0) & (head == 1)
    herald = (place < 2) & (head == 1)
    barrier = pltpu.get_barrier_semaphore()
    for p in (2, 3):
        pl.semaphore_signal(barrier, inc=1, device_id={"blk": base + p, "head": other})

    @pl.when(head == 1)
    def _():
        for p in (0, 1):
            pl.semaphore_signal(barrier, inc=1, device_id={"blk": base + p, "head": other})

    loads = [
        pltpu.make_async_copy(w, weights.at[side], weight_sem.at[side])
        for side, w in enumerate((w_a, w_b))
    ]
    for side, pair in ((1, (ref_b, val_b)), (0, (ref_a, val_a))):
        for t in range(2):
            for p in range(4):
                pltpu.make_async_copy(
                    pair[t].at[:, pl.ds(p * PAIR, PAIR)], staged.at[side, t, p], stage_sem.at[side, t]
                ).start()
    for load in loads:
        load.start()

    @pl.when(jnp.logical_not(herald))
    def _():
        pl.semaphore_wait(barrier, 4)

    @pl.when(head == 0)
    def _():
        for p in (0, 1):
            pl.semaphore_signal(here_sem, inc=1, device_id={"blk": base + p, "head": other})

    @pl.when(herald)
    def _():
        pl.semaphore_wait(here_sem, 4)

    @pl.when(fore)
    def _():
        pl.semaphore_signal(barrier, inc=1, device_id={"blk": following - 1})

    @pl.when(aft)
    def _():
        pl.semaphore_signal(barrier, inc=1, device_id={"blk": previous + 1})


    def landed(ref, sem):
        pltpu.make_async_remote_copy(
            src_ref=ref, dst_ref=ref, send_sem=sem, recv_sem=sem, device_id={"head": other}
        ).wait_recv()

    def left(ref, sem):
        pltpu.make_async_remote_copy(
            src_ref=ref, dst_ref=ref, send_sem=sem, recv_sem=sem, device_id={"head": other}
        ).wait_send()

    def share(side, t, p):
        return pltpu.make_async_remote_copy(
            src_ref=staged.at[side, t, p],
            dst_ref=held.at[side, t, place + 1 + side],
            send_sem=share_send.at[side, t],
            recv_sem=share_recv.at[side, t, place],
            device_id={"blk": base + p, "head": other},
        )

    def shares(side, t):
        pltpu.make_async_copy(staged.at[side, t], staged.at[side, t], stage_sem.at[side, t]).wait()
        for p in range(4):
            share(side, t, p).start()

    shares(1, 0)
    shares(1, 1)
    for t in range(2):

        @pl.when(jnp.logical_not(herald))
        def _():
            left(staged.at[1, t], share_send.at[1, t])

        shares(0, t)

    def tell(sem, places):
        pl.semaphore_wait(barrier, 1)
        for p in range(4):
            pl.semaphore_signal(sem, inc=1, device_id={"blk": base + p, "head": other})
        for p in places:
            pl.semaphore_signal(sem, inc=1, device_id={"blk": base + p})

    @pl.when(fore)
    def _():
        tell(after_sem, (0, 2, 3))

    @pl.when(aft)
    def _():
        tell(before_sem, (1, 2, 3))

    def wait_share(side, t, blocks):
        for block in blocks:
            landed(held.at[side, t, block + 1 + side], share_recv.at[side, t, block])

    bands = ((1, 4, 0, 2, True), (1, 2, 6, 1, False), (0, 4, 0, 1, True), (0, 1, 5, 2, False))

    def band(index, t):
        side, first, target, blocks, forward = bands[index]
        return pltpu.make_async_remote_copy(
            src_ref=held.at[side, t, pl.ds(first, blocks)],
            dst_ref=held.at[side, t, pl.ds(target, blocks)],
            send_sem=band_send.at[t],
            recv_sem=band_recv.at[index, t],
            device_id={"blk": following if forward else previous},
        )

    def turn(side, first, blocks):
        for position in range(first, first + blocks):
            turned[side, position] = held[side, 1, position].T

    def pass_on(t, *indices):
        for index in indices:
            side, first, _, blocks, _ = bands[index]
            wait_share(side, t, range(first - 1 - side, first - 1 - side + blocks))
            band(index, t).start()

    def wait_band(index):
        for t in range(2):
            band(index, t).wait_recv()

    def attn_copies(side, n):
        start, last = divmod(n, 2)
        pieces = [(n, other * HALF, 0, HALF)] + [
            (2 * part + last, head * HALF + part * QUARTER, HALF + start * QUARTER, QUARTER)
            for part in range(2)
        ]
        return [
            pltpu.make_async_remote_copy(
                src_ref=attn.at[side, n, pl.ds(pl.multiple_of(first, QUARTER), rows)],
                dst_ref=gathered.at[side, place, pl.ds(target, rows)],
                send_sem=attn_send.at[side],
                recv_sem=attn_recv.at[side],
                device_id={"blk": base + owner, "head": other},
            )
            for owner, first, target, rows in pieces
        ]

    def pairs(side, n, positions):
        both = split_heads(held[side, 0, n + 1 + side])
        return [
            pair_part(both, held[1 - side, 0, position], turned[1 - side, position])
            for position in positions
        ]

    def ready(side, n, part):
        attn[side, n] = finish(part)

    def begin(side, n, positions):
        part = merge_parts(pairs(side, n, positions))
        if len(positions) == 4:
            ready(side, n, part)
        else:
            stats[side, n, 0:1], stats[side, n, 1:2] = part[0], part[1]
            sums[side, n, :HALF], sums[side, n, HALF:] = part[2], part[3]

    def complete(side, n, positions):
        state = (
            stats[side, n, 0:1],
            stats[side, n, 1:2],
            sums[side, n, :HALF],
            sums[side, n, HALF:],
        )
        ready(side, n, merge_parts([state] + pairs(side, n, positions)))

    def give(*tasks):
        for side, n in tasks:
            for copy in attn_copies(side, n):
                copy.start()

    @pl.when(jnp.logical_not(fore))
    def _():
        pl.semaphore_wait(after_sem, 1)

    pass_on(0, 0)
    pass_on(1, 0)

    @pl.when(jnp.logical_not(aft))
    def _():
        pl.semaphore_wait(before_sem, 1)

    pass_on(0, 1)
    pass_on(1, 1)
    for t in range(2):
        wait_share(1, t, (1,))
    turn(1, 2, 4)
    pass_on(0, 2, 3)
    pass_on(1, 2, 3)
    for t in range(2):
        wait_share(0, t, (2,))
    begin(0, 2, (2, 3, 4, 5))
    give((0, 2),)
    begin(0, 3, (3, 4, 5))
    begin(0, 1, (2, 3, 4))
    begin(0, 0, (2, 3))
    turn(0, 1, 4)
    begin(1, 1, (1, 2, 3, 4))
    give((1, 1),)
    begin(1, 2, (2, 3, 4))
    begin(1, 3, (3, 4))
    begin(1, 0, (1, 2, 3))
    start, last = place // 2, lax.rem(place, 2)

    def part(side, chunk, piece):
        return pltpu.make_async_remote_copy(
            src_ref=outgoing.at[side, chunk, pl.ds(piece * QUARTER, QUARTER)],
            dst_ref=incoming.at[
                side, chunk, pl.ds(pl.multiple_of(start * QUARTER, QUARTER), QUARTER)
            ],
            send_sem=part_send.at[side],
            recv_sem=part_recv.at[side, chunk],
            device_id={"blk": base + 2 * piece + last, "head": other},
        )

    def project(side):
        loads[side].wait()
        landed(gathered.at[side], attn_recv.at[side])
        rows = jnp.concatenate([gathered[side, p] for p in range(4)], axis=1)
        for chunk in range(CHUNKS):
            product = jnp.dot(
                rows,
                weights[side, :, chunk * PIECE : (chunk + 1) * PIECE],
                preferred_element_type=F32,
            )
            outgoing[side, chunk] = product[HALF:].astype(BF16)
            for piece in range(2):
                part(side, chunk, piece).start()
            own[side, chunk] = product[:HALF]

    wait_band(1)
    turn(1, 6, 1)
    complete(0, 3, (6,))
    wait_band(3)
    turn(0, 5, 2)
    complete(1, 2, (5,))
    complete(1, 3, (5, 6))
    give((0, 3), (1, 2), (1, 3))
    wait_band(0)
    turn(1, 1, 1)
    complete(0, 1, (1,))
    give((0, 1),)
    turn(1, 0, 1)
    complete(0, 0, (0, 1))
    give((0, 0),)

    @pl.when(last == 1)
    def _():
        project(1)

    wait_band(2)
    turn(0, 0, 1)
    complete(1, 0, (0,))
    give((1, 0),)
    project(0)

    @pl.when(last == 0)
    def _():
        project(1)

    @pl.when(herald)
    def _():
        for t in range(2):
            left(staged.at[1, t], share_send.at[1, t])

    for t in range(2):
        left(staged.at[0, t], share_send.at[0, t])
        left(held.at[0, 0, pl.ds(0, 6)], band_send.at[t])
    for side in range(2):
        left(attn.at[side], attn_send.at[side])
        left(outgoing.at[side], part_send.at[side])

    for side in range(2):
        for chunk in range(CHUNKS):
            landed(incoming.at[side, chunk], part_recv.at[side, chunk])
            out[side, :, chunk * PIECE : (chunk + 1) * PIECE] = (
                own[side, chunk] + incoming[side, chunk].astype(F32)
            ).astype(BF16)


def solution(mesh):
    count = mesh.shape["blk"]

    def shards(ref_a, val_a, ref_b, val_b, w_out_a, w_out_b):
        hbm = pl.BlockSpec(memory_space=pltpu.HBM)
        vmem = pl.BlockSpec(memory_space=pltpu.VMEM)
        out = pltpu.VMEM((2, HALF, WIDTH), BF16)
        results = pl.pallas_call(
            functools.partial(kernel, count),
            out_shape=out,
            in_specs=[hbm] * 6,
            out_specs=vmem,
            scratch_shapes=[
                pltpu.VMEM((2, 2, 4, ROWS, PAIR), BF16),
                pltpu.VMEM((2, 2, 7, ROWS, PAIR), BF16),
                pltpu.VMEM((2, 7, PAIR, ROWS), BF16),
                pltpu.VMEM((2, WIDTH // 2, WIDTH), BF16),
                pltpu.VMEM((2, 4, 8, 2 * ROWS), F32),
                pltpu.VMEM((2, 4, PAIR, ROWS), F32),
                pltpu.VMEM((2, 4, ROWS, PAIR), BF16),
                pltpu.VMEM((2, 4, ROWS, PAIR), BF16),
                pltpu.VMEM((2, CHUNKS, HALF, PIECE), BF16),
                pltpu.VMEM((2, CHUNKS, HALF, PIECE), BF16),
                pltpu.VMEM((2, CHUNKS, HALF, PIECE), F32),
                pltpu.SemaphoreType.REGULAR,
                pltpu.SemaphoreType.REGULAR,
                pltpu.SemaphoreType.REGULAR,
                pltpu.SemaphoreType.DMA((2,)),
                pltpu.SemaphoreType.DMA((2, 2)),
                pltpu.SemaphoreType.DMA((2, 2)),
                pltpu.SemaphoreType.DMA((2, 2, 4)),
                pltpu.SemaphoreType.DMA((2,)),
                pltpu.SemaphoreType.DMA((4, 2)),
                pltpu.SemaphoreType.DMA((2,)),
                pltpu.SemaphoreType.DMA((2,)),
                pltpu.SemaphoreType.DMA((2,)),
                pltpu.SemaphoreType.DMA((2, CHUNKS)),
            ],
            compiler_params=pltpu.CompilerParams(
                collective_id=0, has_side_effects=True, vmem_limit_bytes=32 * 1024 * 1024
            ),
        )(
            *(
                pltpu.with_memory_space_constraint(array, pltpu.HBM)
                for array in (ref_a, val_a, ref_b, val_b, w_out_a, w_out_b)
            )
        )
        return results[0], results[1]

    return jax.shard_map(
        shards,
        mesh=mesh,
        in_specs=(
            P("blk", "head"),
            P("blk", "head"),
            P("blk", "head"),
            P("blk", "head"),
            P("head", None),
            P("head", None),
        ),
        out_specs=(P(("blk", "head"), None), P(("blk", "head"), None)),
        check_vma=False,
    )
```

```python
import functools
import math

import jax
import jax.numpy as jnp
from jax import lax
from jax.experimental import pallas as pl
from jax.experimental.pallas import tpu as pltpu
from jax.sharding import PartitionSpec as P


ROWS = 128
HALF = 64
QUARTER = 32
PAIR = 128
WIDTH = 1024
CHUNKS = 2
PIECE = WIDTH // CHUNKS
SCORE = 0.125 * math.log2(math.e)
BF16 = jnp.bfloat16
F32 = jnp.float32


def split_heads(query):
    lane = lax.broadcasted_iota(jnp.int32, (ROWS, PAIR), 1)
    query = query.astype(F32)
    zero = jnp.zeros_like(query)
    return jnp.concatenate(
        [jnp.where(lane < HALF, query, zero), jnp.where(lane < HALF, zero, query)], axis=0
    ).astype(BF16)


def pair_part(both, key, value):
    scores = lax.dot_general(key, both, (((1,), (1,)), ((), ())), preferred_element_type=F32)
    top = jnp.max(scores, axis=0, keepdims=True)
    expo = jnp.exp2((scores - top) * SCORE)
    accum = jnp.dot(value, expo.astype(BF16), preferred_element_type=F32)
    return top, jnp.sum(expo, axis=0, keepdims=True), accum[:HALF, :ROWS], accum[HALF:, ROWS:]


def merge_parts(parts):
    top = functools.reduce(jnp.maximum, [part[0] for part in parts])
    scales = [jnp.exp2((part[0] - top) * SCORE) for part in parts]
    return (
        top,
        sum(scale * part[1] for scale, part in zip(scales, parts)),
        sum(scale[:, :ROWS] * part[2] for scale, part in zip(scales, parts)),
        sum(scale[:, ROWS:] * part[3] for scale, part in zip(scales, parts)),
    )


def finish(part):
    _, total, first, second = part
    result = jnp.concatenate([first / total[:, :ROWS], second / total[:, ROWS:]], axis=0)
    return result.T.astype(BF16)


def kernel(
    count,
    ref_a,
    val_a,
    ref_b,
    val_b,
    w_a,
    w_b,
    out,
    staged,
    held,
    turned,
    weights,
    stats,
    sums,
    attn,
    gathered,
    outgoing,
    incoming,
    own,
    here_sem,
    near_sem,
    weight_sem,
    stage_sem,
    share_send,
    share_recv,
    band_send,
    band_recv,
    attn_send,
    attn_recv,
    part_send,
    part_recv,
):
    blk, head = lax.axis_index("blk"), lax.axis_index("head")
    place = lax.rem(blk, 4)
    base = blk - place
    other = 1 - head
    following = lax.rem(blk + 4, count)
    previous = lax.rem(blk + count - 4, count)

    herald = (place == 1) & (head == 1)
    holds_back = (place == 2) & (base + 4 == count)
    barrier = pltpu.get_barrier_semaphore()
    for p in (0, 2, 3):
        pl.semaphore_signal(barrier, inc=1, device_id={"blk": base + p, "head": other})

    @pl.when(head == 1)
    def _():
        pl.semaphore_signal(barrier, inc=1, device_id={"blk": base + 1, "head": other})

    loads = [
        pltpu.make_async_copy(w, weights.at[side], weight_sem.at[side])
        for side, w in enumerate((w_a, w_b))
    ]
    for side, pair in ((1, (ref_b, val_b)), (0, (ref_a, val_a))):
        for t in range(2):
            for p in range(4):
                pltpu.make_async_copy(
                    pair[t].at[:, pl.ds(p * PAIR, PAIR)], staged.at[side, t, p], stage_sem.at[side, t]
                ).start()
    for load in loads:
        load.start()

    @pl.when(jnp.logical_not(herald))
    def _():
        pl.semaphore_wait(barrier, 4)

    @pl.when(head == 0)
    def _():
        pl.semaphore_signal(here_sem, inc=1, device_id={"blk": base + 1, "head": other})

    @pl.when(herald)
    def _():
        pl.semaphore_wait(here_sem, 4)
        for near in (previous, following):
            pl.semaphore_signal(barrier, inc=1, device_id={"blk": near})


    def landed(ref, sem):
        pltpu.make_async_remote_copy(
            src_ref=ref, dst_ref=ref, send_sem=sem, recv_sem=sem, device_id={"head": other}
        ).wait_recv()

    def left(ref, sem):
        pltpu.make_async_remote_copy(
            src_ref=ref, dst_ref=ref, send_sem=sem, recv_sem=sem, device_id={"head": other}
        ).wait_send()

    def share(side, t, p):
        return pltpu.make_async_remote_copy(
            src_ref=staged.at[side, t, p],
            dst_ref=held.at[side, t, place + 1 + side],
            send_sem=share_send.at[side, t],
            recv_sem=share_recv.at[side, t, place],
            device_id={"blk": base + p, "head": other},
        )

    def shares(side, t):
        pltpu.make_async_copy(staged.at[side, t], staged.at[side, t], stage_sem.at[side, t]).wait()
        for p in range(4):
            share(side, t, p).start()

    shares(1, 0)
    shares(1, 1)
    for t in range(2):

        @pl.when(jnp.logical_not(herald))
        def _():
            left(staged.at[1, t], share_send.at[1, t])

        @pl.when(jnp.logical_not(holds_back))
        def _():
            shares(0, t)

    @pl.when(herald)
    def _():
        pl.semaphore_wait(barrier, 2)
        for p in range(4):
            pl.semaphore_signal(near_sem, inc=1, device_id={"blk": base + p, "head": other})
        for p in (0, 2, 3):
            pl.semaphore_signal(near_sem, inc=1, device_id={"blk": base + p})

    def wait_share(side, t, blocks):
        for block in blocks:
            landed(held.at[side, t, block + 1 + side], share_recv.at[side, t, block])

    bands = ((1, 4, 0, 2, True), (1, 2, 6, 1, False), (0, 4, 0, 1, True), (0, 1, 5, 2, False))

    def band(index, t):
        side, first, target, blocks, forward = bands[index]
        return pltpu.make_async_remote_copy(
            src_ref=held.at[side, t, pl.ds(first, blocks)],
            dst_ref=held.at[side, t, pl.ds(target, blocks)],
            send_sem=band_send.at[t],
            recv_sem=band_recv.at[index, t],
            device_id={"blk": following if forward else previous},
        )

    def turn(side, first, blocks):
        for position in range(first, first + blocks):
            turned[side, position] = held[side, 1, position].T

    def pass_on(t, *indices):
        for index in indices:
            side, first, _, blocks, _ = bands[index]
            wait_share(side, t, range(first - 1 - side, first - 1 - side + blocks))
            band(index, t).start()

    def wait_band(index):
        for t in range(2):
            band(index, t).wait_recv()

    def attn_copies(side, n):
        start, last = divmod(n, 2)
        pieces = [(n, other * HALF, 0, HALF)] + [
            (2 * part + last, head * HALF + part * QUARTER, HALF + start * QUARTER, QUARTER)
            for part in range(2)
        ]
        return [
            pltpu.make_async_remote_copy(
                src_ref=attn.at[side, n, pl.ds(pl.multiple_of(first, QUARTER), rows)],
                dst_ref=gathered.at[side, place, pl.ds(target, rows)],
                send_sem=attn_send.at[side],
                recv_sem=attn_recv.at[side],
                device_id={"blk": base + owner, "head": other},
            )
            for owner, first, target, rows in pieces
        ]

    def pairs(side, n, positions):
        both = split_heads(held[side, 0, n + 1 + side])
        return [
            pair_part(both, held[1 - side, 0, position], turned[1 - side, position])
            for position in positions
        ]

    def ready(side, n, part):
        attn[side, n] = finish(part)

    def begin(side, n, positions):
        part = merge_parts(pairs(side, n, positions))
        if len(positions) == 4:
            ready(side, n, part)
        else:
            stats[side, n, 0:1], stats[side, n, 1:2] = part[0], part[1]
            sums[side, n, :HALF], sums[side, n, HALF:] = part[2], part[3]

    def complete(side, n, positions):
        state = (
            stats[side, n, 0:1],
            stats[side, n, 1:2],
            sums[side, n, :HALF],
            sums[side, n, HALF:],
        )
        ready(side, n, merge_parts([state] + pairs(side, n, positions)))

    def give(*tasks):
        for side, n in tasks:
            for copy in attn_copies(side, n):
                copy.start()

    @pl.when(jnp.logical_not(herald))
    def _():
        pl.semaphore_wait(near_sem, 1)

    pass_on(0, 0, 1)
    pass_on(1, 0, 1)
    for t in range(2):
        wait_share(1, t, (1,))
    turn(1, 2, 4)
    pass_on(0, 2)

    @pl.when(holds_back)
    def _():
        for t in range(2):
            shares(0, t)

    pass_on(0, 3)
    pass_on(1, 2, 3)
    for t in range(2):
        wait_share(0, t, (2,))
    begin(0, 2, (2, 3, 4, 5))
    give((0, 2),)
    begin(0, 3, (3, 4, 5))
    begin(0, 1, (2, 3, 4))
    begin(0, 0, (2, 3))
    turn(0, 1, 4)
    begin(1, 1, (1, 2, 3, 4))
    give((1, 1),)
    begin(1, 2, (2, 3, 4))
    begin(1, 3, (3, 4))
    begin(1, 0, (1, 2, 3))
    start, last = place // 2, lax.rem(place, 2)

    def part(side, chunk, piece):
        return pltpu.make_async_remote_copy(
            src_ref=outgoing.at[side, chunk, pl.ds(piece * QUARTER, QUARTER)],
            dst_ref=incoming.at[
                side, chunk, pl.ds(pl.multiple_of(start * QUARTER, QUARTER), QUARTER)
            ],
            send_sem=part_send.at[side],
            recv_sem=part_recv.at[side, chunk],
            device_id={"blk": base + 2 * piece + last, "head": other},
        )

    def project(side):
        loads[side].wait()
        landed(gathered.at[side], attn_recv.at[side])
        rows = jnp.concatenate([gathered[side, p] for p in range(4)], axis=1)
        for chunk in range(CHUNKS):
            product = jnp.dot(
                rows,
                weights[side, :, chunk * PIECE : (chunk + 1) * PIECE],
                preferred_element_type=F32,
            )
            outgoing[side, chunk] = product[HALF:].astype(BF16)
            for piece in range(2):
                part(side, chunk, piece).start()
            own[side, chunk] = product[:HALF]

    wait_band(1)
    turn(1, 6, 1)
    complete(0, 3, (6,))
    wait_band(3)
    turn(0, 5, 2)
    complete(1, 2, (5,))
    complete(1, 3, (5, 6))
    give((0, 3), (1, 2), (1, 3))
    wait_band(0)
    turn(1, 1, 1)
    complete(0, 1, (1,))
    give((0, 1),)
    turn(1, 0, 1)
    complete(0, 0, (0, 1))
    give((0, 0),)

    @pl.when(last == 1)
    def _():
        project(1)
        project(0)

    wait_band(2)
    turn(0, 0, 1)
    complete(1, 0, (0,))
    give((1, 0),)

    @pl.when(last == 0)
    def _():
        project(0)
        project(1)

    @pl.when(herald)
    def _():
        for t in range(2):
            left(staged.at[1, t], share_send.at[1, t])

    for t in range(2):
        left(staged.at[0, t], share_send.at[0, t])
        left(held.at[0, 0, pl.ds(0, 6)], band_send.at[t])
    for side in range(2):
        left(attn.at[side], attn_send.at[side])
        left(outgoing.at[side], part_send.at[side])

    for side in range(2):
        for chunk in range(CHUNKS):
            landed(incoming.at[side, chunk], part_recv.at[side, chunk])
            out[side, :, chunk * PIECE : (chunk + 1) * PIECE] = (
                own[side, chunk] + incoming[side, chunk].astype(F32)
            ).astype(BF16)


def solution(mesh):
    count = mesh.shape["blk"]

    def shards(ref_a, val_a, ref_b, val_b, w_out_a, w_out_b):
        hbm = pl.BlockSpec(memory_space=pltpu.HBM)
        vmem = pl.BlockSpec(memory_space=pltpu.VMEM)
        out = pltpu.VMEM((2, HALF, WIDTH), BF16)
        results = pl.pallas_call(
            functools.partial(kernel, count),
            out_shape=out,
            in_specs=[hbm] * 6,
            out_specs=vmem,
            scratch_shapes=[
                pltpu.VMEM((2, 2, 4, ROWS, PAIR), BF16),
                pltpu.VMEM((2, 2, 7, ROWS, PAIR), BF16),
                pltpu.VMEM((2, 7, PAIR, ROWS), BF16),
                pltpu.VMEM((2, WIDTH // 2, WIDTH), BF16),
                pltpu.VMEM((2, 4, 8, 2 * ROWS), F32),
                pltpu.VMEM((2, 4, PAIR, ROWS), F32),
                pltpu.VMEM((2, 4, ROWS, PAIR), BF16),
                pltpu.VMEM((2, 4, ROWS, PAIR), BF16),
                pltpu.VMEM((2, CHUNKS, HALF, PIECE), BF16),
                pltpu.VMEM((2, CHUNKS, HALF, PIECE), BF16),
                pltpu.VMEM((2, CHUNKS, HALF, PIECE), F32),
                pltpu.SemaphoreType.REGULAR,
                pltpu.SemaphoreType.REGULAR,
                pltpu.SemaphoreType.DMA((2,)),
                pltpu.SemaphoreType.DMA((2, 2)),
                pltpu.SemaphoreType.DMA((2, 2)),
                pltpu.SemaphoreType.DMA((2, 2, 4)),
                pltpu.SemaphoreType.DMA((2,)),
                pltpu.SemaphoreType.DMA((4, 2)),
                pltpu.SemaphoreType.DMA((2,)),
                pltpu.SemaphoreType.DMA((2,)),
                pltpu.SemaphoreType.DMA((2,)),
                pltpu.SemaphoreType.DMA((2, CHUNKS)),
            ],
            compiler_params=pltpu.CompilerParams(
                collective_id=0, has_side_effects=True, vmem_limit_bytes=32 * 1024 * 1024
            ),
        )(
            *(
                pltpu.with_memory_space_constraint(array, pltpu.HBM)
                for array in (ref_a, val_a, ref_b, val_b, w_out_a, w_out_b)
            )
        )
        return results[0], results[1]

    return jax.shard_map(
        shards,
        mesh=mesh,
        in_specs=(
            P("blk", "head"),
            P("blk", "head"),
            P("blk", "head"),
            P("blk", "head"),
            P("head", None),
            P("head", None),
        ),
        out_specs=(P(("blk", "head"), None), P(("blk", "head"), None)),
        check_vma=False,
    )
```

```python
import functools
import math

import jax
import jax.numpy as jnp
from jax import lax
from jax.experimental import pallas as pl
from jax.experimental.pallas import tpu as pltpu
from jax.sharding import PartitionSpec as P


ROWS = 128
HALF = 64
QUARTER = 32
PAIR = 128
WIDTH = 1024
CHUNKS = 2
PIECE = WIDTH // CHUNKS
SCORE = 0.125 * math.log2(math.e)
BF16 = jnp.bfloat16
F32 = jnp.float32


def split_heads(query):
    lane = lax.broadcasted_iota(jnp.int32, (ROWS, PAIR), 1)
    query = query.astype(F32)
    zero = jnp.zeros_like(query)
    return jnp.concatenate(
        [jnp.where(lane < HALF, query, zero), jnp.where(lane < HALF, zero, query)], axis=0
    ).astype(BF16)


def pair_part(both, key, value):
    scores = lax.dot_general(key, both, (((1,), (1,)), ((), ())), preferred_element_type=F32)
    top = jnp.max(scores, axis=0, keepdims=True)
    expo = jnp.exp2((scores - top) * SCORE)
    accum = jnp.dot(value, expo.astype(BF16), preferred_element_type=F32)
    return top, jnp.sum(expo, axis=0, keepdims=True), accum[:HALF, :ROWS], accum[HALF:, ROWS:]


def merge_parts(parts):
    top = functools.reduce(jnp.maximum, [part[0] for part in parts])
    scales = [jnp.exp2((part[0] - top) * SCORE) for part in parts]
    return (
        top,
        sum(scale * part[1] for scale, part in zip(scales, parts)),
        sum(scale[:, :ROWS] * part[2] for scale, part in zip(scales, parts)),
        sum(scale[:, ROWS:] * part[3] for scale, part in zip(scales, parts)),
    )


def finish(part):
    _, total, first, second = part
    result = jnp.concatenate([first / total[:, :ROWS], second / total[:, ROWS:]], axis=0)
    return result.T.astype(BF16)


def kernel(
    count,
    ref_a,
    val_a,
    ref_b,
    val_b,
    w_a,
    w_b,
    out,
    staged,
    held,
    turned,
    weights,
    stats,
    sums,
    attn,
    gathered,
    outgoing,
    incoming,
    own,
    here_sem,
    near_sem,
    weight_sem,
    stage_sem,
    share_send,
    share_recv,
    band_send,
    band_recv,
    attn_send,
    attn_recv,
    part_send,
    part_recv,
):
    blk, head = lax.axis_index("blk"), lax.axis_index("head")
    place = lax.rem(blk, 4)
    base = blk - place
    other = 1 - head
    following = lax.rem(blk + 4, count)
    previous = lax.rem(blk + count - 4, count)

    herald = (place == 1) & (head == 1)
    holds_back = (place == 2) & (base + 4 == count)
    barrier = pltpu.get_barrier_semaphore()
    for p in (0, 2, 3):
        pl.semaphore_signal(barrier, inc=1, device_id={"blk": base + p, "head": other})

    @pl.when(head == 1)
    def _():
        pl.semaphore_signal(barrier, inc=1, device_id={"blk": base + 1, "head": other})

    loads = [
        pltpu.make_async_copy(w, weights.at[side], weight_sem.at[side])
        for side, w in enumerate((w_a, w_b))
    ]
    for side, pair in ((1, (ref_b, val_b)), (0, (ref_a, val_a))):
        for t in range(2):
            for p in range(4):
                pltpu.make_async_copy(
                    pair[t].at[:, pl.ds(p * PAIR, PAIR)], staged.at[side, t, p], stage_sem.at[side, t]
                ).start()
    for load in loads:
        load.start()

    @pl.when(jnp.logical_not(herald))
    def _():
        pl.semaphore_wait(barrier, 4)

    @pl.when(head == 0)
    def _():
        pl.semaphore_signal(here_sem, inc=1, device_id={"blk": base + 1, "head": other})

    @pl.when(herald)
    def _():
        pl.semaphore_wait(here_sem, 4)
        for near in (previous, following):
            pl.semaphore_signal(barrier, inc=1, device_id={"blk": near})


    def landed(ref, sem):
        pltpu.make_async_remote_copy(
            src_ref=ref, dst_ref=ref, send_sem=sem, recv_sem=sem, device_id={"head": other}
        ).wait_recv()

    def left(ref, sem):
        pltpu.make_async_remote_copy(
            src_ref=ref, dst_ref=ref, send_sem=sem, recv_sem=sem, device_id={"head": other}
        ).wait_send()

    def share(side, t, p):
        return pltpu.make_async_remote_copy(
            src_ref=staged.at[side, t, p],
            dst_ref=held.at[side, t, place + 1 + side],
            send_sem=share_send.at[side, t],
            recv_sem=share_recv.at[side, t, place],
            device_id={"blk": base + p, "head": other},
        )

    def shares(side, t):
        pltpu.make_async_copy(staged.at[side, t], staged.at[side, t], stage_sem.at[side, t]).wait()
        for p in range(4):
            share(side, t, p).start()

    shares(1, 0)
    shares(1, 1)
    for t in range(2):

        @pl.when(jnp.logical_not(herald))
        def _():
            left(staged.at[1, t], share_send.at[1, t])

        @pl.when(jnp.logical_not(holds_back))
        def _():
            shares(0, t)

    @pl.when(herald)
    def _():
        pl.semaphore_wait(barrier, 2)
        for p in range(4):
            pl.semaphore_signal(near_sem, inc=1, device_id={"blk": base + p, "head": other})
        for p in (0, 2, 3):
            pl.semaphore_signal(near_sem, inc=1, device_id={"blk": base + p})

    def wait_share(side, t, blocks):
        for block in blocks:
            landed(held.at[side, t, block + 1 + side], share_recv.at[side, t, block])

    bands = ((1, 4, 0, 2, True), (1, 2, 6, 1, False), (0, 4, 0, 1, True), (0, 1, 5, 2, False))

    def band(index, t):
        side, first, target, blocks, forward = bands[index]
        return pltpu.make_async_remote_copy(
            src_ref=held.at[side, t, pl.ds(first, blocks)],
            dst_ref=held.at[side, t, pl.ds(target, blocks)],
            send_sem=band_send.at[t],
            recv_sem=band_recv.at[index, t],
            device_id={"blk": following if forward else previous},
        )

    def turn(side, first, blocks):
        for position in range(first, first + blocks):
            turned[side, position] = held[side, 1, position].T

    def pass_on(t, *indices):
        for index in indices:
            side, first, _, blocks, _ = bands[index]
            wait_share(side, t, range(first - 1 - side, first - 1 - side + blocks))
            band(index, t).start()

    def wait_band(index):
        for t in range(2):
            band(index, t).wait_recv()

    def attn_copies(side, n):
        start, last = divmod(n, 2)
        pieces = [(n, other * HALF, 0, HALF)] + [
            (2 * part + last, head * HALF + part * QUARTER, HALF + start * QUARTER, QUARTER)
            for part in range(2)
        ]
        return [
            pltpu.make_async_remote_copy(
                src_ref=attn.at[side, n, pl.ds(pl.multiple_of(first, QUARTER), rows)],
                dst_ref=gathered.at[side, place, pl.ds(target, rows)],
                send_sem=attn_send.at[side],
                recv_sem=attn_recv.at[side],
                device_id={"blk": base + owner, "head": other},
            )
            for owner, first, target, rows in pieces
        ]

    def pairs(side, n, positions):
        both = split_heads(held[side, 0, n + 1 + side])
        return [
            pair_part(both, held[1 - side, 0, position], turned[1 - side, position])
            for position in positions
        ]

    def ready(side, n, part):
        attn[side, n] = finish(part)

    def begin(side, n, positions):
        part = merge_parts(pairs(side, n, positions))
        if len(positions) == 4:
            ready(side, n, part)
        else:
            stats[side, n, 0:1], stats[side, n, 1:2] = part[0], part[1]
            sums[side, n, :HALF], sums[side, n, HALF:] = part[2], part[3]

    def complete(side, n, positions):
        state = (
            stats[side, n, 0:1],
            stats[side, n, 1:2],
            sums[side, n, :HALF],
            sums[side, n, HALF:],
        )
        ready(side, n, merge_parts([state] + pairs(side, n, positions)))

    def give(*tasks):
        for side, n in tasks:
            for copy in attn_copies(side, n):
                copy.start()

    @pl.when(jnp.logical_not(herald))
    def _():
        pl.semaphore_wait(near_sem, 1)

    pass_on(0, 0, 1)
    pass_on(1, 0, 1)
    for t in range(2):
        wait_share(1, t, (1,))
    turn(1, 2, 4)
    pass_on(0, 2)

    @pl.when(holds_back)
    def _():
        for t in range(2):
            shares(0, t)

    pass_on(0, 3)
    pass_on(1, 2, 3)
    for t in range(2):
        wait_share(0, t, (2,))
    begin(0, 2, (2, 3, 4, 5))
    give((0, 2),)
    begin(0, 3, (3, 4, 5))
    begin(0, 1, (2, 3, 4))
    begin(0, 0, (2, 3))
    turn(0, 1, 4)
    begin(1, 1, (1, 2, 3, 4))
    give((1, 1),)
    begin(1, 2, (2, 3, 4))
    begin(1, 3, (3, 4))
    begin(1, 0, (1, 2, 3))
    start, last = place // 2, lax.rem(place, 2)

    def part(side, chunk, piece):
        return pltpu.make_async_remote_copy(
            src_ref=outgoing.at[side, chunk, pl.ds(piece * QUARTER, QUARTER)],
            dst_ref=incoming.at[
                side, chunk, pl.ds(pl.multiple_of(start * QUARTER, QUARTER), QUARTER)
            ],
            send_sem=part_send.at[side],
            recv_sem=part_recv.at[side, chunk],
            device_id={"blk": base + 2 * piece + last, "head": other},
        )

    def project(side):
        loads[side].wait()
        landed(gathered.at[side], attn_recv.at[side])
        rows = jnp.concatenate([gathered[side, p] for p in range(4)], axis=1)
        for chunk in range(CHUNKS):
            product = jnp.dot(
                rows,
                weights[side, :, chunk * PIECE : (chunk + 1) * PIECE],
                preferred_element_type=F32,
            )
            outgoing[side, chunk] = product[HALF:].astype(BF16)
            for piece in range(2):
                part(side, chunk, piece).start()
            own[side, chunk] = product[:HALF]

    wait_band(1)
    turn(1, 6, 1)
    complete(0, 3, (6,))
    wait_band(3)
    turn(0, 5, 2)
    complete(1, 2, (5,))
    complete(1, 3, (5, 6))
    give((0, 3), (1, 2), (1, 3))
    wait_band(0)
    turn(1, 1, 1)
    complete(0, 1, (1,))
    give((0, 1),)
    turn(1, 0, 1)
    complete(0, 0, (0, 1))
    give((0, 0),)

    @pl.when(last == 1)
    def _():
        project(1)

    wait_band(2)
    turn(0, 0, 1)
    complete(1, 0, (0,))
    give((1, 0),)
    project(0)

    @pl.when(last == 0)
    def _():
        project(1)

    @pl.when(herald)
    def _():
        for t in range(2):
            left(staged.at[1, t], share_send.at[1, t])

    for t in range(2):
        left(staged.at[0, t], share_send.at[0, t])
        left(held.at[0, 0, pl.ds(0, 6)], band_send.at[t])
    for side in range(2):
        left(attn.at[side], attn_send.at[side])
        left(outgoing.at[side], part_send.at[side])

    for side in range(2):
        for chunk in range(CHUNKS):
            landed(incoming.at[side, chunk], part_recv.at[side, chunk])
            out[side, :, chunk * PIECE : (chunk + 1) * PIECE] = (
                own[side, chunk] + incoming[side, chunk].astype(F32)
            ).astype(BF16)


def solution(mesh):
    count = mesh.shape["blk"]

    def shards(ref_a, val_a, ref_b, val_b, w_out_a, w_out_b):
        hbm = pl.BlockSpec(memory_space=pltpu.HBM)
        vmem = pl.BlockSpec(memory_space=pltpu.VMEM)
        out = pltpu.VMEM((2, HALF, WIDTH), BF16)
        results = pl.pallas_call(
            functools.partial(kernel, count),
            out_shape=out,
            in_specs=[hbm] * 6,
            out_specs=vmem,
            scratch_shapes=[
                pltpu.VMEM((2, 2, 4, ROWS, PAIR), BF16),
                pltpu.VMEM((2, 2, 7, ROWS, PAIR), BF16),
                pltpu.VMEM((2, 7, PAIR, ROWS), BF16),
                pltpu.VMEM((2, WIDTH // 2, WIDTH), BF16),
                pltpu.VMEM((2, 4, 8, 2 * ROWS), F32),
                pltpu.VMEM((2, 4, PAIR, ROWS), F32),
                pltpu.VMEM((2, 4, ROWS, PAIR), BF16),
                pltpu.VMEM((2, 4, ROWS, PAIR), BF16),
                pltpu.VMEM((2, CHUNKS, HALF, PIECE), BF16),
                pltpu.VMEM((2, CHUNKS, HALF, PIECE), BF16),
                pltpu.VMEM((2, CHUNKS, HALF, PIECE), F32),
                pltpu.SemaphoreType.REGULAR,
                pltpu.SemaphoreType.REGULAR,
                pltpu.SemaphoreType.DMA((2,)),
                pltpu.SemaphoreType.DMA((2, 2)),
                pltpu.SemaphoreType.DMA((2, 2)),
                pltpu.SemaphoreType.DMA((2, 2, 4)),
                pltpu.SemaphoreType.DMA((2,)),
                pltpu.SemaphoreType.DMA((4, 2)),
                pltpu.SemaphoreType.DMA((2,)),
                pltpu.SemaphoreType.DMA((2,)),
                pltpu.SemaphoreType.DMA((2,)),
                pltpu.SemaphoreType.DMA((2, CHUNKS)),
            ],
            compiler_params=pltpu.CompilerParams(
                collective_id=0, has_side_effects=True, vmem_limit_bytes=32 * 1024 * 1024
            ),
        )(
            *(
                pltpu.with_memory_space_constraint(array, pltpu.HBM)
                for array in (ref_a, val_a, ref_b, val_b, w_out_a, w_out_b)
            )
        )
        return results[0], results[1]

    return jax.shard_map(
        shards,
        mesh=mesh,
        in_specs=(
            P("blk", "head"),
            P("blk", "head"),
            P("blk", "head"),
            P("blk", "head"),
            P("head", None),
            P("head", None),
        ),
        out_specs=(P(("blk", "head"), None), P(("blk", "head"), None)),
        check_vma=False,
    )
```

```python
import functools
import math

import jax
import jax.numpy as jnp
from jax import lax
from jax.experimental import pallas as pl
from jax.experimental.pallas import tpu as pltpu
from jax.sharding import PartitionSpec as P


ROWS = 128
HALF = 64
QUARTER = 32
PAIR = 128
WIDTH = 1024
CHUNKS = 4
PIECE = WIDTH // CHUNKS
SCORE = 0.125 * math.log2(math.e)
BF16 = jnp.bfloat16
F32 = jnp.float32


def split_heads(query):
    lane = lax.broadcasted_iota(jnp.int32, (ROWS, PAIR), 1)
    query = query.astype(F32)
    zero = jnp.zeros_like(query)
    return jnp.concatenate(
        [jnp.where(lane < HALF, query, zero), jnp.where(lane < HALF, zero, query)], axis=0
    ).astype(BF16)


def pair_part(both, key, value):
    scores = lax.dot_general(key, both, (((1,), (1,)), ((), ())), preferred_element_type=F32)
    top = jnp.max(scores, axis=0, keepdims=True)
    expo = jnp.exp2((scores - top) * SCORE)
    accum = jnp.dot(value, expo.astype(BF16), preferred_element_type=F32)
    return top, jnp.sum(expo, axis=0, keepdims=True), accum[:HALF, :ROWS], accum[HALF:, ROWS:]


def merge_parts(parts):
    top = functools.reduce(jnp.maximum, [part[0] for part in parts])
    scales = [jnp.exp2((part[0] - top) * SCORE) for part in parts]
    return (
        top,
        sum(scale * part[1] for scale, part in zip(scales, parts)),
        sum(scale[:, :ROWS] * part[2] for scale, part in zip(scales, parts)),
        sum(scale[:, ROWS:] * part[3] for scale, part in zip(scales, parts)),
    )


def finish(part):
    _, total, first, second = part
    result = jnp.concatenate([first / total[:, :ROWS], second / total[:, ROWS:]], axis=0)
    return result.T.astype(BF16)


def kernel(
    count,
    ref_a,
    val_a,
    ref_b,
    val_b,
    w_a,
    w_b,
    out,
    staged,
    held,
    turned,
    weights,
    stats,
    sums,
    attn,
    gathered,
    outgoing,
    incoming,
    own,
    here_sem,
    near_sem,
    weight_sem,
    stage_sem,
    share_send,
    share_recv,
    band_send,
    band_recv,
    attn_send,
    attn_recv,
    part_send,
    part_recv,
):
    blk, head = lax.axis_index("blk"), lax.axis_index("head")
    place = lax.rem(blk, 4)
    base = blk - place
    other = 1 - head
    following = lax.rem(blk + 4, count)
    previous = lax.rem(blk + count - 4, count)

    herald = (place == 1) & (head == 1)
    holds_back = (place == 2) & (base + 4 == count)
    barrier = pltpu.get_barrier_semaphore()
    for p in (0, 2, 3):
        pl.semaphore_signal(barrier, inc=1, device_id={"blk": base + p, "head": other})

    @pl.when(head == 1)
    def _():
        pl.semaphore_signal(barrier, inc=1, device_id={"blk": base + 1, "head": other})

    loads = [
        pltpu.make_async_copy(w, weights.at[side], weight_sem.at[side])
        for side, w in enumerate((w_a, w_b))
    ]
    for side, pair in ((1, (ref_b, val_b)), (0, (ref_a, val_a))):
        for t in range(2):
            for p in range(4):
                pltpu.make_async_copy(
                    pair[t].at[:, pl.ds(p * PAIR, PAIR)], staged.at[side, t, p], stage_sem.at[side, t]
                ).start()
    for load in loads:
        load.start()

    @pl.when(jnp.logical_not(herald))
    def _():
        pl.semaphore_wait(barrier, 4)

    @pl.when(head == 0)
    def _():
        pl.semaphore_signal(here_sem, inc=1, device_id={"blk": base + 1, "head": other})

    @pl.when(herald)
    def _():
        pl.semaphore_wait(here_sem, 4)
        for near in (previous, following):
            pl.semaphore_signal(barrier, inc=1, device_id={"blk": near})


    def landed(ref, sem):
        pltpu.make_async_remote_copy(
            src_ref=ref, dst_ref=ref, send_sem=sem, recv_sem=sem, device_id={"head": other}
        ).wait_recv()

    def left(ref, sem):
        pltpu.make_async_remote_copy(
            src_ref=ref, dst_ref=ref, send_sem=sem, recv_sem=sem, device_id={"head": other}
        ).wait_send()

    def share(side, t, p):
        return pltpu.make_async_remote_copy(
            src_ref=staged.at[side, t, p],
            dst_ref=held.at[side, t, place + 1 + side],
            send_sem=share_send.at[side, t],
            recv_sem=share_recv.at[side, t, place],
            device_id={"blk": base + p, "head": other},
        )

    def shares(side, t):
        pltpu.make_async_copy(staged.at[side, t], staged.at[side, t], stage_sem.at[side, t]).wait()
        for p in range(4):
            share(side, t, p).start()

    shares(1, 0)
    shares(1, 1)
    for t in range(2):

        @pl.when(jnp.logical_not(herald))
        def _():
            left(staged.at[1, t], share_send.at[1, t])

        @pl.when(jnp.logical_not(holds_back))
        def _():
            shares(0, t)

    @pl.when(herald)
    def _():
        pl.semaphore_wait(barrier, 2)
        for p in range(4):
            pl.semaphore_signal(near_sem, inc=1, device_id={"blk": base + p, "head": other})
        for p in (0, 2, 3):
            pl.semaphore_signal(near_sem, inc=1, device_id={"blk": base + p})

    def wait_share(side, t, blocks):
        for block in blocks:
            landed(held.at[side, t, block + 1 + side], share_recv.at[side, t, block])

    bands = ((1, 4, 0, 2, True), (1, 2, 6, 1, False), (0, 4, 0, 1, True), (0, 1, 5, 2, False))

    def band(index, t):
        side, first, target, blocks, forward = bands[index]
        return pltpu.make_async_remote_copy(
            src_ref=held.at[side, t, pl.ds(first, blocks)],
            dst_ref=held.at[side, t, pl.ds(target, blocks)],
            send_sem=band_send.at[t],
            recv_sem=band_recv.at[index, t],
            device_id={"blk": following if forward else previous},
        )

    def turn(side, first, blocks):
        for position in range(first, first + blocks):
            turned[side, position] = held[side, 1, position].T

    def pass_on(t, *indices):
        for index in indices:
            side, first, _, blocks, _ = bands[index]
            wait_share(side, t, range(first - 1 - side, first - 1 - side + blocks))
            band(index, t).start()

    def wait_band(index):
        for t in range(2):
            band(index, t).wait_recv()

    def attn_copies(side, n):
        start, last = divmod(n, 2)
        pieces = [(n, other * HALF, 0, HALF)] + [
            (2 * part + last, head * HALF + part * QUARTER, HALF + start * QUARTER, QUARTER)
            for part in range(2)
        ]
        return [
            pltpu.make_async_remote_copy(
                src_ref=attn.at[side, n, pl.ds(pl.multiple_of(first, QUARTER), rows)],
                dst_ref=gathered.at[side, place, pl.ds(target, rows)],
                send_sem=attn_send.at[side],
                recv_sem=attn_recv.at[side],
                device_id={"blk": base + owner, "head": other},
            )
            for owner, first, target, rows in pieces
        ]

    def pairs(side, n, positions):
        both = split_heads(held[side, 0, n + 1 + side])
        return [
            pair_part(both, held[1 - side, 0, position], turned[1 - side, position])
            for position in positions
        ]

    def ready(side, n, part):
        attn[side, n] = finish(part)

    def begin(side, n, positions):
        part = merge_parts(pairs(side, n, positions))
        if len(positions) == 4:
            ready(side, n, part)
        else:
            stats[side, n, 0:1], stats[side, n, 1:2] = part[0], part[1]
            sums[side, n, :HALF], sums[side, n, HALF:] = part[2], part[3]

    def complete(side, n, positions):
        state = (
            stats[side, n, 0:1],
            stats[side, n, 1:2],
            sums[side, n, :HALF],
            sums[side, n, HALF:],
        )
        ready(side, n, merge_parts([state] + pairs(side, n, positions)))

    def give(*tasks):
        for side, n in tasks:
            for copy in attn_copies(side, n):
                copy.start()

    @pl.when(jnp.logical_not(herald))
    def _():
        pl.semaphore_wait(near_sem, 1)

    pass_on(0, 0, 1)
    pass_on(1, 0, 1)
    for t in range(2):
        wait_share(1, t, (1,))
    turn(1, 2, 4)
    pass_on(0, 2)

    @pl.when(holds_back)
    def _():
        for t in range(2):
            shares(0, t)

    pass_on(0, 3)
    pass_on(1, 2, 3)
    for t in range(2):
        wait_share(0, t, (2,))
    begin(0, 2, (2, 3, 4, 5))
    give((0, 2),)
    begin(0, 3, (3, 4, 5))
    begin(0, 1, (2, 3, 4))
    begin(0, 0, (2, 3))
    turn(0, 1, 4)
    begin(1, 1, (1, 2, 3, 4))
    give((1, 1),)
    begin(1, 2, (2, 3, 4))
    begin(1, 3, (3, 4))
    begin(1, 0, (1, 2, 3))
    start, last = place // 2, lax.rem(place, 2)

    def part(side, chunk, piece):
        return pltpu.make_async_remote_copy(
            src_ref=outgoing.at[side, chunk, pl.ds(piece * QUARTER, QUARTER)],
            dst_ref=incoming.at[
                side, chunk, pl.ds(pl.multiple_of(start * QUARTER, QUARTER), QUARTER)
            ],
            send_sem=part_send.at[side],
            recv_sem=part_recv.at[side, chunk],
            device_id={"blk": base + 2 * piece + last, "head": other},
        )

    def project(side):
        loads[side].wait()
        landed(gathered.at[side], attn_recv.at[side])
        rows = jnp.concatenate([gathered[side, p] for p in range(4)], axis=1)
        for chunk in range(CHUNKS):
            product = jnp.dot(
                rows,
                weights[side, :, chunk * PIECE : (chunk + 1) * PIECE],
                preferred_element_type=F32,
            )
            outgoing[side, chunk] = product[HALF:].astype(BF16)
            for piece in range(2):
                part(side, chunk, piece).start()
            own[side, chunk] = product[:HALF]

    wait_band(1)
    turn(1, 6, 1)
    complete(0, 3, (6,))
    wait_band(3)
    turn(0, 5, 2)
    complete(1, 2, (5,))
    complete(1, 3, (5, 6))
    give((0, 3), (1, 2), (1, 3))
    wait_band(0)
    turn(1, 1, 1)
    complete(0, 1, (1,))
    give((0, 1),)
    turn(1, 0, 1)
    complete(0, 0, (0, 1))
    give((0, 0),)

    @pl.when(last == 1)
    def _():
        project(1)

    wait_band(2)
    turn(0, 0, 1)
    complete(1, 0, (0,))
    give((1, 0),)
    project(0)

    @pl.when(last == 0)
    def _():
        project(1)

    @pl.when(herald)
    def _():
        for t in range(2):
            left(staged.at[1, t], share_send.at[1, t])

    for t in range(2):
        left(staged.at[0, t], share_send.at[0, t])
        left(held.at[0, 0, pl.ds(0, 6)], band_send.at[t])
    for side in range(2):
        left(attn.at[side], attn_send.at[side])
        left(outgoing.at[side], part_send.at[side])

    for side in range(2):
        for chunk in range(CHUNKS):
            landed(incoming.at[side, chunk], part_recv.at[side, chunk])
            out[side, :, chunk * PIECE : (chunk + 1) * PIECE] = (
                own[side, chunk] + incoming[side, chunk].astype(F32)
            ).astype(BF16)


def solution(mesh):
    count = mesh.shape["blk"]

    def shards(ref_a, val_a, ref_b, val_b, w_out_a, w_out_b):
        hbm = pl.BlockSpec(memory_space=pltpu.HBM)
        vmem = pl.BlockSpec(memory_space=pltpu.VMEM)
        out = pltpu.VMEM((2, HALF, WIDTH), BF16)
        results = pl.pallas_call(
            functools.partial(kernel, count),
            out_shape=out,
            in_specs=[hbm] * 6,
            out_specs=vmem,
            scratch_shapes=[
                pltpu.VMEM((2, 2, 4, ROWS, PAIR), BF16),
                pltpu.VMEM((2, 2, 7, ROWS, PAIR), BF16),
                pltpu.VMEM((2, 7, PAIR, ROWS), BF16),
                pltpu.VMEM((2, WIDTH // 2, WIDTH), BF16),
                pltpu.VMEM((2, 4, 8, 2 * ROWS), F32),
                pltpu.VMEM((2, 4, PAIR, ROWS), F32),
                pltpu.VMEM((2, 4, ROWS, PAIR), BF16),
                pltpu.VMEM((2, 4, ROWS, PAIR), BF16),
                pltpu.VMEM((2, CHUNKS, HALF, PIECE), BF16),
                pltpu.VMEM((2, CHUNKS, HALF, PIECE), BF16),
                pltpu.VMEM((2, CHUNKS, HALF, PIECE), F32),
                pltpu.SemaphoreType.REGULAR,
                pltpu.SemaphoreType.REGULAR,
                pltpu.SemaphoreType.DMA((2,)),
                pltpu.SemaphoreType.DMA((2, 2)),
                pltpu.SemaphoreType.DMA((2, 2)),
                pltpu.SemaphoreType.DMA((2, 2, 4)),
                pltpu.SemaphoreType.DMA((2,)),
                pltpu.SemaphoreType.DMA((4, 2)),
                pltpu.SemaphoreType.DMA((2,)),
                pltpu.SemaphoreType.DMA((2,)),
                pltpu.SemaphoreType.DMA((2,)),
                pltpu.SemaphoreType.DMA((2, CHUNKS)),
            ],
            compiler_params=pltpu.CompilerParams(
                collective_id=0, has_side_effects=True, vmem_limit_bytes=32 * 1024 * 1024
            ),
        )(
            *(
                pltpu.with_memory_space_constraint(array, pltpu.HBM)
                for array in (ref_a, val_a, ref_b, val_b, w_out_a, w_out_b)
            )
        )
        return results[0], results[1]

    return jax.shard_map(
        shards,
        mesh=mesh,
        in_specs=(
            P("blk", "head"),
            P("blk", "head"),
            P("blk", "head"),
            P("blk", "head"),
            P("head", None),
            P("head", None),
        ),
        out_specs=(P(("blk", "head"), None), P(("blk", "head"), None)),
        check_vma=False,
    )
```
